128 devices in a mesh: dp: 16 (over z_lo, x, core), tensor: 8 (over y, z_hi).
Axes of the slice: x: 4, y: 4, z: 4 (z_hi: 2, z_lo: 2; z = z_hi * 2 + z_lo), core: 2. Of those that a mesh axis runs over, the one named last changes fastest.
Arguments:
- block_input: bfloat16 [512, 8192], P('tensor', 'dp'), may hold values from -24 to 24
- cotangent: bfloat16 [512, 8192], P('tensor', 'dp'), may hold values from -6 to 6
- attn_gain: float32 [8192], P('dp'), may hold values from 0.1 to 1.9
- attn_bias: float32 [8192], P('dp'), may hold values from -3 to 3
- mlp_gain: float32 [8192], P('dp'), may hold values from 0.1 to 1.9
- mlp_bias: float32 [8192], P('dp'), may hold values from -3 to 3
- w_qkv: bfloat16 [8192, 9216], P('dp', 'tensor'), may hold values from -0.0625 to 0.0625
- w_out: bfloat16 [8192, 8192], P('tensor', 'dp'), may hold values from -0.0625 to 0.0625
- w_up: bfloat16 [8192, 32768], P('dp', 'tensor'), may hold values from -0.0625 to 0.0625
- w_down: bfloat16 [32768, 8192], P('tensor', 'dp'), may hold values from -0.03125 to 0.03125
Outputs:
- input_grad: bfloat16 [512, 8192], P('tensor', 'dp')
- norm_grads: float32 [4, 8192], P(None, 'dp')
- grad_qkv: bfloat16 [8192, 9216], P('dp', 'tensor')
- grad_out: bfloat16 [8192, 8192], P('tensor', 'dp')
- grad_up: bfloat16 [8192, 32768], P('dp', 'tensor')
- grad_down: bfloat16 [32768, 8192], P('tensor', 'dp')
The draws below stay inside these ranges and needn't reach their ends.
All inputs are finite; a program needn't handle non-finite values.
Results may differ from the reference program's by a relative error of at most 0.03.
Values may be sent and summed in bfloat16 or wider, within the bound.
A program may use at most 128 MiB of HBM per device.

```python
import math
import jax
import jax.numpy as jnp
from jax import lax

D = 8192
FF = 32768
HEADS = 128
G = 8
HD = 64
LENGTH = 512
TOKENS = 512


def draw_block_input(key, part):
    key = jax.random.fold_in(key, 11)
    key_rows, key_cols, key_base = jax.random.split(key, 3)
    row_scale = jnp.exp(jax.random.uniform(key_rows, (TOKENS, 1), jnp.float32, jnp.log(0.1), 0.0))
    rising = jnp.exp(jnp.log(3.0) * jnp.arange(D).astype(jnp.float32) / D)
    col_scale = rising * jnp.exp(jax.random.uniform(key_cols, (D,), jnp.float32, 0.0, jnp.log(2.0)))
    base = jnp.clip(jax.random.normal(key_base, (TOKENS, D), jnp.float32), -4.0, 4.0)
    values = row_scale * col_scale * base
    return values.astype(jnp.bfloat16)


def level_of(stream_key, shape, cuts, least, top_value):
    def one(dim, shards_of):
        heights = jax.random.uniform(jax.random.fold_in(jax.random.fold_in(stream_key, 6), dim), (shards_of,), jnp.float32, least / len(cuts), top_value / len(cuts))
        return jnp.repeat(jnp.exp(heights), shape[dim] // shards_of).reshape((-1,) + (1,) * (len(shape) - dim - 1))

    factor_of = one(*cuts[0])
    for cut in cuts[1:]:
        factor_of = factor_of * one(*cut)
    return factor_of


def normal_values(rng, extent, width, reach, cuts=(), held_as=jnp.bfloat16):
    level = level_of(rng, extent, cuts, -0.22, 0.18) if cuts else 1.0
    drawn = jax.random.normal(rng, extent, jnp.float32) * width * level
    return jnp.minimum(jnp.maximum(drawn, -reach), reach).astype(held_as)


def setup_inputs(seed: int = 0) -> dict:
    splits = jax.random.split(jax.random.key(seed), 11)
    block_input = draw_block_input(jax.random.fold_in(splits[10], 71), 0)
    cotangent = normal_values(splits[1], (TOKENS, D), 1.0, 6.0, ((0, 8), (1, 16)))
    attn_gain = jnp.clip(1.0 + 0.18 * jax.random.normal(splits[2], (D,), jnp.float32), 0.1, 1.9)
    attn_bias = normal_values(splits[3], (D,), 0.5, 3.0, ((0, 16),), jnp.float32)
    mlp_gain = jnp.clip(1.0 + 0.18 * jax.random.normal(splits[4], (D,), jnp.float32), 0.1, 1.9)
    mlp_bias = normal_values(splits[5], (D,), 0.5, 3.0, ((0, 16),), jnp.float32)
    w_qkv = normal_values(splits[6], (D, G * (HEADS // G + 2) * HD), D ** -0.5, 0.0625, ((0, 16), (1, 8)))
    w_out = normal_values(splits[7], (HEADS * HD, D), (HEADS * HD) ** -0.5, 0.0625, ((0, 8), (1, 16)))
    w_up = normal_values(splits[8], (D, FF), D ** -0.5, 0.0625, ((0, 16), (1, 8)))
    w_down = normal_values(splits[9], (FF, D), FF ** -0.5, 0.03125, ((0, 8), (1, 16)))
    return {"block_input": block_input, "cotangent": cotangent, "attn_gain": attn_gain, "attn_bias": attn_bias, "mlp_gain": mlp_gain, "mlp_bias": mlp_bias, "w_qkv": w_qkv, "w_out": w_out, "w_up": w_up, "w_down": w_down}


def gelu_value(argument):
    return 0.5 * argument * (1.0 + lax.erf(argument * 0.7071067811865476))

def gelu_slope(argument):
    return 0.5 * (1.0 + lax.erf(argument * 0.7071067811865476)) + argument * jnp.exp(-0.5 * argument * argument) * 0.3989422804014327

def rope_tables(tokens):
    halfway = HD // 2
    position = (jnp.arange(tokens) % LENGTH).astype(jnp.float32)
    frequency = 10000.0 ** (-2.0 * jnp.arange(halfway).astype(jnp.float32) / HD)
    angle = position[:, None] * frequency[None, :]
    cosine = jnp.concatenate([jnp.cos(angle), jnp.cos(angle)], 1)
    sine = jnp.concatenate([jnp.sin(angle), jnp.sin(angle)], 1)
    return (cosine, sine)

def rotate_last(values, cosine, sine):
    halfway = values.shape[-1] // 2
    turned = jnp.concatenate([-values[..., halfway:], values[..., :halfway]], -1)
    return values * cosine + turned * sine

def unrotate_last(values, cosine, sine):
    halfway = values.shape[-1] // 2
    scaled = values * sine
    back = jnp.concatenate([scaled[..., halfway:], -scaled[..., :halfway]], -1)
    return values * cosine + back

def group_attention(operands):
    queries, keys_one, values_one, out_grad = operands
    tokens = queries.shape[0]
    seqcount = tokens // LENGTH
    per_group = queries.shape[1]
    scaling = 1.0 / math.sqrt(HD)
    query_f = queries.astype(jnp.float32).reshape(seqcount, LENGTH, per_group, HD)
    key_f = keys_one.astype(jnp.float32).reshape(seqcount, LENGTH, HD)
    value_f = values_one.astype(jnp.float32).reshape(seqcount, LENGTH, HD)
    grad_f = out_grad.astype(jnp.float32).reshape(seqcount, LENGTH, per_group, HD)
    scores = jnp.einsum('snhd,smd->shnm', query_f, key_f) * scaling
    causal = jnp.arange(LENGTH)[:, None] >= jnp.arange(LENGTH)[None, :]
    raised = jnp.where(causal, jnp.exp(scores), 0.0)
    probability = raised / lax.optimization_barrier(jnp.sum(raised, -1, keepdims=True))
    prob_low = probability.astype(jnp.bfloat16).astype(jnp.float32)
    outputs = jnp.einsum('shnm,smd->snhd', prob_low, value_f).astype(jnp.bfloat16)
    dropped = jnp.einsum('snhd,smd->shnm', grad_f, value_f)
    row_dot = jnp.einsum('snhd,snhd->shn', grad_f, outputs.astype(jnp.float32))
    score_grad = (probability * (dropped - row_dot[..., None]) * scaling).astype(jnp.bfloat16).astype(jnp.float32)
    query_grad = jnp.einsum('shnm,smd->snhd', score_grad, key_f)
    key_grad = jnp.einsum('shnm,snhd->smd', score_grad, query_f)
    value_grad = jnp.einsum('shnm,snhd->smd', prob_low, grad_f)
    return (outputs.reshape(tokens, per_group, HD), query_grad.reshape(tokens, per_group, HD), key_grad.reshape(tokens, HD), value_grad.reshape(tokens, HD))

def reference(block_input, cotangent, attn_gain, attn_bias, mlp_gain, mlp_bias, w_qkv, w_out, w_up, w_down):
    tokens = block_input.shape[0]
    per_group = HEADS // G
    inputs = block_input.astype(jnp.float32)
    average = lax.optimization_barrier(jnp.sum(inputs, 1)) / D
    spread = lax.optimization_barrier(jnp.sum(inputs * inputs, 1)) / D - average * average
    inverse = lax.rsqrt(spread + 1e-05)
    normed = (inputs - average[:, None]) * inverse[:, None]
    attn_in = (normed * attn_gain + attn_bias).astype(jnp.bfloat16)
    mlp_in = (normed * mlp_gain + mlp_bias).astype(jnp.bfloat16)
    projected = jnp.dot(attn_in, w_qkv, preferred_element_type=jnp.float32).reshape(tokens, G, per_group + 2, HD)
    cosine, sine = rope_tables(tokens)
    queries = rotate_last(projected[:, :, :per_group], cosine[:, None, None], sine[:, None, None]).astype(jnp.bfloat16)
    keys_all = rotate_last(projected[:, :, per_group], cosine[:, None], sine[:, None]).astype(jnp.bfloat16)
    values_all = projected[:, :, per_group + 1].astype(jnp.bfloat16)
    out_grad = jnp.dot(cotangent, w_out.T, preferred_element_type=jnp.float32).astype(jnp.bfloat16)
    out_grad = out_grad.reshape(tokens, G, per_group, HD)
    outputs, query_grad, key_grad, value_grad = lax.map(group_attention, (queries.transpose(1, 0, 2, 3), keys_all.transpose(1, 0, 2), values_all.transpose(1, 0, 2), out_grad.transpose(1, 0, 2, 3)))
    head_out = outputs.transpose(1, 0, 2, 3).reshape(tokens, G * per_group * HD)
    grad_out = jnp.dot(head_out.T, cotangent, preferred_element_type=jnp.float32).astype(jnp.bfloat16)
    query_low = unrotate_last(query_grad.transpose(1, 0, 2, 3), cosine[:, None, None], sine[:, None, None]).astype(jnp.bfloat16)
    key_low = unrotate_last(key_grad.transpose(1, 0, 2), cosine[:, None], sine[:, None]).astype(jnp.bfloat16)
    value_low = value_grad.transpose(1, 0, 2).astype(jnp.bfloat16)
    proj_grad = jnp.concatenate([query_low, key_low[:, :, None], value_low[:, :, None]], 2).reshape(tokens, -1)
    grad_qkv = jnp.dot(attn_in.T, proj_grad, preferred_element_type=jnp.float32).astype(jnp.bfloat16)
    attn_back = jnp.dot(proj_grad, w_qkv.T, preferred_element_type=jnp.float32)
    hidden = jnp.dot(mlp_in, w_up, preferred_element_type=jnp.float32)
    active = gelu_value(hidden).astype(jnp.bfloat16)
    grad_down = jnp.dot(active.T, cotangent, preferred_element_type=jnp.float32).astype(jnp.bfloat16)
    hidden_grad = (jnp.dot(cotangent, w_down.T, preferred_element_type=jnp.float32) * gelu_slope(hidden)).astype(jnp.bfloat16)
    grad_up = jnp.dot(mlp_in.T, hidden_grad, preferred_element_type=jnp.float32).astype(jnp.bfloat16)
    mlp_back = jnp.dot(hidden_grad, w_up.T, preferred_element_type=jnp.float32)
    norm_grads = jnp.stack([lax.optimization_barrier(jnp.sum(attn_back * normed, 0)), lax.optimization_barrier(jnp.sum(attn_back, 0)), lax.optimization_barrier(jnp.sum(mlp_back * normed, 0)), lax.optimization_barrier(jnp.sum(mlp_back, 0))])
    normed_grad = attn_back * attn_gain + mlp_back * mlp_gain
    first = lax.optimization_barrier(jnp.sum(normed_grad, 1)) / D
    second = lax.optimization_barrier(jnp.sum(normed_grad * normed, 1)) / D
    input_grad = (cotangent.astype(jnp.float32) + inverse[:, None] * (normed_grad - first[:, None] - normed * second[:, None])).astype(jnp.bfloat16)
    return (input_grad, norm_grads, grad_qkv, grad_out, grad_up, grad_down)
```

```python
import functools
import math

import jax
import jax.numpy as jnp
from jax import lax
from jax.experimental import pallas as pl
from jax.experimental.pallas import tpu as pltpu
from jax.sharding import PartitionSpec as P

D = 8192
HD = 64
LENGTH = 512
TOK = 512
W = 512
ROWS = 64
NT = 8
ND = 16
FF = 4096
CH = 256
QKV = 1152
MESH = pl.DeviceIdType.MESH
BF = jnp.bfloat16
F32 = jnp.float32


def dot_nn(a, b):
    return jnp.dot(a, b, preferred_element_type=F32)


def dot_nt(a, b):
    return lax.dot_general(a, b, (((1,), (1,)), ((), ())), preferred_element_type=F32)


def gelu_parts(v):
    half = 0.5 * (1.0 + lax.erf(v * 0.7071067811865476))
    return v * half, half + v * jnp.exp(-0.5 * v * v) * 0.3989422804014327


def rope_columns():
    halfway = HD // 2
    position = (jnp.arange(TOK) % LENGTH).astype(F32)
    frequency = 10000.0 ** (-2.0 * jnp.arange(halfway).astype(F32) / HD)
    angle = frequency[:, None] * position[None, :]
    cosine = jnp.concatenate([jnp.cos(angle), jnp.cos(angle)], 0)
    sine = jnp.concatenate([jnp.sin(angle), jnp.sin(angle)], 0)
    return cosine, sine


def rotate(v, cosine, sine):
    turned = jnp.concatenate([-v[32:], v[:32]], 0)
    return v * cosine + turned * sine


def unrotate(v, cosine, sine):
    scaled = v * sine
    back = jnp.concatenate([scaled[32:], -scaled[:32]], 0)
    return v * cosine + back


def kernel(
    x_loc, c_loc, ag, ab, mg, mb, cosine, sine, wq_hbm, wo_hbm, wu_hbm, wd_hbm,
    out_x, out_n, out_q, out_o, out_u, out_d,
    xs, cs, st_in, st, wq, wqt, wo, wu, wd, ain, min_, ain_t, min_t,
    pa, pkv, pa_in, pkv_in, sa, ra, kvx,
    pd_out, pd_in, od, rd, ph_out, ph_in, oh, rh,
    ah, hq, proj, pp, pp_in, psum, pr,
    abt, mbt, ngb, ngr, mom, momr, nrm, nrmr, m2,
    w_sem, x_s, x_r, c_s, c_r, st_s, st_r, tt_s, tt_r,
    a_sem, sa_s, sa_r, kv_sem,
    pd_s, pd_r, rd_s, rd_r, ph_s, ph_r, rh_s, rh_r,
    ah_s, ah_r, fa_s, fa_r, hq_s, hq_r, fh_s, fh_r, pp_sem, pr_s, pr_r, pj_sem,
    o_sem, u_sem, d_sem, ng_s, ng_r, mo_s, mo_r, nr_s, nr_r, m2_s, m2_r,
):
    d = lax.axis_index("dp")
    t = lax.axis_index("tensor")
    c = d % 2
    xx = (d // 2) % 4
    zl = d // 8
    other = 1 - c
    partner = (d + 1 - 2 * c, t)
    mine = d // 2

    def to_chip(s):
        return ((zl + s % 2) % 2) * 4 + (xx + s // 2) % 4

    def from_chip(s):
        return ((zl + s % 2) % 2) * 4 + (xx + 4 - s // 2) % 4

    def remote(src, dst, send, recv, device):
        return pltpu.make_async_remote_copy(
            src_ref=src, dst_ref=dst, send_sem=send, recv_sem=recv, device_id=device, device_id_type=MESH
        )

    def rows(index, size):
        return pl.ds(pl.multiple_of(index * size, size), size)

    weights = [
        pltpu.make_async_copy(src, dst, w_sem.at[i])
        for i, (src, dst) in enumerate([(wd_hbm, wd), (wq_hbm, wq), (wo_hbm, wo), (wu_hbm, wu)])
    ]
    for copy in weights:
        copy.start()

    barrier = pltpu.get_barrier_semaphore()

    def greet_t(k, carry):
        pl.semaphore_signal(barrier, inc=1, device_id=(d, (t + k) % NT), device_id_type=MESH)
        return carry

    def greet_d(k, carry):
        pl.semaphore_signal(barrier, inc=1, device_id=((d + k) % ND, t), device_id_type=MESH)
        return carry

    lax.fori_loop(1, NT, greet_t, 0)
    lax.fori_loop(1, ND, greet_d, 0)
    pl.semaphore_wait(barrier, NT - 1 + ND - 1)

    own = rows(t, ROWS)

    def send_c(k):
        return remote(c_loc, cs.at[own], c_s.at[k], c_r.at[k], (d, (t + k) % NT))

    def send_x(k):
        return remote(x_loc, xs.at[own], x_s.at[k], x_r.at[k], (d, (t + k) % NT))

    def start_gather(k, carry):
        send_c(k).start()
        send_x(k).start()
        return carry

    lax.fori_loop(1, NT, start_gather, 0)
    cs[own, :] = c_loc[...]
    xs[own, :] = x_loc[...]
    lane = lax.broadcasted_iota(jnp.int32, (ROWS, 128), 1)
    xf = x_loc[...].astype(F32)
    st_in[0] = jnp.where(
        lane < 64, jnp.sum(xf, 1, keepdims=True), jnp.sum(xf * xf, 1, keepdims=True)
    )

    def send_st(k):
        return remote(st_in.at[0], st_in.at[k], st_s.at[k], st_r.at[k], ((d + k) % ND, t))

    def send_tt(k):
        return remote(st.at[own], st.at[own], tt_s.at[k], tt_r.at[k], (d, (t + k) % NT))

    def loop(low, high, f):
        def body(k, carry):
            f(k)
            return carry

        lax.fori_loop(low, high, body, 0)

    loop(1, ND, lambda k: send_st(k).start())
    weights[1].wait()
    for i in range(QKV // 128):
        wqt[i * 128 : (i + 1) * 128, :] = wq[:, i * 128 : (i + 1) * 128].T
    loop(1, ND, lambda k: send_st(k).wait_recv())
    total = st_in[0]
    for k in range(1, ND):
        total = total + st_in[k]
    st[own, :] = total
    loop(1, NT, lambda k: send_tt(k).start())

    def pair_copy(out, into, send, recv, r):
        return remote(out.at[r], into.at[r], send.at[r], recv.at[r], partner)

    def chip_copy(buf, into, send, recv, r):
        return remote(buf.at[r], into.at[r], send.at[r], recv.at[r], (to_chip(7 - r) * 2 + c, t))

    def reduce_start(chunk, out, into, keep, land, ps, pr_, ss, sr):
        def produce(r):
            q = to_chip(7 - r)
            out[r] = chunk(2 * q + other).astype(BF)
            pair_copy(out, into, ps, pr_, r).start()
            keep[r] = chunk(2 * q + c).astype(BF)

        def finish(r):
            pair_copy(out, into, ps, pr_, r).wait_recv()
            keep[r] = (keep[r].astype(F32) + into[r].astype(F32)).astype(BF)

        def body(r):
            produce(r)
            finish(r - 1)
            chip_copy(keep, land, ss, sr, r - 1).start()

        produce(0)
        loop(1, 8, body)
        finish(7)

    def reduce_end(out, into, keep, land, ps, pr_, ss, sr):
        def body(r):
            chip_copy(keep, land, ss, sr, r).wait_recv()
            chip_copy(keep, land, ss, sr, r).wait_send()

        loop(0, 7, body)
        loop(0, 8, lambda r: pair_copy(out, into, ps, pr_, r).wait_send())

    loop(1, NT, lambda k: send_c(k).wait_recv())
    weights[0].wait()
    down = (pd_out, pd_in, od, rd, pd_s, pd_r, rd_s, rd_r)
    reduce_start(lambda p: dot_nt(wd[rows(p, CH), :], cs[...]), *down)

    loop(1, NT, lambda k: send_x(k).wait_recv())
    loop(1, NT, lambda k: send_tt(k).wait_recv())

    def norm_rows(block, size):
        here = rows(block, size)
        average = st[here, 0:1] * (1.0 / D)
        spread = st[here, 64:65] * (1.0 / D) - average * average
        inverse = lax.rsqrt(spread + 1e-05)
        return (xs[here, :].astype(F32) - average) * inverse, inverse

    def norm_body(block):
        here = rows(block, ROWS)
        normed, _ = norm_rows(block, ROWS)
        ain[here, :] = (normed * ag[...] + ab[...]).astype(BF)
        min_[here, :] = (normed * mg[...] + mb[...]).astype(BF)

    loop(0, NT, norm_body)

    weights[2].wait()

    def part_body(i):
        og = dot_nt(wo[rows(i, 256), :], cs[...]).astype(BF)
        pa[pl.ds(i * 2, 2), :, 0:64, :] = og.reshape(2, 2, 64, TOK)
        qq = dot_nt(wqt[rows(i, 256), :], ain[...]).astype(BF)
        pa[pl.ds(i * 2, 2), :, 64:128, :] = qq.reshape(2, 2, 64, TOK)

    loop(0, 4, part_body)
    pkv[...] = dot_nt(wqt[1024:1152, :], ain[...]).astype(BF).reshape(2, 64, TOK)
    give_a = remote(pa.at[:, other], pa_in, a_sem.at[0], a_sem.at[1], partner)
    give_kv = remote(pkv.at[other], pkv_in, a_sem.at[2], a_sem.at[3], partner)
    give_a.start()
    give_kv.start()
    give_a.wait_recv()
    give_kv.wait_recv()
    kv_pair = (pkv[c].astype(F32) + pkv_in[...].astype(F32)).astype(BF)

    def send_a(s):
        return remote(sa.at[to_chip(s)], ra.at[s], sa_s.at[s], sa_r.at[s], (to_chip(s) * 2 + c, t))

    def sum_a(s):
        q = to_chip(s)
        sa[q, 0:128, :] = (pa[q, c].astype(F32) + pa_in[q].astype(F32)).astype(BF)
        sa[q, 128:192, :] = kv_pair

    def start_a(i):
        sum_a(8 - i)
        send_a(8 - i).start()

    loop(1, 8, start_a)
    sum_a(0)

    weights[3].wait()
    up = (ph_out, ph_in, oh, rh, ph_s, ph_r, rh_s, rh_r)
    reduce_start(lambda p: dot_nn(min_[...], wu[:, rows(p, CH)]), *up)
    ain_t[...] = ain[...].T
    min_t[...] = min_[...].T

    loop(1, 8, lambda s: send_a(s).wait_recv())
    parts = []
    for i in range(3):
        acc = sa[mine, i * 64 : (i + 1) * 64, :].astype(F32)
        for s in range(1, 8):
            acc = acc + ra[s, i * 64 : (i + 1) * 64, :].astype(F32)
        parts.append(acc)
    og = parts[0].astype(BF)
    co, si = cosine[...], sine[...]
    queries_f = rotate(parts[1], co, si)
    queries = queries_f.astype(BF)
    kvx[c] = jnp.where(c == 0, rotate(parts[2], co, si), parts[2]).astype(BF)
    give = remote(kvx.at[c], kvx.at[c], kv_sem.at[0], kv_sem.at[1], partner)
    give.start()
    queries_t = queries_f.T.astype(BF)
    og_tf = og.astype(F32).T
    og_t = og_tf.astype(BF)
    give.wait_recv()
    keys = kvx[0]
    values = kvx[1]
    scaling = 1.0 / math.sqrt(HD)
    key_grad = jnp.zeros((HD, TOK), F32)
    value_grad = jnp.zeros((HD, TOK), F32)
    outs, qgs = [], []
    for n in range(4):
        low, high = n * 128, (n + 1) * 128
        scores = dot_nn(queries_t[low:high], keys) * scaling
        causal = lax.broadcasted_iota(jnp.int32, (128, TOK), 0) + low >= lax.broadcasted_iota(
            jnp.int32, (128, TOK), 1
        )
        raised = jnp.where(causal, jnp.exp(scores), 0.0)
        prob = raised / jnp.sum(raised, -1, keepdims=True)
        prob_low = prob.astype(BF)
        head = dot_nt(prob_low, values).astype(BF).astype(F32)
        dropped = dot_nn(og_t[low:high], values)
        row_dot = jnp.sum(og_tf[low:high] * head, -1, keepdims=True)
        score_grad = (prob * (dropped - row_dot) * scaling).astype(BF)
        qgs.append(dot_nt(keys, score_grad))
        key_grad = key_grad + dot_nn(queries[:, low:high], score_grad)
        value_grad = value_grad + dot_nn(og[:, low:high], prob_low)
        outs.append(head.T)
    hq[d, 0:64, :] = jnp.concatenate(outs, 1).astype(BF)
    hq[d, 64:128, :] = unrotate(jnp.concatenate(qgs, 1), co, si).astype(BF)
    pp[0] = unrotate(key_grad, co, si).astype(BF)
    pp[1] = value_grad.astype(BF)

    def send_hq(s):
        return remote(hq.at[d], hq.at[d], hq_s.at[s], hq_r.at[s], (to_chip(s) * 2 + c, t))

    def wait_hq(s):
        p = from_chip(s) * 2 + c
        remote(hq.at[p], hq.at[p], hq_s.at[s], hq_r.at[s], (to_chip(s) * 2 + c, t)).wait_recv()

    def pass_hq(s, core):
        p = from_chip(s) * 2 + core
        return remote(hq.at[p], hq.at[p], fh_s.at[s], fh_r.at[s], partner)

    give_pp = remote(pp.at[other], pp_in, pp_sem.at[0], pp_sem.at[1], partner)
    give_pp.start()
    loop(1, 8, lambda i: send_hq(8 - i).start())
    pass_hq(0, c).start()
    give_pp.wait_recv()
    psum[...] = (pp[c].astype(F32) + pp_in[...].astype(F32)).astype(BF)

    def send_pr(s):
        return remote(psum, pr.at[s], pr_s.at[s], pr_r.at[s], (to_chip(s) * 2 + c, t))

    loop(1, 8, lambda i: send_pr(8 - i).start())

    reduce_end(*down)
    reduce_end(*up)
    for h in range(2):
        cols = slice(h * 128, (h + 1) * 128)
        hid = oh[7, :, cols].astype(F32)
        for r in range(7):
            hid = hid + rh[r, :, cols].astype(F32)
        hid = hid.T
        dact = od[7, cols, :].astype(F32)
        for r in range(7):
            dact = dact + rd[r, cols, :].astype(F32)
        value, slope = gelu_parts(hid)
        ah[d, h * 128 : (h + 1) * 128, :] = value.astype(BF)
        ah[d, CH + h * 128 : CH + (h + 1) * 128, :] = (dact * slope).astype(BF)

    def send_ah(s):
        return remote(ah.at[d], ah.at[d], ah_s.at[s], ah_r.at[s], (to_chip(s) * 2 + c, t))

    def wait_ah(s):
        p = from_chip(s) * 2 + c
        remote(ah.at[p], ah.at[p], ah_s.at[s], ah_r.at[s], (to_chip(s) * 2 + c, t)).wait_recv()

    def pass_ah(s, core):
        p = from_chip(s) * 2 + core
        return remote(ah.at[p], ah.at[p], fa_s.at[s], fa_r.at[s], partner)

    loop(1, 8, lambda s: send_ah(s).start())
    pass_ah(0, c).start()

    def hq_body(s):
        wait_hq(s)
        pass_hq(s, c).start()

    loop(1, 8, hq_body)
    loop(1, 8, lambda s: send_pr(s).wait_recv())
    acc = psum[...].astype(F32)
    for s in range(1, 8):
        acc = acc + pr[s].astype(F32)
    there = rows(16 + c, 64)
    proj[there, :] = acc.astype(BF)
    give_pj = remote(proj.at[there], proj.at[there], pj_sem.at[0], pj_sem.at[1], partner)
    give_pj.start()
    loop(0, 8, lambda s: pass_hq(s, other).wait_recv())
    give_pj.wait_recv()

    def go_body(i):
        heads = hq[pl.ds(i * 4, 4), 0:64, :].reshape(256, TOK)
        wo[rows(i, 256), :] = dot_nn(heads, cs[...]).astype(BF)
        proj[rows(i, 256), :] = hq[pl.ds(i * 4, 4), 64:128, :].reshape(256, TOK)

    loop(0, 4, go_body)
    out_o_copy = pltpu.make_async_copy(wo, out_o, o_sem.at[0])
    out_o_copy.start()

    def ab_body(i):
        abt[rows(i, 128), :] = dot_nn(wq[rows(i, 128), :], proj[...])
        wq[rows(i, 128), :] = dot_nt(ain_t[rows(i, 128), :], proj[...]).astype(BF)

    loop(0, 4, ab_body)
    out_q_copy = pltpu.make_async_copy(wq, out_q, o_sem.at[1])
    out_q_copy.start()

    mbt[...] = jnp.zeros((W, TOK), F32)

    def out_d_copy(p):
        return pltpu.make_async_copy(wd.at[rows(p, CH)], out_d.at[rows(p, CH)], d_sem.at[p])

    def out_u_copy(p):
        return pltpu.make_async_copy(wu.at[:, rows(p, CH)], out_u.at[:, rows(p, CH)], u_sem.at[p])

    def consume(p):
        wd[rows(p, CH), :] = dot_nn(ah[p, 0:CH, :], cs[...]).astype(BF)
        out_d_copy(p).start()
        mbt[...] += dot_nn(wu[:, rows(p, CH)], ah[p, CH : 2 * CH, :])
        wu[:, rows(p, CH)] = dot_nt(min_t[...], ah[p, CH : 2 * CH, :]).astype(BF)
        out_u_copy(p).start()

    consume(d)
    pass_ah(0, other).wait_recv()
    consume(d + 1 - 2 * c)

    def ff_body(s):
        wait_ah(s)
        pass_ah(s, c).start()
        consume(from_chip(s) * 2 + c)
        pass_ah(s, other).wait_recv()
        consume(from_chip(s) * 2 + other)

    loop(1, 8, ff_body)

    lane2 = lax.broadcasted_iota(jnp.int32, (128, 128), 1)

    def tail_body(n):
        here = rows(n, 128)
        a_back = abt[:, here].T
        m_back = mbt[:, here].T
        normed, _ = norm_rows(n, 128)
        grad = a_back * ag[...] + m_back * mg[...]
        ngb[here, :] = grad.astype(BF)
        mom[here, :] = jnp.where(
            lane2 < 64, jnp.sum(grad, 1, keepdims=True), jnp.sum(grad * normed, 1, keepdims=True)
        )
        sums = jnp.concatenate(
            [
                jnp.sum(a_back * normed, 0, keepdims=True),
                jnp.sum(a_back, 0, keepdims=True),
                jnp.sum(m_back * normed, 0, keepdims=True),
                jnp.sum(m_back, 0, keepdims=True),
                jnp.zeros((4, W), F32),
            ],
            0,
        )
        nrm[...] += sums

    nrm[...] = jnp.zeros((8, W), F32)
    loop(0, 4, tail_body)

    def send_ng(k):
        p = (t + k) % NT
        return remote(ngb.at[rows(p, ROWS)], ngr.at[k], ng_s.at[k], ng_r.at[k], (d, p))

    def send_mo(k):
        p = (t + k) % NT
        return remote(mom.at[rows(p, ROWS)], momr.at[k], mo_s.at[k], mo_r.at[k], (d, p))

    def send_nr(k):
        return remote(nrm, nrmr.at[k], nr_s.at[k], nr_r.at[k], (d, (t + k) % NT))

    def start_tail(k):
        send_mo(k).start()
        send_ng(k).start()
        send_nr(k).start()

    loop(1, NT, start_tail)
    loop(1, NT, lambda k: send_mo(k).wait_recv())
    acc = mom[own, :]
    for k in range(1, NT):
        acc = acc + momr[k]
    m2[0] = acc

    def send_m2(k):
        return remote(m2.at[0], m2.at[k], m2_s.at[k], m2_r.at[k], ((d + k) % ND, t))

    loop(1, ND, lambda k: send_m2(k).start())
    loop(1, NT, lambda k: send_ng(k).wait_recv())
    loop(1, NT, lambda k: send_nr(k).wait_recv())
    norm_total = nrm[...]
    for k in range(1, NT):
        norm_total = norm_total + nrmr[k]
    out_n[...] = norm_total[0:4, :]
    grad = ngb[own, :].astype(F32)
    for k in range(1, NT):
        grad = grad + ngr[k].astype(F32)
    loop(1, ND, lambda k: send_m2(k).wait_recv())
    moments = m2[0]
    for k in range(1, ND):
        moments = moments + m2[k]
    first = moments[:, 0:1] * (1.0 / D)
    second = moments[:, 64:65] * (1.0 / D)
    normed, inverse = norm_rows(t, ROWS)
    out_x[...] = (c_loc[...].astype(F32) + inverse * (grad - first - normed * second)).astype(BF)

    def drain_t(k):
        send_c(k).wait_send()
        send_x(k).wait_send()
        send_tt(k).wait_send()
        send_mo(k).wait_send()
        send_ng(k).wait_send()
        send_nr(k).wait_send()

    def drain_d(k):
        send_st(k).wait_send()
        send_m2(k).wait_send()

    def drain_s(s):
        send_a(s).wait_send()
        send_hq(s).wait_send()
        send_pr(s).wait_send()
        send_ah(s).wait_send()

    def drain_p(s):
        pass_hq(s, c).wait_send()
        pass_ah(s, c).wait_send()

    def drain_o(p):
        out_d_copy(p).wait()
        out_u_copy(p).wait()

    loop(1, NT, drain_t)
    loop(1, ND, drain_d)
    loop(1, 8, drain_s)
    loop(0, 8, drain_p)
    give_a.wait_send()
    give_kv.wait_send()
    give.wait_send()
    give_pp.wait_send()
    give_pj.wait_send()
    out_o_copy.wait()
    out_q_copy.wait()
    loop(0, ND, drain_o)


def on_device(
    block_input, cotangent, attn_gain, attn_bias, mlp_gain, mlp_bias, w_qkv, w_out, w_up, w_down
):
    cosine, sine = rope_columns()
    vmem = pl.BlockSpec(memory_space=pltpu.VMEM)
    hbm = pl.BlockSpec(memory_space=pl.ANY)
    dma = pltpu.SemaphoreType.DMA

    def buf(*shape):
        return pltpu.VMEM(shape, BF)

    def wide(*shape):
        return pltpu.VMEM(shape, F32)

    buffers = [
        buf(TOK, W), buf(TOK, W), wide(ND, ROWS, 128), wide(TOK, 128),
        buf(W, QKV), buf(QKV, W), buf(1024, W), buf(W, FF), buf(FF, W),
        buf(TOK, W), buf(TOK, W), buf(W, TOK), buf(W, TOK),
        buf(8, 2, 128, TOK), buf(2, 64, TOK), buf(8, 128, TOK), buf(64, TOK),
        buf(8, 192, TOK), buf(8, 192, TOK), buf(2, 64, TOK),
        buf(8, CH, TOK), buf(8, CH, TOK), buf(8, CH, TOK), buf(7, CH, TOK),
        buf(8, TOK, CH), buf(8, TOK, CH), buf(8, TOK, CH), buf(7, TOK, CH),
        buf(ND, 2 * CH, TOK), buf(ND, 128, TOK), buf(QKV, TOK),
        buf(2, 64, TOK), buf(64, TOK), buf(64, TOK), buf(8, 64, TOK),
        wide(W, TOK), wide(W, TOK), buf(TOK, W), buf(NT, ROWS, W),
        wide(TOK, 128), wide(NT, ROWS, 128), wide(8, W), wide(NT, 8, W), wide(ND, ROWS, 128),
    ]
    semaphores = [dma((n,)) for n in (4, 8, 8, 8, 8, 16, 16, 8, 8)]
    semaphores += [dma((n,)) for n in (4, 8, 8, 2)]
    semaphores += [dma((8,))] * 8
    semaphores += [dma((n,)) for n in (8, 8, 8, 8, 8, 8, 8, 8, 2, 8, 8, 2)]
    semaphores += [dma((n,)) for n in (2, 16, 16, 8, 8, 8, 8, 8, 8, 16, 16)]
    return pl.pallas_call(
        kernel,
        out_shape=(
            jax.ShapeDtypeStruct((ROWS, W), BF),
            jax.ShapeDtypeStruct((4, W), F32),
            jax.ShapeDtypeStruct((W, QKV), BF),
            jax.ShapeDtypeStruct((1024, W), BF),
            jax.ShapeDtypeStruct((W, FF), BF),
            jax.ShapeDtypeStruct((FF, W), BF),
        ),
        in_specs=[vmem] * 8 + [hbm] * 4,
        out_specs=(vmem, vmem, hbm, hbm, hbm, hbm),
        scratch_shapes=buffers + semaphores,
        compiler_params=pltpu.CompilerParams(
            collective_id=0, has_side_effects=True, vmem_limit_bytes=60 * 2**20
        ),
        cost_estimate=pl.CostEstimate(flops=14 * 10**9, bytes_accessed=21 * 10**6, transcendentals=10**6),
        name="block_backward",
    )(
        block_input, cotangent, attn_gain[None], attn_bias[None], mlp_gain[None], mlp_bias[None],
        cosine, sine, w_qkv, w_out, w_up, w_down,
    )


def solution(mesh):
    return jax.shard_map(
        on_device,
        mesh=mesh,
        in_specs=(
            P("tensor", "dp"),
            P("tensor", "dp"),
            P("dp"),
            P("dp"),
            P("dp"),
            P("dp"),
            P("dp", "tensor"),
            P("tensor", "dp"),
            P("dp", "tensor"),
            P("tensor", "dp"),
        ),
        out_specs=(
            P("tensor", "dp"),
            P(None, "dp"),
            P("dp", "tensor"),
            P("tensor", "dp"),
            P("dp", "tensor"),
            P("tensor", "dp"),
        ),
        check_vma=False,
    )
```

```python
import functools
import math

import jax
import jax.numpy as jnp
from jax import lax
from jax.experimental import pallas as pl
from jax.experimental.pallas import tpu as pltpu
from jax.sharding import PartitionSpec as P

D = 8192
HD = 64
LENGTH = 512
TOK = 512
W = 512
ROWS = 64
NT = 8
ND = 16
FF = 4096
CH = 256
QKV = 1152
MESH = pl.DeviceIdType.MESH
BF = jnp.bfloat16
F32 = jnp.float32


def dot_nn(a, b):
    return jnp.dot(a, b, preferred_element_type=F32)


def dot_nt(a, b):
    return lax.dot_general(a, b, (((1,), (1,)), ((), ())), preferred_element_type=F32)


def gelu_parts(v):
    half = 0.5 * (1.0 + lax.erf(v * 0.7071067811865476))
    return v * half, half + v * jnp.exp(-0.5 * v * v) * 0.3989422804014327


def rope_columns():
    halfway = HD // 2
    position = (jnp.arange(TOK) % LENGTH).astype(F32)
    frequency = 10000.0 ** (-2.0 * jnp.arange(halfway).astype(F32) / HD)
    angle = frequency[:, None] * position[None, :]
    cosine = jnp.concatenate([jnp.cos(angle), jnp.cos(angle)], 0)
    sine = jnp.concatenate([jnp.sin(angle), jnp.sin(angle)], 0)
    return cosine, sine


def rotate(v, cosine, sine):
    turned = jnp.concatenate([-v[32:], v[:32]], 0)
    return v * cosine + turned * sine


def unrotate(v, cosine, sine):
    scaled = v * sine
    back = jnp.concatenate([scaled[32:], -scaled[:32]], 0)
    return v * cosine + back


class Reduce:
    def __init__(self, place, part, zin, in1, in2m, in2p, zfin, send, recv, split):
        self.place, self.part, self.zin, self.in1 = place, part, zin, in1
        self.in2m, self.in2p, self.zfin, self.send, self.recv = in2m, in2p, zfin, send, recv
        size, a, ma, mb = split
        self.a, self.size = a, size
        self.jobs = ((0, 0, ma, a), (1, 0, ma, a), (0, a, mb, size))

    def copy(self, src, dst, k, device):
        return self.place.remote(src, dst, self.send.at[k], self.recv.at[k], device)

    def block(self, plane, j):
        return self.part.at[self.place.chip(plane, j)]

    def z_first(self, j):
        src = self.block(1, j).at[self.a : self.size]
        return self.copy(src, self.zin.at[j], j, self.place.z_side)

    def one(self, job, way):
        plane, low, mid, high = self.jobs[job]
        here = slice(low, mid) if way == 0 else slice(mid, high)
        device = (self.place.x_up, self.place.x_down)[way]
        return self.copy(self.block(plane, 2).at[here], self.in1.at[plane, here], 4 + 2 * job + way, device)

    def two(self, job, way):
        plane, low, _, high = self.jobs[job]
        here = slice(low, high)
        device = (self.place.x_up, self.place.x_down)[way]
        land = (self.in2m, self.in2p)[way]
        return self.copy(self.block(plane, (1, 3)[way]).at[here], land.at[plane, here], 10 + 2 * job + way, device)

    def z_last(self):
        return self.copy(self.block(1, 0).at[0 : self.a], self.zfin, 16, self.place.z_side)

    def add(self, plane, j, here, more):
        target = self.block(plane, j)
        total = target[here].astype(F32)
        for term in more:
            total = total + term.astype(F32)
        target[here] = total.astype(BF)

    def start(self):
        for job in (1, 0):
            for way in (0, 1):
                self.one(job, way).start()

    def z_merge(self):
        for j in (2, 1, 0, 3):
            self.z_first(j).wait_recv()
            self.add(0, j, slice(self.a, self.size), [self.zin[j]])
            if j == 2:
                self.one(2, 0).start()
                self.one(2, 1).start()

    def step_two(self, job):
        plane, low, mid, high = self.jobs[job]
        for way, here in ((0, slice(low, mid)), (1, slice(mid, high))):
            self.one(job, way).wait_recv()
            self.add(plane, (1, 3)[way], here, [self.in1[plane, here]])
            self.two(job, way).start()

    def step_z(self):
        self.two(1, 0).wait_recv()
        self.two(1, 1).wait_recv()
        here = slice(0, self.a)
        self.add(1, 0, here, [self.in2m[1, here], self.in2p[1, here]])
        self.z_last().start()

    def finish(self):
        for job in (0, 2):
            self.two(job, 0).wait_recv()
            self.two(job, 1).wait_recv()
        self.z_last().wait_recv()

    def total(self, low, high, cols=slice(None)):
        out = self.block(0, 0)[low:high, cols].astype(F32)
        out = out + self.in2m[0, low:high, cols].astype(F32) + self.in2p[0, low:high, cols].astype(F32)
        top = min(high, self.a)
        if top <= low:
            return out
        upper = out[: top - low] + self.zfin[low:top, cols].astype(F32)
        return upper if top == high else jnp.concatenate([upper, out[top - low :]], 0)

    def drain(self):
        for j in range(4):
            self.z_first(j).wait_send()
        for job in range(3):
            for way in range(2):
                self.one(job, way).wait_send()
                self.two(job, way).wait_send()
        self.z_last().wait_send()


class Gather:
    def __init__(self, place, buf, send, recv, split):
        self.place, self.buf, self.send, self.recv = place, buf, send, recv
        size, a, mo, ma = split
        up, down, side = place.x_up, place.x_down, place.z_side
        own, left, right, far = (0, 0), (0, 3), (0, 1), (0, 2)
        z_own, z_left, z_right, z_far = (1, 0), (1, 3), (1, 1), (1, 2)
        self.moves = (
            (own, left, 0, size, up),
            (own, right, 0, size, down),
            (own, z_own, 0, size, side),
            (left, far, 0, mo, up),
            (right, far, mo, size, down),
            (left, z_left, a, size, side),
            (right, z_right, a, size, side),
            (far, z_far, a, size, side),
            (z_own, z_left, 0, a, up),
            (z_own, z_right, 0, a, down),
            (z_left, z_far, 0, ma, up),
            (z_right, z_far, ma, a, down),
        )

    def index(self, where):
        return self.place.chip(*where) * 2 + self.place.c

    def copy(self, index, low, high, k, device):
        at = self.buf.at[index, low:high]
        return self.place.remote(at, at, self.send.at[k], self.recv.at[k], device)

    def go(self, *moves):
        for k in moves:
            src, _, low, high, device = self.moves[k]
            self.copy(self.index(src), low, high, k, device).start()

    def wait(self, *moves):
        for k in moves:
            _, dst, low, high, device = self.moves[k]
            self.copy(self.index(dst), low, high, k, device).wait_recv()

    def hand(self, plane, j, core):
        index = self.place.chip(plane, j) * 2 + core
        k = 12 + j + 4 * plane
        at = self.buf.at[index]
        return self.place.remote(at, at, self.send.at[k], self.recv.at[k], self.place.partner)

    def give(self, *wheres):
        for plane, j in wheres:
            self.hand(plane, j, self.place.c).start()

    def take(self, plane, j):
        self.hand(plane, j, self.place.other).wait_recv()

    def start(self):
        self.go(0, 1, 2)
        self.give((0, 0))

    def step_one(self):
        self.wait(0)
        self.go(3, 5)
        self.wait(1)
        self.go(4, 6)
        self.wait(2)
        self.go(8, 9)
        self.give((0, 3), (0, 1), (1, 0))

    def step_two(self):
        self.wait(3, 4)
        self.go(7)
        self.wait(8)
        self.go(10)
        self.wait(9)
        self.go(11)
        self.give((0, 2))

    def step_three(self):
        self.wait(5, 6)
        self.give((1, 3), (1, 1))
        self.wait(7, 10, 11)
        self.give((1, 2))

    def drain(self):
        for k, (src, _, low, high, device) in enumerate(self.moves):
            self.copy(self.index(src), low, high, k, device).wait_send()
        for plane in range(2):
            for j in range(4):
                self.hand(plane, j, self.place.c).wait_send()


class Place:
    def __init__(self):
        self.d = d = lax.axis_index("dp")
        self.t = t = lax.axis_index("tensor")
        self.c = d % 2
        self.other = 1 - self.c
        self.x = x = (d // 2) % 4
        self.z = z = d // 8
        self.partner = (d + 1 - 2 * self.c, t)
        self.x_up = (z * 8 + ((x + 1) % 4) * 2 + self.c, t)
        self.x_down = (z * 8 + ((x + 3) % 4) * 2 + self.c, t)
        self.z_side = ((1 - z) * 8 + x * 2 + self.c, t)
        self.x_even = (z * 8 + (x + 1 - 2 * (x % 2)) * 2 + self.c, t)
        self.x_odd = (z * 8 + ((x + 3 + 2 * (x % 2)) % 4) * 2 + self.c, t)

    def chip(self, plane, j):
        return ((self.z + plane) % 2) * 4 + (self.x + j) % 4

    def remote(self, src, dst, send, recv, device):
        return pltpu.make_async_remote_copy(
            src_ref=src, dst_ref=dst, send_sem=send, recv_sem=recv, device_id=device, device_id_type=MESH
        )


class Doubling:
    def __init__(self, place, out, into, send, recv):
        self.place, self.out, self.into, self.send, self.recv = place, out, into, send, recv
        self.devices = (place.z_side, place.x_even, place.x_odd)

    def copy(self, k):
        return self.place.remote(
            self.out.at[k], self.into.at[k], self.send.at[k], self.recv.at[k], self.devices[k]
        )

    def start(self, value):
        self.out[0] = value
        self.copy(0).start()

    def step(self, k):
        self.copy(k - 1).wait_recv()
        total = self.out[k - 1].astype(F32) + self.into[k - 1].astype(F32)
        if k == 3:
            return total
        self.out[k] = total.astype(BF)
        self.copy(k).start()
        return total

    def drain(self):
        for k in range(3):
            self.copy(k).wait_send()


def kernel(
    x_loc, c_loc, ag, ab, mg, mb, cosine, sine, wq_hbm, wo_hbm, wu_hbm, wd_hbm,
    out_x, out_n, out_q, out_o, out_u, out_d,
    xs, cs, st_in, st, wq, wqt, wo, wu, wd, ain, min_, ain_t, min_t,
    pa, pa_in, pkv, pkv_in, kvo, kvi, kvx,
    t_part, t_z, t_1, t_2m, t_2p, t_f,
    d_out, d_in, d_part, d_z, d_1, d_2m, d_2p, d_f,
    h_out, h_in, h_part, h_z, h_1, h_2m, h_2p, h_f,
    act, hid, hq, proj, pp, pp_in, ppo, ppi,
    abt, mbt, ngb, ngr, mom, momr, nrm, nrmr, m2,
    w_sem, x_s, x_r, c_s, c_r, st_s, st_r, tt_s, tt_r,
    p_s, p_r, dp_s, dp_r, hp_s, hp_r, ts, tr, ds, dr, hs, hr, kv_s, kv_r, pp_s, pp_r,
    as_, ar, gs, gr, qs, qr, o_sem, u_sem, d_sem,
    ng_s, ng_r, mo_s, mo_r, nr_s, nr_r, m2_s, m2_r,
):
    place = Place()
    d, t, c, other, partner, remote = place.d, place.t, place.c, place.other, place.partner, place.remote

    def rows(index, size):
        return pl.ds(pl.multiple_of(index * size, size), size)

    def loop(low, high, f):
        def body(k, carry):
            f(k)
            return carry

        lax.fori_loop(low, high, body, 0)

    weights = [
        pltpu.make_async_copy(src, dst, w_sem.at[i])
        for i, (src, dst) in enumerate([(wd_hbm, wd), (wq_hbm, wq), (wo_hbm, wo), (wu_hbm, wu)])
    ]
    for copy in weights:
        copy.start()

    barrier = pltpu.get_barrier_semaphore()
    loop(
        1, NT,
        lambda k: pl.semaphore_signal(barrier, inc=1, device_id=(d, (t + k) % NT), device_id_type=MESH),
    )
    loop(
        1, ND,
        lambda k: pl.semaphore_signal(barrier, inc=1, device_id=((d + k) % ND, t), device_id_type=MESH),
    )
    pl.semaphore_wait(barrier, NT - 1 + ND - 1)

    own = rows(t, ROWS)

    def send_c(k):
        return remote(c_loc, cs.at[own], c_s.at[k], c_r.at[k], (d, (t + k) % NT))

    def send_x(k):
        return remote(x_loc, xs.at[own], x_s.at[k], x_r.at[k], (d, (t + k) % NT))

    def send_st(k):
        return remote(st_in.at[0], st_in.at[k], st_s.at[k], st_r.at[k], ((d + k) % ND, t))

    def send_tt(k):
        return remote(st.at[own], st.at[own], tt_s.at[k], tt_r.at[k], (d, (t + k) % NT))

    loop(1, NT, lambda k: send_c(k).start())
    lane = lax.broadcasted_iota(jnp.int32, (ROWS, 128), 1)
    xf = x_loc[...].astype(F32)
    st_in[0] = jnp.where(
        lane < 64, jnp.sum(xf, 1, keepdims=True), jnp.sum(xf * xf, 1, keepdims=True)
    )
    loop(1, ND, lambda k: send_st(k).start())
    cs[own, :] = c_loc[...]
    xs[own, :] = x_loc[...]
    weights[1].wait()
    for i in range(QKV // 128):
        wqt[i * 128 : (i + 1) * 128, :] = wq[:, i * 128 : (i + 1) * 128].T
    loop(1, ND, lambda k: send_st(k).wait_recv())
    total = st_in[0]
    for k in range(1, ND):
        total = total + st_in[k]
    st[own, :] = total
    loop(1, NT, lambda k: send_tt(k).start())
    loop(1, NT, lambda k: send_c(k).wait_recv())
    loop(1, NT, lambda k: send_x(k).start())

    def produce(chunk, job, out, into, send, recv):
        def pair(q, k):
            return remote(out.at[q], into.at[q], send.at[k], recv.at[k], partner)

        def body(i):
            @pl.when(i < 4)
            def _():
                j = (2 + 3 * i) % 4
                for plane in (1, 0):
                    q = place.chip(plane, j)
                    out[q] = chunk(2 * q + other).astype(BF)
                    pair(q, 2 * i + plane).start()
                for plane in (1, 0):
                    q = place.chip(plane, j)
                    job.part[q] = chunk(2 * q + c).astype(BF)

            @pl.when(i > 0)
            def _():
                j = (3 * i - 1) % 4
                for plane in (1, 0):
                    q = place.chip(plane, j)
                    pair(q, 2 * (i - 1) + plane).wait_recv()
                    job.part[q] = (job.part[q].astype(F32) + into[q].astype(F32)).astype(BF)
                    if plane == 1:
                        job.z_first(j).start()

            @pl.when(i == 1)
            def _():
                job.start()

        loop(0, 5, body)

    def pair_drain(out, into, send, recv):
        loop(0, 8, lambda k: remote(out.at[k], into.at[k], send.at[k], recv.at[k], partner).wait_send())

    down = Reduce(place, d_part, d_z, d_1, d_2m, d_2p, d_f, ds, dr, (256, 144, 80, 192))
    up = Reduce(place, h_part, h_z, h_1, h_2m, h_2p, h_f, hs, hr, (512, 288, 160, 384))
    attn = Reduce(place, t_part, t_z, t_1, t_2m, t_2p, t_f, ts, tr, (128, 80, 48, 96))
    weights[0].wait()
    produce(lambda p: dot_nt(wd[rows(p, CH), :], cs[...]), down, d_out, d_in, dp_s, dp_r)

    loop(1, NT, lambda k: send_x(k).wait_recv())
    loop(1, NT, lambda k: send_tt(k).wait_recv())

    def norm_rows(block, size):
        here = rows(block, size)
        average = st[here, 0:1] * (1.0 / D)
        spread = st[here, 64:65] * (1.0 / D) - average * average
        inverse = lax.rsqrt(spread + 1e-05)
        return (xs[here, :].astype(F32) - average) * inverse, inverse

    def norm_body(block):
        here = rows(block, ROWS)
        normed, _ = norm_rows(block, ROWS)
        ain[here, :] = (normed * ag[...] + ab[...]).astype(BF)
        min_[here, :] = (normed * mg[...] + mb[...]).astype(BF)

    loop(0, NT, norm_body)

    weights[2].wait()

    def part_body(i):
        og = dot_nt(wo[rows(i, 256), :], cs[...]).astype(BF)
        pa[pl.ds(i * 2, 2), :, 0:64, :] = og.reshape(2, 2, 64, TOK)
        qq = dot_nt(wqt[rows(i, 256), :], ain[...]).astype(BF)
        pa[pl.ds(i * 2, 2), :, 64:128, :] = qq.reshape(2, 2, 64, TOK)

    pkv[...] = dot_nt(wqt[1024:1152, :], ain[...]).astype(BF).reshape(2, 64, TOK)
    give_kv = remote(pkv.at[other], pkv_in, p_s.at[0], p_r.at[0], partner)
    give_kv.start()
    loop(0, 4, part_body)
    give_a = remote(pa.at[:, other], pa_in, p_s.at[1], p_r.at[1], partner)
    give_a.start()

    down.z_merge()
    down.step_two(1)
    down.step_two(0)

    kv_sum = Doubling(place, kvo, kvi, kv_s, kv_r)
    give_kv.wait_recv()
    kv_sum.start((pkv[c].astype(F32) + pkv_in[...].astype(F32)).astype(BF))
    give_a.wait_recv()

    def sum_a(q):
        t_part[q] = (pa[q, c].astype(F32) + pa_in[q].astype(F32)).astype(BF)

    loop(0, 8, sum_a)
    for j in (2, 1, 0, 3):
        attn.z_first(j).start()
    attn.start()

    weights[3].wait()
    produce(lambda p: dot_nn(min_[...], wu[:, rows(p, CH)]), up, h_out, h_in, hp_s, hp_r)

    down.step_two(2)
    down.step_z()
    kv_sum.step(1)
    attn.z_merge()
    attn.step_two(1)
    attn.step_two(0)
    kv_sum.step(2)
    up.z_merge()
    up.step_two(1)
    up.step_two(0)
    attn.step_two(2)
    attn.step_z()
    ain_t[...] = ain[...].T
    min_t[...] = min_[...].T

    attn.finish()
    og = attn.total(0, 64).astype(BF)
    q_sum = attn.total(64, 128)
    kv_total = kv_sum.step(3)

    co, si = cosine[...], sine[...]
    queries_f = rotate(q_sum, co, si)
    queries = queries_f.astype(BF)
    kvx[c] = jnp.where(c == 0, rotate(kv_total, co, si), kv_total).astype(BF)
    give = remote(kvx.at[c], kvx.at[c], p_s.at[2], p_r.at[2], partner)
    give.start()
    queries_t = queries_f.T.astype(BF)
    og_tf = og.astype(F32).T
    og_t = og_tf.astype(BF)
    give.wait_recv()
    keys = kvx[0]
    values = kvx[1]
    scaling = 1.0 / math.sqrt(HD)
    key_grad = jnp.zeros((HD, TOK), F32)
    value_grad = jnp.zeros((HD, TOK), F32)
    outs, qgs = [], []
    for n in range(4):
        low, high = n * 128, (n + 1) * 128
        scores = dot_nn(queries_t[low:high], keys) * scaling
        causal = lax.broadcasted_iota(jnp.int32, (128, TOK), 0) + low >= lax.broadcasted_iota(
            jnp.int32, (128, TOK), 1
        )
        raised = jnp.where(causal, jnp.exp(scores), 0.0)
        prob = raised / jnp.sum(raised, -1, keepdims=True)
        prob_low = prob.astype(BF)
        head = dot_nt(prob_low, values).astype(BF).astype(F32)
        dropped = dot_nn(og_t[low:high], values)
        row_dot = jnp.sum(og_tf[low:high] * head, -1, keepdims=True)
        score_grad = (prob * (dropped - row_dot) * scaling).astype(BF)
        qgs.append(dot_nt(keys, score_grad))
        key_grad = key_grad + dot_nn(queries[:, low:high], score_grad)
        value_grad = value_grad + dot_nn(og[:, low:high], prob_low)
        outs.append(head.T)
    hq[d, 0:64, :] = jnp.concatenate(outs, 1).astype(BF)
    hq[d, 64:128, :] = unrotate(jnp.concatenate(qgs, 1), co, si).astype(BF)
    pp[0] = unrotate(key_grad, co, si).astype(BF)
    pp[1] = value_grad.astype(BF)

    heads = Gather(place, hq, qs, qr, (128, 80, 64, 48))
    heads.start()
    give_pp = remote(pp.at[other], pp_in, p_s.at[3], p_r.at[3], partner)
    give_pp.start()

    up.step_two(2)
    up.step_z()
    give_pp.wait_recv()
    pp_sum = Doubling(place, ppo, ppi, pp_s, pp_r)
    pp_sum.start((pp[c].astype(F32) + pp_in[...].astype(F32)).astype(BF))
    heads.step_one()
    pp_sum.step(1)
    down.finish()
    up.finish()

    for h in range(2):
        cols = slice(h * 128, (h + 1) * 128)
        hidden = up.total(0, 512, cols).T
        dact = down.total(h * 128, (h + 1) * 128)
        value, slope = gelu_parts(hidden)
        act[d, cols, :] = value.astype(BF)
        hid[d, cols, :] = (dact * slope).astype(BF)

    gather_act = Gather(place, act, as_, ar, (256, 144, 128, 80))
    gather_hid = Gather(place, hid, gs, gr, (256, 144, 128, 80))
    gather_act.start()
    gather_hid.start()

    heads.step_two()
    pp_sum.step(2)
    heads.step_three()
    there = rows(16 + c, 64)
    proj[there, :] = pp_sum.step(3).astype(BF)
    give_pj = remote(proj.at[there], proj.at[there], p_s.at[4], p_r.at[4], partner)
    give_pj.start()
    for plane in range(2):
        for j in range(4):
            heads.take(plane, j)
    give_pj.wait_recv()

    def go_body(i):
        four = hq[pl.ds(i * 4, 4), 0:64, :].reshape(256, TOK)
        wo[rows(i, 256), :] = dot_nn(four, cs[...]).astype(BF)
        proj[rows(i, 256), :] = hq[pl.ds(i * 4, 4), 64:128, :].reshape(256, TOK)

    loop(0, 4, go_body)
    out_o_copy = pltpu.make_async_copy(wo, out_o, o_sem.at[0])
    out_o_copy.start()

    def ab_body(i):
        abt[rows(i, 128), :] = dot_nn(wq[rows(i, 128), :], proj[...])
        wq[rows(i, 128), :] = dot_nt(ain_t[rows(i, 128), :], proj[...]).astype(BF)

    loop(0, 4, ab_body)
    out_q_copy = pltpu.make_async_copy(wq, out_q, o_sem.at[1])
    out_q_copy.start()

    mbt[...] = jnp.zeros((W, TOK), F32)

    def out_d_copy(p):
        return pltpu.make_async_copy(wd.at[rows(p, CH)], out_d.at[rows(p, CH)], d_sem.at[p])

    def out_u_copy(p):
        return pltpu.make_async_copy(wu.at[:, rows(p, CH)], out_u.at[:, rows(p, CH)], u_sem.at[p])

    def consume(p):
        wd[rows(p, CH), :] = dot_nn(act[p], cs[...]).astype(BF)
        out_d_copy(p).start()
        mbt[...] += dot_nn(wu[:, rows(p, CH)], hid[p])
        wu[:, rows(p, CH)] = dot_nt(min_t[...], hid[p]).astype(BF)
        out_u_copy(p).start()

    def ff_body(i):
        @pl.when(i == 1)
        def _():
            gather_act.step_one()
            gather_hid.step_one()

        @pl.when(i == 3)
        def _():
            gather_act.step_two()
            gather_hid.step_two()

        @pl.when(i == 5)
        def _():
            gather_act.step_three()
            gather_hid.step_three()

        plane = i // 5 + (i + 6) // 7 - (i + 5) // 7
        k = (i + 1) % 3
        j = ((i + 1) // 3 + 1) // 2 * (1 + 2 * k - 3 * (k // 2))
        consume(place.chip(plane, j) * 2 + c)
        gather_act.take(plane, j)
        gather_hid.take(plane, j)
        consume(place.chip(plane, j) * 2 + other)

    loop(0, 8, ff_body)

    lane2 = lax.broadcasted_iota(jnp.int32, (128, 128), 1)

    def tail_body(n):
        here = rows(n, 128)
        a_back = abt[:, here].T
        m_back = mbt[:, here].T
        normed, _ = norm_rows(n, 128)
        grad = a_back * ag[...] + m_back * mg[...]
        ngb[here, :] = grad.astype(BF)
        mom[here, :] = jnp.where(
            lane2 < 64, jnp.sum(grad, 1, keepdims=True), jnp.sum(grad * normed, 1, keepdims=True)
        )
        sums = jnp.concatenate(
            [
                jnp.sum(a_back * normed, 0, keepdims=True),
                jnp.sum(a_back, 0, keepdims=True),
                jnp.sum(m_back * normed, 0, keepdims=True),
                jnp.sum(m_back, 0, keepdims=True),
                jnp.zeros((4, W), F32),
            ],
            0,
        )
        nrm[...] += sums

    nrm[...] = jnp.zeros((8, W), F32)
    loop(0, 4, tail_body)

    def send_ng(k):
        p = (t + k) % NT
        return remote(ngb.at[rows(p, ROWS)], ngr.at[k], ng_s.at[k], ng_r.at[k], (d, p))

    def send_mo(k):
        p = (t + k) % NT
        return remote(mom.at[rows(p, ROWS)], momr.at[k], mo_s.at[k], mo_r.at[k], (d, p))

    def send_nr(k):
        return remote(nrm, nrmr.at[k], nr_s.at[k], nr_r.at[k], (d, (t + k) % NT))

    def start_tail(k):
        send_mo(k).start()
        send_ng(k).start()
        send_nr(k).start()

    loop(1, NT, start_tail)
    loop(1, NT, lambda k: send_mo(k).wait_recv())
    acc = mom[own, :]
    for k in range(1, NT):
        acc = acc + momr[k]
    m2[0] = acc

    def send_m2(k):
        return remote(m2.at[0], m2.at[k], m2_s.at[k], m2_r.at[k], ((d + k) % ND, t))

    loop(1, ND, lambda k: send_m2(k).start())
    loop(1, NT, lambda k: send_ng(k).wait_recv())
    loop(1, NT, lambda k: send_nr(k).wait_recv())
    norm_total = nrm[...]
    for k in range(1, NT):
        norm_total = norm_total + nrmr[k]
    out_n[...] = norm_total[0:4, :]
    grad = ngb[own, :].astype(F32)
    for k in range(1, NT):
        grad = grad + ngr[k].astype(F32)
    loop(1, ND, lambda k: send_m2(k).wait_recv())
    moments = m2[0]
    for k in range(1, ND):
        moments = moments + m2[k]
    first = moments[:, 0:1] * (1.0 / D)
    second = moments[:, 64:65] * (1.0 / D)
    normed, inverse = norm_rows(t, ROWS)
    out_x[...] = (c_loc[...].astype(F32) + inverse * (grad - first - normed * second)).astype(BF)

    def drain_t(k):
        send_c(k).wait_send()
        send_x(k).wait_send()
        send_tt(k).wait_send()
        send_mo(k).wait_send()
        send_ng(k).wait_send()
        send_nr(k).wait_send()

    def drain_d(k):
        send_st(k).wait_send()
        send_m2(k).wait_send()

    def drain_o(p):
        out_d_copy(p).wait()
        out_u_copy(p).wait()

    loop(1, NT, drain_t)
    loop(1, ND, drain_d)
    for copy in (give_a, give_kv, give, give_pp, give_pj):
        copy.wait_send()
    pair_drain(d_out, d_in, dp_s, dp_r)
    pair_drain(h_out, h_in, hp_s, hp_r)
    for job in (down, up, attn, kv_sum, pp_sum, heads, gather_act, gather_hid):
        job.drain()
    out_o_copy.wait()
    out_q_copy.wait()
    loop(0, ND, drain_o)


def on_device(
    block_input, cotangent, attn_gain, attn_bias, mlp_gain, mlp_bias, w_qkv, w_out, w_up, w_down
):
    cosine, sine = rope_columns()
    vmem = pl.BlockSpec(memory_space=pltpu.VMEM)
    hbm = pl.BlockSpec(memory_space=pl.ANY)
    dma = pltpu.SemaphoreType.DMA

    def buf(*shape):
        return pltpu.VMEM(shape, BF)

    def wide(*shape):
        return pltpu.VMEM(shape, F32)

    def sums(size, a, width):
        return [
            buf(8, size, width), buf(4, size - a, width), buf(2, size, width),
            buf(2, size, width), buf(2, size, width), buf(a, width),
        ]

    buffers = [
        buf(TOK, W), buf(TOK, W), wide(ND, ROWS, 128), wide(TOK, 128),
        buf(W, QKV), buf(QKV, W), buf(1024, W), buf(W, FF), buf(FF, W),
        buf(TOK, W), buf(TOK, W), buf(W, TOK), buf(W, TOK),
        buf(8, 2, 128, TOK), buf(8, 128, TOK), buf(2, 64, TOK), buf(64, TOK),
        buf(3, 64, TOK), buf(3, 64, TOK), buf(2, 64, TOK),
        *sums(128, 80, TOK),
        buf(8, CH, TOK), buf(8, CH, TOK), *sums(256, 144, TOK),
        buf(8, TOK, CH), buf(8, TOK, CH), *sums(512, 288, CH),
        buf(ND, CH, TOK), buf(ND, CH, TOK), buf(ND, 128, TOK), buf(QKV, TOK),
        buf(2, 64, TOK), buf(64, TOK), buf(3, 64, TOK), buf(3, 64, TOK),
        wide(W, TOK), wide(W, TOK), buf(TOK, W), buf(NT, ROWS, W),
        wide(TOK, 128), wide(NT, ROWS, 128), wide(8, W), wide(NT, 8, W), wide(ND, ROWS, 128),
    ]
    counts = [4, 8, 8, 8, 8, 16, 16, 8, 8]
    counts += [5, 5, 8, 8, 8, 8] + [17] * 6 + [3] * 4
    counts += [20] * 6 + [2, 16, 16, 8, 8, 8, 8, 8, 8, 16, 16]
    semaphores = [dma((n,)) for n in counts]
    return pl.pallas_call(
        kernel,
        out_shape=(
            jax.ShapeDtypeStruct((ROWS, W), BF),
            jax.ShapeDtypeStruct((4, W), F32),
            jax.ShapeDtypeStruct((W, QKV), BF),
            jax.ShapeDtypeStruct((1024, W), BF),
            jax.ShapeDtypeStruct((W, FF), BF),
            jax.ShapeDtypeStruct((FF, W), BF),
        ),
        in_specs=[vmem] * 8 + [hbm] * 4,
        out_specs=(vmem, vmem, hbm, hbm, hbm, hbm),
        scratch_shapes=buffers + semaphores,
        compiler_params=pltpu.CompilerParams(
            collective_id=0, has_side_effects=True, vmem_limit_bytes=60 * 2**20
        ),
        cost_estimate=pl.CostEstimate(flops=14 * 10**9, bytes_accessed=21 * 10**6, transcendentals=10**6),
        name="block_backward",
    )(
        block_input, cotangent, attn_gain[None], attn_bias[None], mlp_gain[None], mlp_bias[None],
        cosine, sine, w_qkv, w_out, w_up, w_down,
    )


def solution(mesh):
    return jax.shard_map(
        on_device,
        mesh=mesh,
        in_specs=(
            P("tensor", "dp"),
            P("tensor", "dp"),
            P("dp"),
            P("dp"),
            P("dp"),
            P("dp"),
            P("dp", "tensor"),
            P("tensor", "dp"),
            P("dp", "tensor"),
            P("tensor", "dp"),
        ),
        out_specs=(
            P("tensor", "dp"),
            P(None, "dp"),
            P("dp", "tensor"),
            P("tensor", "dp"),
            P("dp", "tensor"),
            P("tensor", "dp"),
        ),
        check_vma=False,
    )
```

```python
import functools
import math

import jax
import jax.numpy as jnp
from jax import lax
from jax.experimental import pallas as pl
from jax.experimental.pallas import tpu as pltpu
from jax.sharding import PartitionSpec as P

D = 8192
HD = 64
LENGTH = 512
TOK = 512
W = 512
ROWS = 64
NT = 8
ND = 16
FF = 4096
CH = 256
QKV = 1152
MESH = pl.DeviceIdType.MESH
BF = jnp.bfloat16
F32 = jnp.float32


def dot_nn(a, b):
    return jnp.dot(a, b, preferred_element_type=F32)


def dot_nt(a, b):
    return lax.dot_general(a, b, (((1,), (1,)), ((), ())), preferred_element_type=F32)


def gelu_parts(v):
    half = 0.5 * (1.0 + lax.erf(v * 0.7071067811865476))
    return v * half, half + v * jnp.exp(-0.5 * v * v) * 0.3989422804014327


def rope_columns():
    halfway = HD // 2
    position = (jnp.arange(TOK) % LENGTH).astype(F32)
    frequency = 10000.0 ** (-2.0 * jnp.arange(halfway).astype(F32) / HD)
    angle = frequency[:, None] * position[None, :]
    cosine = jnp.concatenate([jnp.cos(angle), jnp.cos(angle)], 0)
    sine = jnp.concatenate([jnp.sin(angle), jnp.sin(angle)], 0)
    return cosine, sine


def rotate(v, cosine, sine):
    turned = jnp.concatenate([-v[32:], v[:32]], 0)
    return v * cosine + turned * sine


def unrotate(v, cosine, sine):
    scaled = v * sine
    back = jnp.concatenate([scaled[32:], -scaled[:32]], 0)
    return v * cosine + back


class Reduce:
    def __init__(self, place, part, zin, in1, in2m, in2p, zfin, send, recv, split):
        self.place, self.part, self.zin, self.in1 = place, part, zin, in1
        self.in2m, self.in2p, self.zfin, self.send, self.recv = in2m, in2p, zfin, send, recv
        size, a, ma, mb = split
        self.a, self.size = a, size
        self.jobs = ((0, 0, ma, a), (1, 0, ma, a), (0, a, mb, size))

    def copy(self, src, dst, k, device):
        return self.place.remote(src, dst, self.send.at[k], self.recv.at[k], device)

    def block(self, plane, j):
        return self.part.at[self.place.chip(plane, j)]

    def z_first(self, j):
        src = self.block(1, j).at[self.a : self.size]
        return self.copy(src, self.zin.at[j], j, self.place.z_side)

    def one(self, job, way):
        plane, low, mid, high = self.jobs[job]
        here = slice(low, mid) if way == 0 else slice(mid, high)
        device = (self.place.x_up, self.place.x_down)[way]
        return self.copy(self.block(plane, 2).at[here], self.in1.at[plane, here], 4 + 2 * job + way, device)

    def two(self, job, way):
        plane, low, _, high = self.jobs[job]
        here = slice(low, high)
        device = (self.place.x_up, self.place.x_down)[way]
        land = (self.in2m, self.in2p)[way]
        return self.copy(self.block(plane, (1, 3)[way]).at[here], land.at[plane, here], 10 + 2 * job + way, device)

    def z_last(self):
        return self.copy(self.block(1, 0).at[0 : self.a], self.zfin, 16, self.place.z_side)

    def add(self, plane, j, here, more):
        target = self.block(plane, j)
        total = target[here].astype(F32)
        for term in more:
            total = total + term.astype(F32)
        target[here] = total.astype(BF)

    def start(self):
        for job in (1, 0):
            for way in (0, 1):
                self.one(job, way).start()

    def z_merge(self):
        for j in (2, 1, 0, 3):
            self.z_first(j).wait_recv()
            self.add(0, j, slice(self.a, self.size), [self.zin[j]])
            if j == 2:
                self.one(2, 0).start()
                self.one(2, 1).start()

    def step_two(self, job):
        plane, low, mid, high = self.jobs[job]
        for way, here in ((0, slice(low, mid)), (1, slice(mid, high))):
            self.one(job, way).wait_recv()
            self.add(plane, (1, 3)[way], here, [self.in1[plane, here]])
            self.two(job, way).start()

    def step_z(self):
        self.two(1, 0).wait_recv()
        self.two(1, 1).wait_recv()
        here = slice(0, self.a)
        self.add(1, 0, here, [self.in2m[1, here], self.in2p[1, here]])
        self.z_last().start()

    def finish(self):
        for job in (0, 2):
            self.two(job, 0).wait_recv()
            self.two(job, 1).wait_recv()
        self.z_last().wait_recv()

    def total(self, low, high, cols=slice(None)):
        out = self.block(0, 0)[low:high, cols].astype(F32)
        out = out + self.in2m[0, low:high, cols].astype(F32) + self.in2p[0, low:high, cols].astype(F32)
        top = min(high, self.a)
        if top <= low:
            return out
        upper = out[: top - low] + self.zfin[low:top, cols].astype(F32)
        return upper if top == high else jnp.concatenate([upper, out[top - low :]], 0)

    def drain(self):
        for j in range(4):
            self.z_first(j).wait_send()
        for job in range(3):
            for way in range(2):
                self.one(job, way).wait_send()
                self.two(job, way).wait_send()
        self.z_last().wait_send()


class Gather:
    def __init__(self, place, buf, send, recv, split):
        self.place, self.buf, self.send, self.recv = place, buf, send, recv
        size, a, mo, ma = split
        up, down, side = place.x_up, place.x_down, place.z_side
        own, left, right, far = (0, 0), (0, 3), (0, 1), (0, 2)
        z_own, z_left, z_right, z_far = (1, 0), (1, 3), (1, 1), (1, 2)
        self.moves = (
            (own, left, 0, size, up),
            (own, right, 0, size, down),
            (own, z_own, 0, size, side),
            (left, far, 0, mo, up),
            (right, far, mo, size, down),
            (left, z_left, a, size, side),
            (right, z_right, a, size, side),
            (far, z_far, a, size, side),
            (z_own, z_left, 0, a, up),
            (z_own, z_right, 0, a, down),
            (z_left, z_far, 0, ma, up),
            (z_right, z_far, ma, a, down),
        )

    def index(self, where):
        return self.place.chip(*where) * 2 + self.place.c

    def copy(self, index, low, high, k, device):
        at = self.buf.at[index, low:high]
        return self.place.remote(at, at, self.send.at[k], self.recv.at[k], device)

    def go(self, *moves):
        for k in moves:
            src, _, low, high, device = self.moves[k]
            self.copy(self.index(src), low, high, k, device).start()

    def wait(self, *moves):
        for k in moves:
            _, dst, low, high, device = self.moves[k]
            self.copy(self.index(dst), low, high, k, device).wait_recv()

    def hand(self, plane, j, core):
        index = self.place.chip(plane, j) * 2 + core
        k = 12 + j + 4 * plane
        at = self.buf.at[index]
        return self.place.remote(at, at, self.send.at[k], self.recv.at[k], self.place.partner)

    def give(self, *wheres):
        for plane, j in wheres:
            self.hand(plane, j, self.place.c).start()

    def take(self, plane, j):
        self.hand(plane, j, self.place.other).wait_recv()

    def start(self):
        self.go(0, 1, 2)
        self.give((0, 0))

    def step_one(self):
        self.wait(0)
        self.go(3, 5)
        self.wait(1)
        self.go(4, 6)
        self.wait(2)
        self.go(8, 9)
        self.give((0, 3), (0, 1), (1, 0))

    def step_two(self):
        self.wait(3, 4)
        self.go(7)
        self.wait(8)
        self.go(10)
        self.wait(9)
        self.go(11)
        self.give((0, 2))

    def step_three(self):
        self.wait(5, 6)
        self.give((1, 3), (1, 1))

    def step_four(self):
        self.wait(7, 10, 11)
        self.give((1, 2))

    def drain(self):
        for k, (src, _, low, high, device) in enumerate(self.moves):
            self.copy(self.index(src), low, high, k, device).wait_send()
        for plane in range(2):
            for j in range(4):
                self.hand(plane, j, self.place.c).wait_send()


class Spread:
    def __init__(self, place, buf, send, recv):
        self.place, self.buf, self.send, self.recv = place, buf, send, recv
        up, down, side = place.y_up, place.y_down, place.half_side
        own, left, right, far = (0, 0), (0, 3), (0, 1), (0, 2)
        h_own, h_left, h_right, h_far = (1, 0), (1, 3), (1, 1), (1, 2)
        mid = ROWS // 2
        self.moves = (
            (own, left, 0, ROWS, up),
            (own, right, 0, ROWS, down),
            (own, h_own, 0, ROWS, side),
            (left, far, 0, mid, up),
            (right, far, mid, ROWS, down),
            (h_own, h_left, 0, ROWS, up),
            (h_own, h_right, 0, ROWS, down),
            (h_left, h_far, 0, mid, up),
            (h_right, h_far, mid, ROWS, down),
        )

    def copy(self, where, low, high, k, device):
        first = pl.multiple_of(self.place.block(*where) * ROWS + low, 32)
        at = self.buf.at[pl.ds(first, high - low)]
        return self.place.remote(at, at, self.send.at[k], self.recv.at[k], device)

    def go(self, *moves):
        for k in moves:
            src, _, low, high, device = self.moves[k]
            self.copy(src, low, high, k, device).start()

    def wait(self, *moves):
        for k in moves:
            _, dst, low, high, device = self.moves[k]
            self.copy(dst, low, high, k, device).wait_recv()

    def start(self):
        self.go(2, 0, 1)

    def step_one(self):
        self.wait(2)
        self.go(5, 6)
        self.wait(0)
        self.go(3)
        self.wait(1)
        self.go(4)

    def step_two(self):
        self.wait(5)
        self.go(7)
        self.wait(6)
        self.go(8)

    def step_three(self):
        self.wait(3, 4, 7, 8)

    def drain(self):
        for k, (src, _, low, high, device) in enumerate(self.moves):
            self.copy(src, low, high, k, device).wait_send()


class Place:
    def __init__(self):
        self.d = d = lax.axis_index("dp")
        self.t = t = lax.axis_index("tensor")
        self.c = d % 2
        self.other = 1 - self.c
        self.x = x = (d // 2) % 4
        self.z = z = d // 8
        self.partner = (d + 1 - 2 * self.c, t)
        self.x_up = (z * 8 + ((x + 1) % 4) * 2 + self.c, t)
        self.x_down = (z * 8 + ((x + 3) % 4) * 2 + self.c, t)
        self.z_side = ((1 - z) * 8 + x * 2 + self.c, t)
        self.x_even = (z * 8 + (x + 1 - 2 * (x % 2)) * 2 + self.c, t)
        self.x_odd = (z * 8 + ((x + 3 + 2 * (x % 2)) % 4) * 2 + self.c, t)
        self.y = y = t // 2
        self.half = half = t % 2
        self.y_up = (d, ((y + 1) % 4) * 2 + half)
        self.y_down = (d, ((y + 3) % 4) * 2 + half)
        self.half_side = (d, y * 2 + 1 - half)

    def block(self, plane, j):
        return ((self.y + j) % 4) * 2 + (self.half + plane) % 2

    def chip(self, plane, j):
        return ((self.z + plane) % 2) * 4 + (self.x + j) % 4

    def remote(self, src, dst, send, recv, device):
        return pltpu.make_async_remote_copy(
            src_ref=src, dst_ref=dst, send_sem=send, recv_sem=recv, device_id=device, device_id_type=MESH
        )


class Doubling:
    def __init__(self, place, out, into, send, recv):
        self.place, self.out, self.into, self.send, self.recv = place, out, into, send, recv
        self.devices = (place.z_side, place.x_even, place.x_odd)

    def copy(self, k):
        return self.place.remote(
            self.out.at[k], self.into.at[k], self.send.at[k], self.recv.at[k], self.devices[k]
        )

    def start(self, value):
        self.out[0] = value
        self.copy(0).start()

    def step(self, k):
        self.copy(k - 1).wait_recv()
        total = self.out[k - 1].astype(F32) + self.into[k - 1].astype(F32)
        if k == 3:
            return total
        self.out[k] = total.astype(BF)
        self.copy(k).start()
        return total

    def drain(self):
        for k in range(3):
            self.copy(k).wait_send()


def kernel(
    x_loc, c_loc, ag, ab, mg, mb, cosine, sine, wq_hbm, wo_hbm, wu_hbm, wd_hbm,
    out_x, out_n, out_q, out_o, out_u, out_d,
    xs, cs, st_in, st, wq, wqt, wo, wu, wd, ain, min_, ain_t, min_t,
    pa, pa_in, pkv, pkv_in, kvo, kvi, kvx,
    t_part, t_z, t_1, t_2m, t_2p, t_f,
    d_out, d_in, d_part, d_z, d_1, d_2m, d_2p, d_f,
    h_out, h_in, h_part, h_z, h_1, h_2m, h_2p, h_f,
    act, hid, hq, proj, pp, pp_in, ppo, ppi,
    abt, mbt, ngb, ngr, mom, momr, nrm, nrmr, m2, nrmd, ga, turned,
    w_sem, x_s, x_r, c_s, c_r, st_s, st_r, tt_s, tt_r,
    p_s, p_r, dp_s, dp_r, hp_s, hp_r, ts, tr, ds, dr, hs, hr, kv_s, kv_r, pp_s, pp_r,
    as_, ar, gs, gr, qs, qr, o_sem, u_sem, d_sem,
    ng_s, ng_r, mo_s, mo_r, nr_s, nr_r, m2_s, m2_r,
):
    place = Place()
    d, t, c, other, partner, remote = place.d, place.t, place.c, place.other, place.partner, place.remote

    def rows(index, size):
        return pl.ds(pl.multiple_of(index * size, size), size)

    def loop(low, high, f):
        def body(k, carry):
            f(k)
            return carry

        lax.fori_loop(low, high, body, 0)

    weights = [
        pltpu.make_async_copy(src, dst, w_sem.at[i])
        for i, (src, dst) in enumerate([(wd_hbm, wd), (wq_hbm, wq), (wo_hbm, wo), (wu_hbm, wu)])
    ]
    for copy in weights:
        copy.start()

    barrier = pltpu.get_barrier_semaphore()
    loop(
        1, NT,
        lambda k: pl.semaphore_signal(barrier, inc=1, device_id=(d, (t + k) % NT), device_id_type=MESH),
    )
    loop(
        1, ND,
        lambda k: pl.semaphore_signal(barrier, inc=1, device_id=((d + k) % ND, t), device_id_type=MESH),
    )
    pl.semaphore_wait(barrier, NT - 1 + ND - 1)

    own = rows(t, ROWS)

    def send_st(k):
        return remote(st_in.at[0], st_in.at[k], st_s.at[k], st_r.at[k], ((d + k) % ND, t))

    def send_tt(k):
        return remote(st.at[t], st.at[t], tt_s.at[k], tt_r.at[k], (d, (t + k) % NT))

    def wait_tt(k):
        p = (t + NT - k) % NT
        remote(st.at[p], st.at[p], tt_s.at[k], tt_r.at[k], (d, (t + k) % NT)).wait_recv()

    spread_c = Spread(place, cs, c_s, c_r)
    spread_x = Spread(place, xs, x_s, x_r)
    cs[own, :] = c_loc[...]
    spread_c.start()
    xs[own, :] = x_loc[...]
    spread_x.start()
    lane = lax.broadcasted_iota(jnp.int32, (128, 128), 1)

    def in_rows(one, two):
        return jnp.where(lane < 4, one, two).T[0:8]

    xf = x_loc[...].astype(F32)
    pad = jnp.zeros((ROWS, 1), F32)
    st_in[0] = in_rows(
        jnp.concatenate([jnp.sum(xf, 1, keepdims=True), pad], 0),
        jnp.concatenate([jnp.sum(xf * xf, 1, keepdims=True), pad], 0),
    )
    loop(1, ND, lambda k: send_st(k).start())
    spread_c.step_one()
    spread_x.step_one()
    loop(1, ND, lambda k: send_st(k).wait_recv())
    total = st_in[0]
    for k in range(1, ND):
        total = total + st_in[k]
    st[t] = total
    loop(1, NT, lambda k: send_tt(k).start())
    spread_c.step_two()
    spread_x.step_two()
    weights[1].wait()
    for i in range(QKV // 128):
        wqt[i * 128 : (i + 1) * 128, :] = wq[:, i * 128 : (i + 1) * 128].T
    spread_c.step_three()

    def produce(chunk, job, out, into, send, recv, hook):
        def pair(q, k):
            return remote(out.at[q], into.at[q], send.at[k], recv.at[k], partner)

        def body(i):
            @pl.when(i < 4)
            def _():
                j = (2 + 3 * i) % 4
                for plane in (1, 0):
                    q = place.chip(plane, j)
                    out[q] = chunk(2 * q + other).astype(BF)
                    pair(q, 2 * i + plane).start()
                for plane in (1, 0):
                    q = place.chip(plane, j)
                    job.part[q] = chunk(2 * q + c).astype(BF)

            @pl.when(i > 0)
            def _():
                j = (3 * i - 1) % 4
                for plane in (1, 0):
                    q = place.chip(plane, j)
                    pair(q, 2 * (i - 1) + plane).wait_recv()
                    job.part[q] = (job.part[q].astype(F32) + into[q].astype(F32)).astype(BF)
                    if plane == 1:
                        job.z_first(j).start()

            @pl.when(i == 1)
            def _():
                job.start()

            hook(i)

        loop(0, 5, body)

    def pair_drain(out, into, send, recv):
        loop(0, 8, lambda k: remote(out.at[k], into.at[k], send.at[k], recv.at[k], partner).wait_send())

    down = Reduce(place, d_part, d_z, d_1, d_2m, d_2p, d_f, ds, dr, (256, 144, 80, 192))
    up = Reduce(place, h_part, h_z, h_1, h_2m, h_2p, h_f, hs, hr, (512, 288, 160, 384))
    attn = Reduce(place, t_part, t_z, t_1, t_2m, t_2p, t_f, ts, tr, (128, 80, 48, 96))
    weights[0].wait()
    produce(
        lambda p: dot_nt(wd[rows(p, CH), :], cs[...]), down, d_out, d_in, dp_s, dp_r, lambda i: None
    )

    weights[2].wait()

    def og_body(i):
        og = dot_nt(wo[rows(i, 256), :], cs[...]).astype(BF)
        pa[pl.ds(i * 2, 2), :, 0:64, :] = og.reshape(2, 2, 64, TOK)

    loop(0, 4, og_body)

    spread_x.step_three()
    loop(1, NT, wait_tt)

    def scales(block):
        columns = jnp.concatenate([st[block]] * 16, 0).T
        average = columns[0:ROWS, 0:1] * (1.0 / D)
        spread = columns[0:ROWS, 4:5] * (1.0 / D) - average * average
        return average, lax.rsqrt(spread + 1e-05)

    def norm_body(block):
        here = rows(block, ROWS)
        average, inverse = scales(block)
        normed = (xs[here, :].astype(F32) - average) * inverse
        nrmd[here, :] = normed
        ain[here, :] = (normed * ag[...] + ab[...]).astype(BF)
        min_[here, :] = (normed * mg[...] + mb[...]).astype(BF)

    loop(0, NT, norm_body)

    def part_body(i):
        qq = dot_nt(wqt[rows(i, 256), :], ain[...]).astype(BF)
        pa[pl.ds(i * 2, 2), :, 64:128, :] = qq.reshape(2, 2, 64, TOK)

    pkv[...] = dot_nt(wqt[1024:1152, :], ain[...]).astype(BF).reshape(2, 64, TOK)
    give_kv = remote(pkv.at[other], pkv_in, p_s.at[0], p_r.at[0], partner)
    give_kv.start()
    loop(0, 4, part_body)
    give_a = remote(pa.at[:, other], pa_in, p_s.at[1], p_r.at[1], partner)
    give_a.start()

    down.step_two(1)
    down.step_two(0)
    down.z_merge()

    kv_sum = Doubling(place, kvo, kvi, kv_s, kv_r)
    give_kv.wait_recv()
    kv_sum.start((pkv[c].astype(F32) + pkv_in[...].astype(F32)).astype(BF))
    give_a.wait_recv()

    def sum_a(q):
        t_part[q] = (pa[q, c].astype(F32) + pa_in[q].astype(F32)).astype(BF)

    loop(0, 8, sum_a)
    for j in (2, 1, 0, 3):
        attn.z_first(j).start()
    attn.start()

    weights[3].wait()

    def hook(i):
        @pl.when(i == 2)
        def _():
            down.step_two(2)
            kv_sum.step(1)

        @pl.when(i == 3)
        def _():
            down.step_z()
            attn.step_two(1)
            attn.step_two(0)

    produce(lambda p: dot_nn(min_[...], wu[:, rows(p, CH)]), up, h_out, h_in, hp_s, hp_r, hook)

    attn.z_merge()
    kv_sum.step(2)
    up.step_two(1)
    up.step_two(0)
    attn.step_two(2)
    attn.step_z()
    ain_t[...] = ain[...].T
    min_t[...] = min_[...].T
    up.z_merge()
    up.step_two(2)
    up.step_z()

    attn.finish()
    og = attn.total(0, 64).astype(BF)
    q_sum = attn.total(64, 128)
    kv_total = kv_sum.step(3)

    co, si = cosine[...], sine[...]
    queries_f = rotate(q_sum, co, si)
    queries = queries_f.astype(BF)
    kvx[c] = jnp.where(c == 0, rotate(kv_total, co, si), kv_total).astype(BF)
    give = remote(kvx.at[c], kvx.at[c], p_s.at[2], p_r.at[2], partner)
    give.start()
    queries_t = queries_f.T.astype(BF)
    og_tf = og.astype(F32).T
    og_t = og_tf.astype(BF)
    give.wait_recv()
    keys = kvx[0]
    values = kvx[1]
    scaling = 1.0 / math.sqrt(HD)
    key_grad = jnp.zeros((HD, TOK), F32)
    value_grad = jnp.zeros((HD, TOK), F32)
    outs, qgs = [], []
    for n in range(4):
        low, high = n * 128, (n + 1) * 128
        scores = dot_nn(queries_t[low:high], keys) * scaling
        causal = lax.broadcasted_iota(jnp.int32, (128, TOK), 0) + low >= lax.broadcasted_iota(
            jnp.int32, (128, TOK), 1
        )
        raised = jnp.where(causal, jnp.exp(scores), 0.0)
        prob = raised / jnp.sum(raised, -1, keepdims=True)
        prob_low = prob.astype(BF)
        head = dot_nt(prob_low, values).astype(BF).astype(F32)
        dropped = dot_nn(og_t[low:high], values)
        row_dot = jnp.sum(og_tf[low:high] * head, -1, keepdims=True)
        score_grad = (prob * (dropped - row_dot) * scaling).astype(BF)
        qgs.append(dot_nt(keys, score_grad))
        key_grad = key_grad + dot_nn(queries[:, low:high], score_grad)
        value_grad = value_grad + dot_nn(og[:, low:high], prob_low)
        outs.append(head.T)
    hq[d, 0:64, :] = jnp.concatenate(outs, 1).astype(BF)
    hq[d, 64:128, :] = unrotate(jnp.concatenate(qgs, 1), co, si).astype(BF)
    pp[0] = unrotate(key_grad, co, si).astype(BF)
    pp[1] = value_grad.astype(BF)

    heads = Gather(place, hq, qs, qr, (128, 80, 64, 48))
    heads.start()
    give_pp = remote(pp.at[other], pp_in, p_s.at[3], p_r.at[3], partner)
    give_pp.start()

    give_pp.wait_recv()
    pp_sum = Doubling(place, ppo, ppi, pp_s, pp_r)
    pp_sum.start((pp[c].astype(F32) + pp_in[...].astype(F32)).astype(BF))
    down.finish()
    up.finish()

    for h in range(2):
        cols = slice(h * 128, (h + 1) * 128)
        hidden = up.total(0, 512, cols).T
        dact = down.total(h * 128, (h + 1) * 128)
        value, slope = gelu_parts(hidden)
        act[d, cols, :] = value.astype(BF)
        hid[d, cols, :] = (dact * slope).astype(BF)

    gather_act = Gather(place, act, as_, ar, (256, 144, 128, 80))
    gather_hid = Gather(place, hid, gs, gr, (256, 144, 128, 80))
    gather_act.start()
    gather_hid.start()
    mbt[...] = jnp.zeros((W, TOK), F32)

    def out_d_copy(p):
        return pltpu.make_async_copy(wd.at[rows(p, CH)], out_d.at[rows(p, CH)], d_sem.at[p])

    def out_u_copy(p):
        return pltpu.make_async_copy(wu.at[:, rows(p, CH)], out_u.at[:, rows(p, CH)], u_sem.at[p])

    def use_act(plane, j):
        def one(k):
            p = place.chip(plane, j) * 2 + (c + k) % 2
            wd[rows(p, CH), :] = dot_nn(act[p], cs[...]).astype(BF)
            out_d_copy(p).start()

        one(0)
        gather_act.take(plane, j)
        one(1)

    def use_hid(plane, j):
        def one(k):
            p = place.chip(plane, j) * 2 + (c + k) % 2
            mbt[...] += dot_nn(wu[:, rows(p, CH)], hid[p])
            wu[:, rows(p, CH)] = dot_nt(min_t[...], hid[p]).astype(BF)
            out_u_copy(p).start()

        one(0)
        gather_hid.take(plane, j)
        one(1)

    def near(f):
        loop(0, 3, lambda i: f((3 - i) // 3, i + i // 2))

    heads.step_one()
    use_act(0, 0)
    use_hid(0, 0)
    pp_sum.step(1)

    gather_act.step_one()
    heads.step_two()
    pp_sum.step(2)
    near(use_act)

    gather_hid.step_one()
    heads.step_three()
    heads.step_four()
    there = rows(16 + c, 64)
    proj[there, :] = pp_sum.step(3).astype(BF)
    give_pj = remote(proj.at[there], proj.at[there], p_s.at[4], p_r.at[4], partner)
    give_pj.start()
    for plane in range(2):
        for j in range(4):
            heads.take(plane, j)
    give_pj.wait_recv()

    def go_body(i):
        four = hq[pl.ds(i * 4, 4), 0:64, :].reshape(256, TOK)
        wo[rows(i, 256), :] = dot_nn(four, cs[...]).astype(BF)
        proj[rows(i, 256), :] = hq[pl.ds(i * 4, 4), 64:128, :].reshape(256, TOK)

    loop(0, 4, go_body)
    out_o_copy = pltpu.make_async_copy(wo, out_o, o_sem.at[0])
    out_o_copy.start()

    def ab_body(i):
        abt[rows(i, 128), :] = dot_nn(wq[rows(i, 128), :], proj[...])
        wq[rows(i, 128), :] = dot_nt(ain_t[rows(i, 128), :], proj[...]).astype(BF)

    loop(0, 4, ab_body)
    out_q_copy = pltpu.make_async_copy(wq, out_q, o_sem.at[1])
    out_q_copy.start()

    gather_act.step_two()
    near(use_hid)
    gather_hid.step_two()

    nrm[...] = jnp.zeros((8, W), F32)

    def early_body(n):
        here = rows(n, 128)
        a_back = abt[:, here].T
        ga[here, :] = a_back * ag[...]
        nrm[0:1, :] += jnp.sum(a_back * nrmd[here, :], 0, keepdims=True)
        nrm[1:2, :] += jnp.sum(a_back, 0, keepdims=True)

    loop(0, 4, early_body)

    gather_act.step_three()
    use_act(0, 2)
    use_hid(0, 2)
    gather_hid.step_three()
    loop(0, 2, lambda i: use_act(1, 2 * i + 1))
    gather_act.step_four()
    loop(0, 2, lambda i: use_hid(1, 2 * i + 1))
    gather_hid.step_four()
    use_act(1, 2)
    use_hid(1, 2)

    def send_ng(k):
        p = (t + k) % NT
        return remote(ngb.at[rows(p, ROWS)], ngr.at[k], ng_s.at[k], ng_r.at[k], (d, p))

    def send_mo(k):
        p = (t + k) % NT
        return remote(mom.at[p // 2], momr.at[k], mo_s.at[k], mo_r.at[k], (d, p))

    def send_nr(k):
        return remote(nrm, nrmr.at[k], nr_s.at[k], nr_r.at[k], (d, (t + k) % NT))

    def tail_body(i):
        n = (t // 2 + 1 + i) % 4
        here = rows(n, 128)
        m_back = mbt[:, here].T
        normed = nrmd[here, :]
        grad = ga[here, :] + m_back * mg[...]
        ngb[here, :] = grad.astype(BF)
        mom[n] = in_rows(jnp.sum(grad, 1, keepdims=True), jnp.sum(grad * normed, 1, keepdims=True))
        nrm[2:3, :] += jnp.sum(m_back * normed, 0, keepdims=True)
        nrm[3:4, :] += jnp.sum(m_back, 0, keepdims=True)

        def send(k):
            @pl.when(k > 0)
            def _():
                send_mo(k).start()
                send_ng(k).start()

        send((2 * n - t + NT) % NT)
        send((2 * n + 1 - t + NT) % NT)

    loop(0, 4, tail_body)

    loop(1, NT, lambda k: send_nr(k).start())
    loop(1, NT, lambda k: send_mo(k).wait_recv())
    acc = mom[t // 2]
    for k in range(1, NT):
        acc = acc + momr[k]
    m2[0] = acc

    def send_m2(k):
        return remote(m2.at[0], m2.at[k], m2_s.at[k], m2_r.at[k], ((d + k) % ND, t))

    loop(1, ND, lambda k: send_m2(k).start())
    loop(1, NT, lambda k: send_ng(k).wait_recv())
    loop(1, NT, lambda k: send_nr(k).wait_recv())
    norm_total = nrm[...]
    for k in range(1, NT):
        norm_total = norm_total + nrmr[k]
    out_n[...] = norm_total[0:4, :]
    grad = ngb[own, :].astype(F32)
    for k in range(1, NT):
        grad = grad + ngr[k].astype(F32)
    loop(1, ND, lambda k: send_m2(k).wait_recv())
    moments = m2[0]
    for k in range(1, ND):
        moments = moments + m2[k]
    turned[...] = jnp.concatenate([moments] * 16, 0).T
    mine = turned[rows(t % 2, ROWS), :]
    first = mine[:, 0:1] * (1.0 / D)
    second = mine[:, 4:5] * (1.0 / D)
    _, inverse = scales(t)
    out_x[...] = (
        c_loc[...].astype(F32) + inverse * (grad - first - nrmd[own, :] * second)
    ).astype(BF)

    def drain_t(k):
        send_tt(k).wait_send()
        send_mo(k).wait_send()
        send_ng(k).wait_send()
        send_nr(k).wait_send()

    def drain_d(k):
        send_st(k).wait_send()
        send_m2(k).wait_send()

    def drain_o(p):
        out_d_copy(p).wait()
        out_u_copy(p).wait()

    loop(1, NT, drain_t)
    loop(1, ND, drain_d)
    for copy in (give_a, give_kv, give, give_pp, give_pj):
        copy.wait_send()
    pair_drain(d_out, d_in, dp_s, dp_r)
    pair_drain(h_out, h_in, hp_s, hp_r)
    for job in (spread_c, spread_x, down, up, attn, kv_sum, pp_sum, heads, gather_act, gather_hid):
        job.drain()
    out_o_copy.wait()
    out_q_copy.wait()
    loop(0, ND, drain_o)


def on_device(
    block_input, cotangent, attn_gain, attn_bias, mlp_gain, mlp_bias, w_qkv, w_out, w_up, w_down
):
    cosine, sine = rope_columns()
    vmem = pl.BlockSpec(memory_space=pltpu.VMEM)
    hbm = pl.BlockSpec(memory_space=pl.ANY)
    dma = pltpu.SemaphoreType.DMA

    def buf(*shape):
        return pltpu.VMEM(shape, BF)

    def wide(*shape):
        return pltpu.VMEM(shape, F32)

    def sums(size, a, width):
        return [
            buf(8, size, width), buf(4, size - a, width), buf(2, size, width),
            buf(2, size, width), buf(2, size, width), buf(a, width),
        ]

    buffers = [
        buf(TOK, W), buf(TOK, W), wide(ND, 8, 128), wide(NT, 8, 128),
        buf(W, QKV), buf(QKV, W), buf(1024, W), buf(W, FF), buf(FF, W),
        buf(TOK, W), buf(TOK, W), buf(W, TOK), buf(W, TOK),
        buf(8, 2, 128, TOK), buf(8, 128, TOK), buf(2, 64, TOK), buf(64, TOK),
        buf(3, 64, TOK), buf(3, 64, TOK), buf(2, 64, TOK),
        *sums(128, 80, TOK),
        buf(8, CH, TOK), buf(8, CH, TOK), *sums(256, 144, TOK),
        buf(8, TOK, CH), buf(8, TOK, CH), *sums(512, 288, CH),
        buf(ND, CH, TOK), buf(ND, CH, TOK), buf(ND, 128, TOK), buf(QKV, TOK),
        buf(2, 64, TOK), buf(64, TOK), buf(3, 64, TOK), buf(3, 64, TOK),
        wide(W, TOK), wide(W, TOK), buf(TOK, W), buf(NT, ROWS, W),
        wide(4, 8, 128), wide(NT, 8, 128), wide(8, W), wide(NT, 8, W), wide(ND, 8, 128),
        wide(TOK, W), wide(TOK, W), wide(128, 128),
    ]
    counts = [4, 9, 9, 9, 9, 16, 16, 8, 8]
    counts += [5, 5, 8, 8, 8, 8] + [17] * 6 + [3] * 4
    counts += [20] * 6 + [2, 16, 16, 8, 8, 8, 8, 8, 8, 16, 16]
    semaphores = [dma((n,)) for n in counts]
    return pl.pallas_call(
        kernel,
        out_shape=(
            jax.ShapeDtypeStruct((ROWS, W), BF),
            jax.ShapeDtypeStruct((4, W), F32),
            jax.ShapeDtypeStruct((W, QKV), BF),
            jax.ShapeDtypeStruct((1024, W), BF),
            jax.ShapeDtypeStruct((W, FF), BF),
            jax.ShapeDtypeStruct((FF, W), BF),
        ),
        in_specs=[vmem] * 8 + [hbm] * 4,
        out_specs=(vmem, vmem, hbm, hbm, hbm, hbm),
        scratch_shapes=buffers + semaphores,
        compiler_params=pltpu.CompilerParams(
            collective_id=0, has_side_effects=True, vmem_limit_bytes=60 * 2**20
        ),
        cost_estimate=pl.CostEstimate(flops=14 * 10**9, bytes_accessed=21 * 10**6, transcendentals=10**6),
        name="block_backward",
    )(
        block_input, cotangent, attn_gain[None], attn_bias[None], mlp_gain[None], mlp_bias[None],
        cosine, sine, w_qkv, w_out, w_up, w_down,
    )


def solution(mesh):
    return jax.shard_map(
        on_device,
        mesh=mesh,
        in_specs=(
            P("tensor", "dp"),
            P("tensor", "dp"),
            P("dp"),
            P("dp"),
            P("dp"),
            P("dp"),
            P("dp", "tensor"),
            P("tensor", "dp"),
            P("dp", "tensor"),
            P("tensor", "dp"),
        ),
        out_specs=(
            P("tensor", "dp"),
            P(None, "dp"),
            P("dp", "tensor"),
            P("tensor", "dp"),
            P("dp", "tensor"),
            P("tensor", "dp"),
        ),
        check_vma=False,
    )
```

```python
import functools
import math

import jax
import jax.numpy as jnp
import numpy as np
from jax import lax
from jax.experimental import pallas as pl
from jax.experimental.pallas import tpu as pltpu
from jax.sharding import PartitionSpec as P

D = 8192
HD = 64
LENGTH = 512
TOK = 512
W = 512
ROWS = 64
NT = 8
ND = 16
FF = 4096
CH = 256
QKV = 1152
MESH = pl.DeviceIdType.MESH
BF = jnp.bfloat16
F32 = jnp.float32


def dot_nn(a, b):
    return jnp.dot(a, b, preferred_element_type=F32)


def dot_nt(a, b):
    return lax.dot_general(a, b, (((1,), (1,)), ((), ())), preferred_element_type=F32)


def gelu_parts(v):
    half = 0.5 * (1.0 + lax.erf(v * 0.7071067811865476))
    return v * half, half + v * jnp.exp(-0.5 * v * v) * 0.3989422804014327


def rope_columns():
    halfway = HD // 2
    position = (np.arange(TOK) % LENGTH).astype(np.float32)
    frequency = (10000.0 ** (-2.0 * np.arange(halfway) / HD)).astype(np.float32)
    angle = frequency[:, None] * position[None, :]
    cosine = np.concatenate([np.cos(angle), np.cos(angle)], 0).astype(np.float32)
    sine = np.concatenate([np.sin(angle), np.sin(angle)], 0).astype(np.float32)
    return jnp.asarray(cosine), jnp.asarray(sine)


def rotate(v, cosine, sine):
    turned = jnp.concatenate([-v[32:], v[:32]], 0)
    return v * cosine + turned * sine


def unrotate(v, cosine, sine):
    scaled = v * sine
    back = jnp.concatenate([scaled[32:], -scaled[:32]], 0)
    return v * cosine + back


class Reduce:
    def __init__(self, place, part, zin, in1, in2m, in2p, zfin, send, recv, split):
        self.place, self.part, self.zin, self.in1 = place, part, zin, in1
        self.in2m, self.in2p, self.zfin, self.send, self.recv = in2m, in2p, zfin, send, recv
        size, a, ma, mb = split
        self.a, self.size = a, size
        self.jobs = ((0, 0, ma, a), (1, 0, ma, a), (0, a, mb, size))

    def copy(self, src, dst, k, device):
        return self.place.remote(src, dst, self.send.at[k], self.recv.at[k], device)

    def block(self, plane, j):
        return self.part.at[self.place.chip(plane, j)]

    def z_first(self, j):
        src = self.block(1, j).at[self.a : self.size]
        return self.copy(src, self.zin.at[j], j, self.place.z_side)

    def one(self, job, way):
        plane, low, mid, high = self.jobs[job]
        here = slice(low, mid) if way == 0 else slice(mid, high)
        device = (self.place.x_up, self.place.x_down)[way]
        return self.copy(self.block(plane, 2).at[here], self.in1.at[plane, here], 4 + 2 * job + way, device)

    def two(self, job, way):
        plane, low, _, high = self.jobs[job]
        here = slice(low, high)
        device = (self.place.x_up, self.place.x_down)[way]
        land = (self.in2m, self.in2p)[way]
        return self.copy(self.block(plane, (1, 3)[way]).at[here], land.at[plane, here], 10 + 2 * job + way, device)

    def z_last(self):
        return self.copy(self.block(1, 0).at[0 : self.a], self.zfin, 16, self.place.z_side)

    def add(self, plane, j, here, more):
        target = self.block(plane, j)
        total = target[here].astype(F32)
        for term in more:
            total = total + term.astype(F32)
        target[here] = total.astype(BF)

    def start(self):
        for job in (1, 0):
            for way in (0, 1):
                self.one(job, way).start()

    def z_merge(self):
        for j in (2, 1, 0, 3):
            self.z_first(j).wait_recv()
            self.add(0, j, slice(self.a, self.size), [self.zin[j]])
            if j == 2:
                self.one(2, 0).start()
                self.one(2, 1).start()

    def step_two(self, job):
        plane, low, mid, high = self.jobs[job]
        for way, here in ((0, slice(low, mid)), (1, slice(mid, high))):
            self.one(job, way).wait_recv()
            self.add(plane, (1, 3)[way], here, [self.in1[plane, here]])
            self.two(job, way).start()

    def step_z(self):
        self.two(1, 0).wait_recv()
        self.two(1, 1).wait_recv()
        here = slice(0, self.a)
        self.add(1, 0, here, [self.in2m[1, here], self.in2p[1, here]])
        self.z_last().start()

    def finish(self):
        for job in (0, 2):
            self.two(job, 0).wait_recv()
            self.two(job, 1).wait_recv()
        self.z_last().wait_recv()

    def total(self, low, high, cols=slice(None)):
        out = self.block(0, 0)[low:high, cols].astype(F32)
        out = out + self.in2m[0, low:high, cols].astype(F32) + self.in2p[0, low:high, cols].astype(F32)
        top = min(high, self.a)
        if top <= low:
            return out
        upper = out[: top - low] + self.zfin[low:top, cols].astype(F32)
        return upper if top == high else jnp.concatenate([upper, out[top - low :]], 0)

    def drain(self):
        for j in range(4):
            self.z_first(j).wait_send()
        for job in range(3):
            for way in range(2):
                self.one(job, way).wait_send()
                self.two(job, way).wait_send()
        self.z_last().wait_send()


class Gather:
    def __init__(self, place, buf, send, recv, split):
        self.place, self.buf, self.send, self.recv = place, buf, send, recv
        size, a, mo, ma = split
        up, down, side = place.x_up, place.x_down, place.z_side
        own, left, right, far = (0, 0), (0, 3), (0, 1), (0, 2)
        z_own, z_left, z_right, z_far = (1, 0), (1, 3), (1, 1), (1, 2)
        self.moves = (
            (own, left, 0, size, up),
            (own, right, 0, size, down),
            (own, z_own, 0, size, side),
            (left, far, 0, mo, up),
            (right, far, mo, size, down),
            (left, z_left, a, size, side),
            (right, z_right, a, size, side),
            (far, z_far, a, size, side),
            (z_own, z_left, 0, a, up),
            (z_own, z_right, 0, a, down),
            (z_left, z_far, 0, ma, up),
            (z_right, z_far, ma, a, down),
        )

    def index(self, where):
        return self.place.chip(*where) * 2 + self.place.c

    def copy(self, index, low, high, k, device):
        at = self.buf.at[index, low:high]
        return self.place.remote(at, at, self.send.at[k], self.recv.at[k], device)

    def go(self, *moves):
        for k in moves:
            src, _, low, high, device = self.moves[k]
            self.copy(self.index(src), low, high, k, device).start()

    def wait(self, *moves):
        for k in moves:
            _, dst, low, high, device = self.moves[k]
            self.copy(self.index(dst), low, high, k, device).wait_recv()

    def hand(self, plane, j, core):
        index = self.place.chip(plane, j) * 2 + core
        k = 12 + j + 4 * plane
        at = self.buf.at[index]
        return self.place.remote(at, at, self.send.at[k], self.recv.at[k], self.place.partner)

    def give(self, *wheres):
        for plane, j in wheres:
            self.hand(plane, j, self.place.c).start()

    def take(self, plane, j):
        self.hand(plane, j, self.place.other).wait_recv()

    def start(self):
        self.go(0, 1, 2)
        self.give((0, 0))

    def step_one(self):
        self.wait(0)
        self.go(3, 5)
        self.wait(1)
        self.go(4, 6)
        self.wait(2)
        self.go(8, 9)
        self.give((0, 3), (0, 1), (1, 0))

    def step_two(self):
        self.wait(3, 4)
        self.go(7)
        self.wait(8)
        self.go(10)
        self.wait(9)
        self.go(11)
        self.give((0, 2))

    def step_three(self):
        self.wait(5, 6)
        self.give((1, 3), (1, 1))

    def step_four(self):
        self.wait(7, 10, 11)
        self.give((1, 2))

    def drain(self):
        for k, (src, _, low, high, device) in enumerate(self.moves):
            self.copy(self.index(src), low, high, k, device).wait_send()
        for plane in range(2):
            for j in range(4):
                self.hand(plane, j, self.place.c).wait_send()


class Spread:
    def __init__(self, place, buf, send, recv):
        self.place, self.buf, self.send, self.recv = place, buf, send, recv
        up, down, side = place.y_up, place.y_down, place.half_side
        own, left, right, far = (0, 0), (0, 3), (0, 1), (0, 2)
        h_own, h_left, h_right, h_far = (1, 0), (1, 3), (1, 1), (1, 2)
        mid = ROWS // 2
        self.moves = (
            (own, left, 0, ROWS, up),
            (own, right, 0, ROWS, down),
            (own, h_own, 0, ROWS, side),
            (left, far, 0, mid, up),
            (right, far, mid, ROWS, down),
            (h_own, h_left, 0, ROWS, up),
            (h_own, h_right, 0, ROWS, down),
            (h_left, h_far, 0, mid, up),
            (h_right, h_far, mid, ROWS, down),
        )

    def copy(self, where, low, high, k, device):
        first = pl.multiple_of(self.place.block(*where) * ROWS + low, 32)
        at = self.buf.at[pl.ds(first, high - low)]
        return self.place.remote(at, at, self.send.at[k], self.recv.at[k], device)

    def go(self, *moves):
        for k in moves:
            src, _, low, high, device = self.moves[k]
            self.copy(src, low, high, k, device).start()

    def wait(self, *moves):
        for k in moves:
            _, dst, low, high, device = self.moves[k]
            self.copy(dst, low, high, k, device).wait_recv()

    def start(self):
        self.go(2, 0, 1)

    def step_one(self):
        self.wait(2)
        self.go(5, 6)
        self.wait(0)
        self.go(3)
        self.wait(1)
        self.go(4)

    def step_two(self):
        self.wait(5)
        self.go(7)
        self.wait(6)
        self.go(8)

    def step_three(self):
        self.wait(3, 4, 7, 8)

    def drain(self):
        for k, (src, _, low, high, device) in enumerate(self.moves):
            self.copy(src, low, high, k, device).wait_send()


class Place:
    def __init__(self):
        self.d = d = lax.axis_index("dp")
        self.t = t = lax.axis_index("tensor")
        self.c = d % 2
        self.other = 1 - self.c
        self.x = x = (d // 2) % 4
        self.z = z = d // 8
        self.partner = (d + 1 - 2 * self.c, t)
        self.x_up = (z * 8 + ((x + 1) % 4) * 2 + self.c, t)
        self.x_down = (z * 8 + ((x + 3) % 4) * 2 + self.c, t)
        self.z_side = ((1 - z) * 8 + x * 2 + self.c, t)
        self.x_even = (z * 8 + (x + 1 - 2 * (x % 2)) * 2 + self.c, t)
        self.x_odd = (z * 8 + ((x + 3 + 2 * (x % 2)) % 4) * 2 + self.c, t)
        self.y = y = t // 2
        self.half = half = t % 2
        self.y_up = (d, ((y + 1) % 4) * 2 + half)
        self.y_down = (d, ((y + 3) % 4) * 2 + half)
        self.half_side = (d, y * 2 + 1 - half)

    def block(self, plane, j):
        return ((self.y + j) % 4) * 2 + (self.half + plane) % 2

    def chip(self, plane, j):
        return ((self.z + plane) % 2) * 4 + (self.x + j) % 4

    def remote(self, src, dst, send, recv, device):
        return pltpu.make_async_remote_copy(
            src_ref=src, dst_ref=dst, send_sem=send, recv_sem=recv, device_id=device, device_id_type=MESH
        )


class Doubling:
    def __init__(self, place, out, into, send, recv):
        self.place, self.out, self.into, self.send, self.recv = place, out, into, send, recv
        self.devices = (place.z_side, place.x_even, place.x_odd)

    def copy(self, k):
        return self.place.remote(
            self.out.at[k], self.into.at[k], self.send.at[k], self.recv.at[k], self.devices[k]
        )

    def start(self, value):
        self.out[0] = value
        self.copy(0).start()

    def step(self, k):
        self.copy(k - 1).wait_recv()
        total = self.out[k - 1].astype(F32) + self.into[k - 1].astype(F32)
        if k == 3:
            return total
        self.out[k] = total.astype(BF)
        self.copy(k).start()
        return total

    def drain(self):
        for k in range(3):
            self.copy(k).wait_send()


def kernel(
    x_loc, c_loc, ag, ab, mg, mb, cosine, sine, wq_hbm, wo_hbm, wu_hbm, wd_hbm,
    out_x, out_n, wq, wo, wu, wd,
    xs, cs, st_in, st, wqt, ain, min_, ain_t, min_t,
    pa, pa_in, pkv, pkv_in, kvo, kvi, kvx,
    t_part, t_z, t_1, t_2m, t_2p, t_f,
    d_out, d_in, d_part, d_z, d_1, d_2m, d_2p, d_f,
    h_out, h_in, h_part, h_z, h_1, h_2m, h_2p, h_f,
    act, hid, hq, proj, pp, pp_in, ppo, ppi,
    abt, mbt, ngb, ngr, mom, momr, nrm, nrmr, m2, nrmd, ga, turned,
    w_sem, x_s, x_r, c_s, c_r, st_s, st_r, tt_s, tt_r,
    p_s, p_r, dp_s, dp_r, hp_s, hp_r, ts, tr, ds, dr, hs, hr, kv_s, kv_r, pp_s, pp_r,
    as_, ar, gs, gr, qs, qr,
    ng_s, ng_r, mo_s, mo_r, nr_s, nr_r, m2_s, m2_r,
):
    place = Place()
    d, t, c, other, partner, remote = place.d, place.t, place.c, place.other, place.partner, place.remote

    def rows(index, size):
        return pl.ds(pl.multiple_of(index * size, size), size)

    def loop(low, high, f):
        def body(k, carry):
            f(k)
            return carry

        lax.fori_loop(low, high, body, 0)

    weights = [
        pltpu.make_async_copy(src, dst, w_sem.at[i])
        for i, (src, dst) in enumerate([(wd_hbm, wd), (wq_hbm, wq), (wo_hbm, wo), (wu_hbm, wu)])
    ]
    for copy in weights:
        copy.start()

    barrier = pltpu.get_barrier_semaphore()
    loop(
        1, NT,
        lambda k: pl.semaphore_signal(barrier, inc=1, device_id=(d, (t + k) % NT), device_id_type=MESH),
    )
    loop(
        1, ND,
        lambda k: pl.semaphore_signal(barrier, inc=1, device_id=((d + k) % ND, t), device_id_type=MESH),
    )

    own = rows(t, ROWS)
    cs[own, :] = c_loc[...]
    xs[own, :] = x_loc[...]
    lane = lax.broadcasted_iota(jnp.int32, (128, 128), 1)

    def in_rows(one, two):
        return jnp.where(lane < 4, one, two).T[0:8]

    xf = x_loc[...].astype(F32)
    pad = jnp.zeros((ROWS, 1), F32)
    st_in[0] = in_rows(
        jnp.concatenate([jnp.sum(xf, 1, keepdims=True), pad], 0),
        jnp.concatenate([jnp.sum(xf * xf, 1, keepdims=True), pad], 0),
    )
    pl.semaphore_wait(barrier, NT - 1 + ND - 1)

    def send_st(k):
        return remote(st_in.at[0], st_in.at[k], st_s.at[k], st_r.at[k], ((d + k) % ND, t))

    def send_tt(k):
        return remote(st.at[t], st.at[t], tt_s.at[k], tt_r.at[k], (d, (t + k) % NT))

    def wait_tt(k):
        p = (t + NT - k) % NT
        remote(st.at[p], st.at[p], tt_s.at[k], tt_r.at[k], (d, (t + k) % NT)).wait_recv()

    spread_c = Spread(place, cs, c_s, c_r)
    spread_x = Spread(place, xs, x_s, x_r)
    spread_c.start()
    spread_x.start()
    loop(1, ND, lambda k: send_st(k).start())
    weights[1].wait()
    for i in range(QKV // 128):
        wqt[i * 128 : (i + 1) * 128, :] = wq[:, i * 128 : (i + 1) * 128].T
    spread_c.step_one()
    spread_x.step_one()
    loop(1, ND, lambda k: send_st(k).wait_recv())
    total = st_in[0]
    for k in range(1, ND):
        total = total + st_in[k]
    st[t] = total
    loop(1, NT, lambda k: send_tt(k).start())
    spread_c.step_two()
    spread_x.step_two()
    spread_c.step_three()

    def produce(chunk, job, out, into, send, recv, hook):
        def pair(q, k):
            return remote(out.at[q], into.at[q], send.at[k], recv.at[k], partner)

        def body(i):
            @pl.when(i < 4)
            def _():
                j = (2 + 3 * i) % 4
                for plane in (1, 0):
                    q = place.chip(plane, j)
                    out[q] = chunk(2 * q + other).astype(BF)
                    pair(q, 2 * i + plane).start()
                for plane in (1, 0):
                    q = place.chip(plane, j)
                    job.part[q] = chunk(2 * q + c).astype(BF)

            @pl.when(i > 0)
            def _():
                j = (3 * i - 1) % 4
                for plane in (1, 0):
                    q = place.chip(plane, j)
                    pair(q, 2 * (i - 1) + plane).wait_recv()
                    job.part[q] = (job.part[q].astype(F32) + into[q].astype(F32)).astype(BF)
                    if plane == 1:
                        job.z_first(j).start()

            @pl.when(i == 1)
            def _():
                job.start()

            hook(i)

        loop(0, 5, body)

    def pair_drain(out, into, send, recv):
        loop(0, 8, lambda k: remote(out.at[k], into.at[k], send.at[k], recv.at[k], partner).wait_send())

    down = Reduce(place, d_part, d_z, d_1, d_2m, d_2p, d_f, ds, dr, (256, 144, 80, 192))
    up = Reduce(place, h_part, h_z, h_1, h_2m, h_2p, h_f, hs, hr, (512, 288, 160, 384))
    attn = Reduce(place, t_part, t_z, t_1, t_2m, t_2p, t_f, ts, tr, (128, 80, 48, 96))
    weights[0].wait()
    produce(
        lambda p: dot_nt(wd[rows(p, CH), :], cs[...]), down, d_out, d_in, dp_s, dp_r, lambda i: None
    )

    weights[2].wait()

    def og_body(i):
        og = dot_nt(wo[rows(i, 256), :], cs[...]).astype(BF)
        pa[pl.ds(i * 2, 2), :, 0:64, :] = og.reshape(2, 2, 64, TOK)

    loop(0, 4, og_body)

    spread_x.step_three()
    loop(1, NT, wait_tt)

    def scales(block):
        columns = jnp.concatenate([st[block]] * 16, 0).T
        average = columns[0:ROWS, 0:1] * (1.0 / D)
        spread = columns[0:ROWS, 4:5] * (1.0 / D) - average * average
        return average, lax.rsqrt(spread + 1e-05)

    def norm_body(block):
        here = rows(block, ROWS)
        average, inverse = scales(block)
        normed = (xs[here, :].astype(F32) - average) * inverse
        nrmd[here, :] = normed
        ain[here, :] = (normed * ag[...] + ab[...]).astype(BF)
        min_[here, :] = (normed * mg[...] + mb[...]).astype(BF)

    loop(0, NT, norm_body)

    def part_body(i):
        qq = dot_nt(wqt[rows(i, 256), :], ain[...]).astype(BF)
        pa[pl.ds(i * 2, 2), :, 64:128, :] = qq.reshape(2, 2, 64, TOK)

    pkv[...] = dot_nt(wqt[1024:1152, :], ain[...]).astype(BF).reshape(2, 64, TOK)
    give_kv = remote(pkv.at[other], pkv_in, p_s.at[0], p_r.at[0], partner)
    give_kv.start()
    loop(0, 4, part_body)
    give_a = remote(pa.at[:, other], pa_in, p_s.at[1], p_r.at[1], partner)
    give_a.start()

    down.step_two(1)
    down.step_two(0)
    down.z_merge()

    kv_sum = Doubling(place, kvo, kvi, kv_s, kv_r)
    give_kv.wait_recv()
    kv_sum.start((pkv[c].astype(F32) + pkv_in[...].astype(F32)).astype(BF))
    give_a.wait_recv()

    def sum_a(q):
        t_part[q] = (pa[q, c].astype(F32) + pa_in[q].astype(F32)).astype(BF)

    loop(0, 8, sum_a)
    for j in (2, 1, 0, 3):
        attn.z_first(j).start()
    attn.start()

    weights[3].wait()

    def hook(i):
        @pl.when(i == 2)
        def _():
            down.step_two(2)
            kv_sum.step(1)

        @pl.when(i == 3)
        def _():
            down.step_z()
            attn.step_two(1)
            attn.step_two(0)

    produce(lambda p: dot_nn(min_[...], wu[:, rows(p, CH)]), up, h_out, h_in, hp_s, hp_r, hook)

    attn.z_merge()
    kv_sum.step(2)
    up.step_two(1)
    up.step_two(0)

    attn.step_two(2)
    attn.step_z()
    ain_t[...] = ain[...].T
    min_t[...] = min_[...].T

    up.z_merge()

    up.step_two(2)
    up.step_z()

    attn.finish()
    og = attn.total(0, 64).astype(BF)
    q_sum = attn.total(64, 128)
    kv_total = kv_sum.step(3)

    co, si = cosine[...], sine[...]
    queries_f = rotate(q_sum, co, si)
    queries = queries_f.astype(BF)
    kvx[c] = jnp.where(c == 0, rotate(kv_total, co, si), kv_total).astype(BF)
    give = remote(kvx.at[c], kvx.at[c], p_s.at[2], p_r.at[2], partner)
    give.start()
    queries_t = queries_f.T.astype(BF)
    og_tf = og.astype(F32).T
    og_t = og_tf.astype(BF)
    give.wait_recv()
    keys = kvx[0]
    values = kvx[1]
    scaling = 1.0 / math.sqrt(HD)
    key_grad = jnp.zeros((HD, TOK), F32)
    value_grad = jnp.zeros((HD, TOK), F32)
    outs, qgs = [], []
    for n in range(4):
        low, high = n * 128, (n + 1) * 128
        scores = dot_nn(queries_t[low:high], keys) * scaling
        causal = lax.broadcasted_iota(jnp.int32, (128, TOK), 0) + low >= lax.broadcasted_iota(
            jnp.int32, (128, TOK), 1
        )
        raised = jnp.where(causal, jnp.exp(scores), 0.0)
        prob = raised / jnp.sum(raised, -1, keepdims=True)
        prob_low = prob.astype(BF)
        head = dot_nt(prob_low, values).astype(BF).astype(F32)
        dropped = dot_nn(og_t[low:high], values)
        row_dot = jnp.sum(og_tf[low:high] * head, -1, keepdims=True)
        score_grad = (prob * (dropped - row_dot) * scaling).astype(BF)
        qgs.append(dot_nt(keys, score_grad))
        key_grad = key_grad + dot_nn(queries[:, low:high], score_grad)
        value_grad = value_grad + dot_nn(og[:, low:high], prob_low)
        outs.append(head.T)
    hq[d, 0:64, :] = jnp.concatenate(outs, 1).astype(BF)
    hq[d, 64:128, :] = unrotate(jnp.concatenate(qgs, 1), co, si).astype(BF)
    pp[0] = unrotate(key_grad, co, si).astype(BF)
    pp[1] = value_grad.astype(BF)

    heads = Gather(place, hq, qs, qr, (128, 80, 64, 48))
    heads.start()
    give_pp = remote(pp.at[other], pp_in, p_s.at[3], p_r.at[3], partner)
    give_pp.start()

    give_pp.wait_recv()
    pp_sum = Doubling(place, ppo, ppi, pp_s, pp_r)
    pp_sum.start((pp[c].astype(F32) + pp_in[...].astype(F32)).astype(BF))
    down.finish()
    up.finish()

    for h in range(2):
        cols = slice(h * 128, (h + 1) * 128)
        hidden = up.total(0, 512, cols).T
        dact = down.total(h * 128, (h + 1) * 128)
        value, slope = gelu_parts(hidden)
        act[d, cols, :] = value.astype(BF)
        hid[d, cols, :] = (dact * slope).astype(BF)

    gather_act = Gather(place, act, as_, ar, (256, 144, 128, 80))
    gather_hid = Gather(place, hid, gs, gr, (256, 144, 128, 80))
    gather_act.start()
    gather_hid.start()
    mbt[...] = jnp.zeros((W, TOK), F32)

    def use_act(plane, j):
        def one(k):
            p = place.chip(plane, j) * 2 + (c + k) % 2
            wd[rows(p, CH), :] = dot_nn(act[p], cs[...]).astype(BF)

        one(0)
        gather_act.take(plane, j)
        one(1)

    def use_hid(plane, j):
        def one(k):
            p = place.chip(plane, j) * 2 + (c + k) % 2
            mbt[...] += dot_nn(wu[:, rows(p, CH)], hid[p])
            wu[:, rows(p, CH)] = dot_nt(min_t[...], hid[p]).astype(BF)

        one(0)
        gather_hid.take(plane, j)
        one(1)

    def near(f):
        loop(0, 3, lambda i: f((3 - i) // 3, i + i // 2))

    heads.step_one()
    use_act(0, 0)
    use_hid(0, 0)
    pp_sum.step(1)
    heads.step_two()
    pp_sum.step(2)

    gather_act.step_one()
    gather_hid.step_one()

    near(use_act)
    near(use_hid)

    heads.step_three()
    heads.step_four()
    there = rows(16 + c, 64)
    proj[there, :] = pp_sum.step(3).astype(BF)
    give_pj = remote(proj.at[there], proj.at[there], p_s.at[4], p_r.at[4], partner)
    give_pj.start()
    for plane in range(2):
        for j in range(4):
            heads.take(plane, j)
    give_pj.wait_recv()

    def go_body(i):
        four = hq[pl.ds(i * 4, 4), 0:64, :].reshape(256, TOK)
        wo[rows(i, 256), :] = dot_nn(four, cs[...]).astype(BF)
        proj[rows(i, 256), :] = hq[pl.ds(i * 4, 4), 64:128, :].reshape(256, TOK)

    loop(0, 4, go_body)

    def ab_body(i):
        abt[rows(i, 128), :] = dot_nn(wq[rows(i, 128), :], proj[...])
        wq[rows(i, 128), :] = dot_nt(ain_t[rows(i, 128), :], proj[...]).astype(BF)

    loop(0, 4, ab_body)

    gather_act.step_two()
    gather_hid.step_two()

    nrm[...] = jnp.zeros((8, W), F32)

    def early_body(n):
        here = rows(n, 128)
        a_back = abt[:, here].T
        ga[here, :] = a_back * ag[...]
        nrm[0:1, :] += jnp.sum(a_back * nrmd[here, :], 0, keepdims=True)
        nrm[1:2, :] += jnp.sum(a_back, 0, keepdims=True)

    loop(0, 4, early_body)

    use_act(0, 2)
    use_hid(0, 2)
    gather_act.step_three()
    gather_hid.step_three()
    loop(0, 2, lambda i: use_act(1, 2 * i + 1))
    loop(0, 2, lambda i: use_hid(1, 2 * i + 1))
    gather_act.step_four()
    gather_hid.step_four()
    use_act(1, 2)
    use_hid(1, 2)

    def send_ng(k):
        p = (t + k) % NT
        return remote(ngb.at[rows(p, ROWS)], ngr.at[k], ng_s.at[k], ng_r.at[k], (d, p))

    def send_mo(k):
        p = (t + k) % NT
        return remote(mom.at[p // 2], momr.at[k], mo_s.at[k], mo_r.at[k], (d, p))

    def send_nr(k):
        return remote(nrm, nrmr.at[k], nr_s.at[k], nr_r.at[k], (d, (t + k) % NT))

    def tail_body(i):
        n = (t // 2 + 1 + i) % 4
        here = rows(n, 128)
        m_back = mbt[:, here].T
        normed = nrmd[here, :]
        grad = ga[here, :] + m_back * mg[...]
        ngb[here, :] = grad.astype(BF)
        mom[n] = in_rows(jnp.sum(grad, 1, keepdims=True), jnp.sum(grad * normed, 1, keepdims=True))
        nrm[2:3, :] += jnp.sum(m_back * normed, 0, keepdims=True)
        nrm[3:4, :] += jnp.sum(m_back, 0, keepdims=True)

        def send(k):
            @pl.when(k > 0)
            def _():
                send_mo(k).start()
                send_ng(k).start()

        send((2 * n - t + NT) % NT)
        send((2 * n + 1 - t + NT) % NT)

    loop(0, 4, tail_body)

    loop(1, NT, lambda k: send_nr(k).start())
    loop(1, NT, lambda k: send_mo(k).wait_recv())
    acc = mom[t // 2]
    for k in range(1, NT):
        acc = acc + momr[k]
    m2[0] = acc

    def send_m2(k):
        return remote(m2.at[0], m2.at[k], m2_s.at[k], m2_r.at[k], ((d + k) % ND, t))

    loop(1, ND, lambda k: send_m2(k).start())
    loop(1, NT, lambda k: send_ng(k).wait_recv())
    loop(1, NT, lambda k: send_nr(k).wait_recv())
    norm_total = nrm[...]
    for k in range(1, NT):
        norm_total = norm_total + nrmr[k]
    out_n[...] = norm_total[0:4, :]
    grad = ngb[own, :].astype(F32)
    for k in range(1, NT):
        grad = grad + ngr[k].astype(F32)
    loop(1, ND, lambda k: send_m2(k).wait_recv())
    moments = m2[0]
    for k in range(1, ND):
        moments = moments + m2[k]
    turned[...] = jnp.concatenate([moments] * 16, 0).T
    mine = turned[rows(t % 2, ROWS), :]
    first = mine[:, 0:1] * (1.0 / D)
    second = mine[:, 4:5] * (1.0 / D)
    _, inverse = scales(t)
    out_x[...] = (
        c_loc[...].astype(F32) + inverse * (grad - first - nrmd[own, :] * second)
    ).astype(BF)

    def drain_t(k):
        send_tt(k).wait_send()
        send_mo(k).wait_send()
        send_ng(k).wait_send()
        send_nr(k).wait_send()

    def drain_d(k):
        send_st(k).wait_send()
        send_m2(k).wait_send()

    loop(1, NT, drain_t)
    loop(1, ND, drain_d)
    for copy in (give_a, give_kv, give, give_pp, give_pj):
        copy.wait_send()
    pair_drain(d_out, d_in, dp_s, dp_r)
    pair_drain(h_out, h_in, hp_s, hp_r)
    for job in (spread_c, spread_x, down, up, attn, kv_sum, pp_sum, heads, gather_act, gather_hid):
        job.drain()


def write_out(*refs):
    copies = [pltpu.make_async_copy(refs[i], refs[6 + i], refs[12].at[i]) for i in range(6)]
    for copy in copies:
        copy.start()
    for copy in copies:
        copy.wait()


def on_device(
    block_input, cotangent, attn_gain, attn_bias, mlp_gain, mlp_bias, w_qkv, w_out, w_up, w_down
):
    cosine, sine = rope_columns()
    vmem = pl.BlockSpec(memory_space=pltpu.VMEM)
    hbm = pl.BlockSpec(memory_space=pl.ANY)
    dma = pltpu.SemaphoreType.DMA

    def buf(*shape):
        return pltpu.VMEM(shape, BF)

    def wide(*shape):
        return pltpu.VMEM(shape, F32)

    def sums(size, a, width):
        return [
            buf(8, size, width), buf(4, size - a, width), buf(2, size, width),
            buf(2, size, width), buf(2, size, width), buf(a, width),
        ]

    buffers = [
        buf(TOK, W), buf(TOK, W), wide(ND, 8, 128), wide(NT, 8, 128),
        buf(QKV, W),
        buf(TOK, W), buf(TOK, W), buf(W, TOK), buf(W, TOK),
        buf(8, 2, 128, TOK), buf(8, 128, TOK), buf(2, 64, TOK), buf(64, TOK),
        buf(3, 64, TOK), buf(3, 64, TOK), buf(2, 64, TOK),
        *sums(128, 80, TOK),
        buf(8, CH, TOK), buf(8, CH, TOK), *sums(256, 144, TOK),
        buf(8, TOK, CH), buf(8, TOK, CH), *sums(512, 288, CH),
        buf(ND, CH, TOK), buf(ND, CH, TOK), buf(ND, 128, TOK), buf(QKV, TOK),
        buf(2, 64, TOK), buf(64, TOK), buf(3, 64, TOK), buf(3, 64, TOK),
        wide(W, TOK), wide(W, TOK), buf(TOK, W), buf(NT, ROWS, W),
        wide(4, 8, 128), wide(NT, 8, 128), wide(8, W), wide(NT, 8, W), wide(ND, 8, 128),
        wide(TOK, W), wide(TOK, W), wide(128, 128),
    ]
    counts = [4, 9, 9, 9, 9, 16, 16, 8, 8]
    counts += [5, 5, 8, 8, 8, 8] + [17] * 6 + [3] * 4
    counts += [20] * 6 + [8, 8, 8, 8, 8, 8, 16, 16]
    semaphores = [dma((n,)) for n in counts]
    results = pl.pallas_call(
        kernel,
        out_shape=(
            pltpu.VMEM((ROWS, W), BF),
            pltpu.VMEM((4, W), F32),
            pltpu.VMEM((W, QKV), BF),
            pltpu.VMEM((1024, W), BF),
            pltpu.VMEM((W, FF), BF),
            pltpu.VMEM((FF, W), BF),
        ),
        in_specs=[vmem] * 8 + [hbm] * 4,
        out_specs=(vmem,) * 6,
        scratch_shapes=buffers + semaphores,
        compiler_params=pltpu.CompilerParams(
            collective_id=0, has_side_effects=True, vmem_limit_bytes=46 * 2**20
        ),
        cost_estimate=pl.CostEstimate(flops=14 * 10**9, bytes_accessed=21 * 10**6, transcendentals=10**6),
        name="block_backward",
    )(
        block_input, cotangent, attn_gain[None], attn_bias[None], mlp_gain[None], mlp_bias[None],
        cosine, sine, w_qkv, w_out, w_up, w_down,
    )
    return pl.pallas_call(
        write_out,
        out_shape=tuple(jax.ShapeDtypeStruct(r.shape, r.dtype) for r in results),
        in_specs=[vmem] * 6,
        out_specs=(hbm,) * 6,
        scratch_shapes=[dma((6,))],
        compiler_params=pltpu.CompilerParams(vmem_limit_bytes=4 * 2**20),
        name="write_results",
    )(*[pltpu.with_memory_space_constraint(r, pltpu.VMEM) for r in results])


def solution(mesh):
    return jax.shard_map(
        on_device,
        mesh=mesh,
        in_specs=(
            P("tensor", "dp"),
            P("tensor", "dp"),
            P("dp"),
            P("dp"),
            P("dp"),
            P("dp"),
            P("dp", "tensor"),
            P("tensor", "dp"),
            P("dp", "tensor"),
            P("tensor", "dp"),
        ),
        out_specs=(
            P("tensor", "dp"),
            P(None, "dp"),
            P("dp", "tensor"),
            P("tensor", "dp"),
            P("dp", "tensor"),
            P("tensor", "dp"),
        ),
        check_vma=False,
    )
```

```python
import functools
import math

import jax
import jax.numpy as jnp
import numpy as np
from jax import lax
from jax.experimental import pallas as pl
from jax.experimental.pallas import tpu as pltpu
from jax.sharding import PartitionSpec as P

D = 8192
HD = 64
LENGTH = 512
TOK = 512
W = 512
ROWS = 64
NT = 8
ND = 16
FF = 4096
CH = 256
QKV = 1152
MESH = pl.DeviceIdType.MESH
BF = jnp.bfloat16
F32 = jnp.float32


def dot_nn(a, b):
    return jnp.dot(a, b, preferred_element_type=F32)


def dot_nt(a, b):
    return lax.dot_general(a, b, (((1,), (1,)), ((), ())), preferred_element_type=F32)


def gelu_parts(v):
    half = 0.5 * (1.0 + lax.erf(v * 0.7071067811865476))
    return v * half, half + v * jnp.exp(-0.5 * v * v) * 0.3989422804014327


def rope_columns():
    halfway = HD // 2
    position = (np.arange(TOK) % LENGTH).astype(np.float32)
    frequency = (10000.0 ** (-2.0 * np.arange(halfway) / HD)).astype(np.float32)
    angle = frequency[:, None] * position[None, :]
    cosine = np.concatenate([np.cos(angle), np.cos(angle)], 0).astype(np.float32)
    sine = np.concatenate([np.sin(angle), np.sin(angle)], 0).astype(np.float32)
    return jnp.asarray(cosine), jnp.asarray(sine)


def rotate(v, cosine, sine):
    turned = jnp.concatenate([-v[32:], v[:32]], 0)
    return v * cosine + turned * sine


def unrotate(v, cosine, sine):
    scaled = v * sine
    back = jnp.concatenate([scaled[32:], -scaled[:32]], 0)
    return v * cosine + back


class Reduce:
    def __init__(self, place, part, zin, in1, in2m, in2p, zfin, send, recv, split):
        self.place, self.part, self.zin, self.in1 = place, part, zin, in1
        self.in2m, self.in2p, self.zfin, self.send, self.recv = in2m, in2p, zfin, send, recv
        size, a, ma, mb = split
        self.a, self.size = a, size
        self.jobs = ((0, 0, ma, a), (1, 0, ma, a), (0, a, mb, size))

    def copy(self, src, dst, k, device):
        return self.place.remote(src, dst, self.send.at[k], self.recv.at[k], device)

    def block(self, plane, j):
        return self.part.at[self.place.chip(plane, j)]

    def z_first(self, j):
        src = self.block(1, j).at[self.a : self.size]
        return self.copy(src, self.zin.at[j], j, self.place.z_side)

    def one(self, job, way):
        plane, low, mid, high = self.jobs[job]
        here = slice(low, mid) if way == 0 else slice(mid, high)
        device = (self.place.x_up, self.place.x_down)[way]
        return self.copy(self.block(plane, 2).at[here], self.in1.at[plane, here], 4 + 2 * job + way, device)

    def two(self, job, way):
        plane, low, _, high = self.jobs[job]
        here = slice(low, high)
        device = (self.place.x_up, self.place.x_down)[way]
        land = (self.in2m, self.in2p)[way]
        return self.copy(self.block(plane, (1, 3)[way]).at[here], land.at[plane, here], 10 + 2 * job + way, device)

    def z_last(self):
        return self.copy(self.block(1, 0).at[0 : self.a], self.zfin, 16, self.place.z_side)

    def add(self, plane, j, here, more):
        target = self.block(plane, j)
        total = target[here].astype(F32)
        for term in more:
            total = total + term.astype(F32)
        target[here] = total.astype(BF)

    def start(self):
        for job in (1, 0):
            for way in (0, 1):
                self.one(job, way).start()

    def z_merge(self):
        for j in (2, 1, 0, 3):
            self.z_first(j).wait_recv()
            self.add(0, j, slice(self.a, self.size), [self.zin[j]])
            if j == 2:
                self.one(2, 0).start()
                self.one(2, 1).start()

    def step_two(self, job):
        plane, low, mid, high = self.jobs[job]
        for way, here in ((0, slice(low, mid)), (1, slice(mid, high))):
            self.one(job, way).wait_recv()
            self.add(plane, (1, 3)[way], here, [self.in1[plane, here]])
            self.two(job, way).start()

    def step_z(self):
        self.two(1, 0).wait_recv()
        self.two(1, 1).wait_recv()
        here = slice(0, self.a)
        self.add(1, 0, here, [self.in2m[1, here], self.in2p[1, here]])
        self.z_last().start()

    def finish(self):
        for job in (0, 2):
            self.two(job, 0).wait_recv()
            self.two(job, 1).wait_recv()
        self.z_last().wait_recv()

    def total(self, low, high, cols=slice(None)):
        out = self.block(0, 0)[low:high, cols].astype(F32)
        out = out + self.in2m[0, low:high, cols].astype(F32) + self.in2p[0, low:high, cols].astype(F32)
        top = min(high, self.a)
        if top <= low:
            return out
        upper = out[: top - low] + self.zfin[low:top, cols].astype(F32)
        return upper if top == high else jnp.concatenate([upper, out[top - low :]], 0)

    def drain(self):
        for j in range(4):
            self.z_first(j).wait_send()
        for job in range(3):
            for way in range(2):
                self.one(job, way).wait_send()
                self.two(job, way).wait_send()
        self.z_last().wait_send()


class Gather:
    def __init__(self, place, buf, send, recv, split):
        self.place, self.buf, self.send, self.recv = place, buf, send, recv
        size, a, mo, ma = split
        up, down, side = place.x_up, place.x_down, place.z_side
        own, left, right, far = (0, 0), (0, 3), (0, 1), (0, 2)
        z_own, z_left, z_right, z_far = (1, 0), (1, 3), (1, 1), (1, 2)
        self.moves = (
            (own, left, 0, size, up),
            (own, right, 0, size, down),
            (own, z_own, 0, size, side),
            (left, far, 0, mo, up),
            (right, far, mo, size, down),
            (left, z_left, a, size, side),
            (right, z_right, a, size, side),
            (far, z_far, a, size, side),
            (z_own, z_left, 0, a, up),
            (z_own, z_right, 0, a, down),
            (z_left, z_far, 0, ma, up),
            (z_right, z_far, ma, a, down),
        )

    def index(self, where):
        return self.place.chip(*where) * 2 + self.place.c

    def copy(self, index, low, high, k, device):
        at = self.buf.at[index, low:high]
        return self.place.remote(at, at, self.send.at[k], self.recv.at[k], device)

    def go(self, *moves):
        for k in moves:
            src, _, low, high, device = self.moves[k]
            self.copy(self.index(src), low, high, k, device).start()

    def wait(self, *moves):
        for k in moves:
            _, dst, low, high, device = self.moves[k]
            self.copy(self.index(dst), low, high, k, device).wait_recv()

    def hand(self, plane, j, core):
        index = self.place.chip(plane, j) * 2 + core
        k = 12 + j + 4 * plane
        at = self.buf.at[index]
        return self.place.remote(at, at, self.send.at[k], self.recv.at[k], self.place.partner)

    def give(self, *wheres):
        for plane, j in wheres:
            self.hand(plane, j, self.place.c).start()

    def take(self, plane, j):
        self.hand(plane, j, self.place.other).wait_recv()

    def start(self):
        self.go(0, 1, 2)
        self.give((0, 0))

    def step_one(self):
        self.wait(0)
        self.go(3, 5)
        self.wait(1)
        self.go(4, 6)
        self.wait(2)
        self.go(8, 9)
        self.give((0, 3), (0, 1), (1, 0))

    def step_two(self):
        self.wait(3, 4)
        self.go(7)
        self.wait(8)
        self.go(10)
        self.wait(9)
        self.go(11)
        self.give((0, 2))

    def step_three(self):
        self.wait(5, 6)
        self.give((1, 3), (1, 1))

    def step_four(self):
        self.wait(7, 10, 11)
        self.give((1, 2))

    def drain(self):
        for k, (src, _, low, high, device) in enumerate(self.moves):
            self.copy(self.index(src), low, high, k, device).wait_send()
        for plane in range(2):
            for j in range(4):
                self.hand(plane, j, self.place.c).wait_send()


class Spread:
    def __init__(self, place, buf, send, recv):
        self.place, self.buf, self.send, self.recv = place, buf, send, recv
        up, down, side = place.y_up, place.y_down, place.half_side
        own, left, right, far = (0, 0), (0, 3), (0, 1), (0, 2)
        h_own, h_left, h_right, h_far = (1, 0), (1, 3), (1, 1), (1, 2)
        mid = ROWS // 2
        self.moves = (
            (own, left, 0, ROWS, up),
            (own, right, 0, ROWS, down),
            (own, h_own, 0, ROWS, side),
            (left, far, 0, mid, up),
            (right, far, mid, ROWS, down),
            (h_own, h_left, 0, ROWS, up),
            (h_own, h_right, 0, ROWS, down),
            (h_left, h_far, 0, mid, up),
            (h_right, h_far, mid, ROWS, down),
        )

    def copy(self, where, low, high, k, device):
        first = pl.multiple_of(self.place.block(*where) * ROWS + low, 32)
        at = self.buf.at[pl.ds(first, high - low)]
        return self.place.remote(at, at, self.send.at[k], self.recv.at[k], device)

    def go(self, *moves):
        for k in moves:
            src, _, low, high, device = self.moves[k]
            self.copy(src, low, high, k, device).start()

    def wait(self, *moves):
        for k in moves:
            _, dst, low, high, device = self.moves[k]
            self.copy(dst, low, high, k, device).wait_recv()

    def start(self):
        self.go(2, 0, 1)

    def step_one(self):
        self.wait(2)
        self.go(5, 6)
        self.wait(0)
        self.go(3)
        self.wait(1)
        self.go(4)

    def step_two(self):
        self.wait(5)
        self.go(7)
        self.wait(6)
        self.go(8)

    def step_three(self):
        self.wait(3, 4, 7, 8)

    def drain(self):
        for k, (src, _, low, high, device) in enumerate(self.moves):
            self.copy(src, low, high, k, device).wait_send()


class Place:
    def __init__(self):
        self.d = d = lax.axis_index("dp")
        self.t = t = lax.axis_index("tensor")
        self.c = d % 2
        self.other = 1 - self.c
        self.x = x = (d // 2) % 4
        self.z = z = d // 8
        self.partner = (d + 1 - 2 * self.c, t)
        self.x_up = (z * 8 + ((x + 1) % 4) * 2 + self.c, t)
        self.x_down = (z * 8 + ((x + 3) % 4) * 2 + self.c, t)
        self.z_side = ((1 - z) * 8 + x * 2 + self.c, t)
        self.x_even = (z * 8 + (x + 1 - 2 * (x % 2)) * 2 + self.c, t)
        self.x_odd = (z * 8 + ((x + 3 + 2 * (x % 2)) % 4) * 2 + self.c, t)
        self.y = y = t // 2
        self.half = half = t % 2
        self.y_up = (d, ((y + 1) % 4) * 2 + half)
        self.y_down = (d, ((y + 3) % 4) * 2 + half)
        self.half_side = (d, y * 2 + 1 - half)

    def block(self, plane, j):
        return ((self.y + j) % 4) * 2 + (self.half + plane) % 2

    def chip(self, plane, j):
        return ((self.z + plane) % 2) * 4 + (self.x + j) % 4

    def remote(self, src, dst, send, recv, device):
        return pltpu.make_async_remote_copy(
            src_ref=src, dst_ref=dst, send_sem=send, recv_sem=recv, device_id=device, device_id_type=MESH
        )


class Doubling:
    def __init__(self, place, out, into, send, recv):
        self.place, self.out, self.into, self.send, self.recv = place, out, into, send, recv
        self.devices = (place.z_side, place.x_even, place.x_odd)

    def copy(self, k):
        return self.place.remote(
            self.out.at[k], self.into.at[k], self.send.at[k], self.recv.at[k], self.devices[k]
        )

    def start(self, value):
        self.out[0] = value
        self.copy(0).start()

    def step(self, k):
        self.copy(k - 1).wait_recv()
        total = self.out[k - 1].astype(F32) + self.into[k - 1].astype(F32)
        if k == 3:
            return total
        self.out[k] = total.astype(BF)
        self.copy(k).start()
        return total

    def drain(self):
        for k in range(3):
            self.copy(k).wait_send()


def kernel(
    x_loc, c_loc, ag, ab, mg, mb, cosine, sine, wq_hbm, wo_hbm, wu_hbm, wd_hbm,
    out_x, out_n, wq, wo, wu, wd,
    xs, cs, st_in, st, wqt, ain, min_, ain_t, min_t,
    pa, pa_in, pkv, pkv_in, kvo, kvi, kvx,
    t_z, t_1, t_2m, t_2p, t_f,
    d_out, d_in, d_z, d_1, d_2m, d_2p, d_f,
    h_out, h_in, h_z, h_1, h_2m, h_2p, h_f,
    act, hid, hq, proj, pp, pp_in, ppo, ppi,
    abt, mbt, ngb, ngr, mom, momr, nrm, nrmr, m2, nrmd, ga, turned,
    w_sem, x_s, x_r, c_s, c_r, st_s, st_r, tt_s, tt_r,
    p_s, p_r, dp_s, dp_r, hp_s, hp_r, ts, tr, ds, dr, hs, hr, kv_s, kv_r, pp_s, pp_r,
    as_, ar, gs, gr, qs, qr,
    ng_s, ng_r, mo_s, mo_r, nr_s, nr_r, m2_s, m2_r,
):
    place = Place()
    d, t, c, other, partner, remote = place.d, place.t, place.c, place.other, place.partner, place.remote

    def rows(index, size):
        return pl.ds(pl.multiple_of(index * size, size), size)

    def loop(low, high, f):
        def body(k, carry):
            f(k)
            return carry

        lax.fori_loop(low, high, body, 0)

    weights = [
        pltpu.make_async_copy(src, dst, w_sem.at[i])
        for i, (src, dst) in enumerate([(wd_hbm, wd), (wq_hbm, wq), (wo_hbm, wo), (wu_hbm, wu)])
    ]
    for copy in weights:
        copy.start()

    barrier = pltpu.get_barrier_semaphore()
    loop(
        1, NT,
        lambda k: pl.semaphore_signal(barrier, inc=1, device_id=(d, (t + k) % NT), device_id_type=MESH),
    )
    loop(
        1, ND,
        lambda k: pl.semaphore_signal(barrier, inc=1, device_id=((d + k) % ND, t), device_id_type=MESH),
    )

    own = rows(t, ROWS)
    cs[own, :] = c_loc[...]
    xs[own, :] = x_loc[...]
    lane = lax.broadcasted_iota(jnp.int32, (128, 128), 1)

    def in_rows(one, two):
        return jnp.where(lane < 4, one, two).T[0:8]

    xf = x_loc[...].astype(F32)
    pad = jnp.zeros((ROWS, 1), F32)
    st_in[0] = in_rows(
        jnp.concatenate([jnp.sum(xf, 1, keepdims=True), pad], 0),
        jnp.concatenate([jnp.sum(xf * xf, 1, keepdims=True), pad], 0),
    )
    pl.semaphore_wait(barrier, NT - 1 + ND - 1)

    def send_st(k):
        return remote(st_in.at[0], st_in.at[k], st_s.at[k], st_r.at[k], ((d + k) % ND, t))

    def send_tt(k):
        return remote(st.at[t], st.at[t], tt_s.at[k], tt_r.at[k], (d, (t + k) % NT))

    def wait_tt(k):
        p = (t + NT - k) % NT
        remote(st.at[p], st.at[p], tt_s.at[k], tt_r.at[k], (d, (t + k) % NT)).wait_recv()

    def send_c(k):
        return remote(cs.at[own], cs.at[own], c_s.at[k], c_r.at[k], (d, (t + k) % NT))

    def wait_c(k):
        there = rows((t + NT - k) % NT, ROWS)
        remote(cs.at[there], cs.at[there], c_s.at[k], c_r.at[k], (d, (t + k) % NT)).wait_recv()

    spread_x = Spread(place, xs, x_s, x_r)
    loop(1, NT, lambda k: send_c(k).start())
    loop(1, ND, lambda k: send_st(k).start())
    weights[1].wait()
    for i in range(QKV // 128):
        wqt[i * 128 : (i + 1) * 128, :] = wq[:, i * 128 : (i + 1) * 128].T
    loop(1, ND, lambda k: send_st(k).wait_recv())
    total = st_in[0]
    for k in range(1, ND):
        total = total + st_in[k]
    st[t] = total
    loop(1, NT, lambda k: send_tt(k).start())
    loop(1, NT, wait_c)
    spread_x.start()

    def produce(both, job, out, into, send, recv, hook):
        def pair(q, k):
            return remote(out.at[q, other], into.at[q], send.at[k], recv.at[k], partner)

        def body(i):
            @pl.when(i < 4)
            def _():
                j = (2 + 3 * i) % 4
                for plane in (1, 0):
                    q = place.chip(plane, j)
                    out[q, 0], out[q, 1] = both(q)
                    pair(q, 2 * i + plane).start()

            @pl.when(i > 0)
            def _():
                j = (3 * i - 1) % 4
                for plane in (1, 0):
                    q = place.chip(plane, j)
                    pair(q, 2 * (i - 1) + plane).wait_recv()
                    job.part[q] = (out[q, c].astype(F32) + into[q].astype(F32)).astype(BF)
                    if plane == 1:
                        job.z_first(j).start()

            @pl.when(i == 1)
            def _():
                job.start()

            hook(i)

        loop(0, 5, body)

    def pair_drain(out, into, send, recv):
        loop(0, 8, lambda k: remote(out.at[k, other], into.at[k], send.at[k], recv.at[k], partner).wait_send())

    down = Reduce(place, d_in, d_z, d_1, d_2m, d_2p, d_f, ds, dr, (256, 144, 80, 192))
    up = Reduce(place, h_in, h_z, h_1, h_2m, h_2p, h_f, hs, hr, (512, 288, 160, 384))
    attn = Reduce(place, pa_in, t_z, t_1, t_2m, t_2p, t_f, ts, tr, (128, 80, 48, 96))
    weights[0].wait()

    def down_both(q):
        two = dot_nt(wd[rows(q, 2 * CH), :], cs[...]).astype(BF)
        return two[:CH], two[CH:]

    def up_both(q):
        two = dot_nn(min_[...], wu[:, rows(q, 2 * CH)]).astype(BF)
        return two[:, :CH], two[:, CH:]

    def down_hook(i):
        @pl.when(i == 3)
        def _():
            spread_x.step_one()

        @pl.when(i == 4)
        def _():
            down.step_two(1)
            down.step_two(0)
            spread_x.step_two()

    produce(down_both, down, d_out, d_in, dp_s, dp_r, down_hook)

    weights[2].wait()

    def og_body(i):
        og = dot_nt(wo[rows(i, 256), :], cs[...]).astype(BF)
        pa[pl.ds(i * 2, 2), :, 0:64, :] = og.reshape(2, 2, 64, TOK)

    loop(0, 4, og_body)

    spread_x.step_three()
    loop(1, NT, wait_tt)

    def scales(block):
        columns = jnp.concatenate([st[block]] * 16, 0).T
        average = columns[0:ROWS, 0:1] * (1.0 / D)
        spread = columns[0:ROWS, 4:5] * (1.0 / D) - average * average
        return average, lax.rsqrt(spread + 1e-05)

    def norm_body(block):
        here = rows(block, ROWS)
        average, inverse = scales(block)
        normed = (xs[here, :].astype(F32) - average) * inverse
        nrmd[here, :] = normed
        ain[here, :] = (normed * ag[...] + ab[...]).astype(BF)
        min_[here, :] = (normed * mg[...] + mb[...]).astype(BF)

    loop(0, NT, norm_body)

    down.z_merge()

    def part_body(i):
        qq = dot_nt(wqt[rows(i, 256), :], ain[...]).astype(BF)
        pa[pl.ds(i * 2, 2), :, 64:128, :] = qq.reshape(2, 2, 64, TOK)

    pkv[...] = dot_nt(wqt[1024:1152, :], ain[...]).astype(BF).reshape(2, 64, TOK)
    give_kv = remote(pkv.at[other], pkv_in, p_s.at[0], p_r.at[0], partner)
    give_kv.start()
    loop(0, 4, part_body)
    give_a = remote(pa.at[:, other], pa_in, p_s.at[1], p_r.at[1], partner)
    give_a.start()

    kv_sum = Doubling(place, kvo, kvi, kv_s, kv_r)
    give_kv.wait_recv()
    kv_sum.start((pkv[c].astype(F32) + pkv_in[...].astype(F32)).astype(BF))
    give_a.wait_recv()

    def sum_a(q):
        pa_in[q] = (pa[q, c].astype(F32) + pa_in[q].astype(F32)).astype(BF)

    loop(0, 8, sum_a)
    for j in (2, 1, 0, 3):
        attn.z_first(j).start()
    attn.start()

    down.step_two(2)

    weights[3].wait()

    def hook(i):
        @pl.when(i == 2)
        def _():
            down.step_z()

        @pl.when(i == 3)
        def _():
            kv_sum.step(1)

        @pl.when(i == 4)
        def _():
            attn.step_two(1)
            attn.step_two(0)

    produce(up_both, up, h_out, h_in, hp_s, hp_r, hook)

    up.step_two(1)
    up.step_two(0)

    attn.z_merge()
    kv_sum.step(2)
    attn.step_z()
    ain_t[...] = ain[...].T
    min_t[...] = min_[...].T

    up.z_merge()
    up.step_z()

    attn.step_two(2)

    up.step_two(2)

    attn.finish()
    og = attn.total(0, 64).astype(BF)
    q_sum = attn.total(64, 128)
    kv_total = kv_sum.step(3)

    co, si = cosine[...], sine[...]
    queries_f = rotate(q_sum, co, si)
    queries = queries_f.astype(BF)
    kvx[c] = jnp.where(c == 0, rotate(kv_total, co, si), kv_total).astype(BF)
    give = remote(kvx.at[c], kvx.at[c], p_s.at[2], p_r.at[2], partner)
    give.start()
    queries_t = queries_f.T.astype(BF)
    og_tf = og.astype(F32).T
    og_t = og_tf.astype(BF)
    give.wait_recv()
    keys = kvx[0]
    values = kvx[1]
    scaling = 1.0 / math.sqrt(HD)
    key_grad = jnp.zeros((HD, TOK), F32)
    value_grad = jnp.zeros((HD, TOK), F32)
    outs, qgs = [], []
    for n in range(4):
        low, high = n * 128, (n + 1) * 128
        scores = dot_nn(queries_t[low:high], keys) * scaling
        causal = lax.broadcasted_iota(jnp.int32, (128, TOK), 0) + low >= lax.broadcasted_iota(
            jnp.int32, (128, TOK), 1
        )
        raised = jnp.where(causal, jnp.exp(scores), 0.0)
        prob = raised / jnp.sum(raised, -1, keepdims=True)
        prob_low = prob.astype(BF)
        head = dot_nt(prob_low, values).astype(BF).astype(F32)
        dropped = dot_nn(og_t[low:high], values)
        row_dot = jnp.sum(og_tf[low:high] * head, -1, keepdims=True)
        score_grad = (prob * (dropped - row_dot) * scaling).astype(BF)
        qgs.append(dot_nt(keys, score_grad))
        key_grad = key_grad + dot_nn(queries[:, low:high], score_grad)
        value_grad = value_grad + dot_nn(og[:, low:high], prob_low)
        outs.append(head.T)
    hq[d, 0:64, :] = jnp.concatenate(outs, 1).astype(BF)
    hq[d, 64:128, :] = unrotate(jnp.concatenate(qgs, 1), co, si).astype(BF)
    pp[0] = unrotate(key_grad, co, si).astype(BF)
    pp[1] = value_grad.astype(BF)

    heads = Gather(place, hq, qs, qr, (128, 80, 64, 48))
    heads.start()
    give_pp = remote(pp.at[other], pp_in, p_s.at[3], p_r.at[3], partner)
    give_pp.start()

    give_pp.wait_recv()
    pp_sum = Doubling(place, ppo, ppi, pp_s, pp_r)
    pp_sum.start((pp[c].astype(F32) + pp_in[...].astype(F32)).astype(BF))
    down.finish()
    up.finish()

    for h in range(2):
        cols = slice(h * 128, (h + 1) * 128)
        hidden = up.total(0, 512, cols).T
        dact = down.total(h * 128, (h + 1) * 128)
        value, slope = gelu_parts(hidden)
        act[d, cols, :] = value.astype(BF)
        hid[d, cols, :] = (dact * slope).astype(BF)

    gather_act = Gather(place, act, as_, ar, (256, 144, 128, 80))
    gather_hid = Gather(place, hid, gs, gr, (256, 144, 128, 80))
    gather_act.start()
    gather_hid.give((0, 0))
    mbt[...] = jnp.zeros((W, TOK), F32)

    def use_act(plane, j):
        q = place.chip(plane, j)
        gather_act.take(plane, j)
        wd[rows(q, 2 * CH), :] = dot_nn(act[pl.ds(2 * q, 2)].reshape(2 * CH, TOK), cs[...]).astype(BF)

    def back_hid(plane, j):
        q = place.chip(plane, j)
        gather_hid.take(plane, j)
        mbt[...] += dot_nn(wu[:, rows(q, 2 * CH)], hid[pl.ds(2 * q, 2)].reshape(2 * CH, TOK))

    def grad_hid(plane, j):
        q = place.chip(plane, j)
        two = hid[pl.ds(2 * q, 2)].reshape(2 * CH, TOK)
        wu[:, rows(q, 2 * CH)] = dot_nt(min_t[...], two).astype(BF)

    def use_hid(plane, j):
        back_hid(plane, j)
        grad_hid(plane, j)

    def near(f):
        loop(0, 3, lambda i: f((3 - i) // 3, i + i // 2))

    heads.step_one()
    pp_sum.step(1)
    use_act(0, 0)
    use_hid(0, 0)

    heads.step_two()
    gather_hid.go(0, 1, 2)
    pp_sum.step(2)

    gather_act.step_one()

    heads.step_three()
    heads.step_four()
    there = rows(16 + c, 64)
    proj[there, :] = pp_sum.step(3).astype(BF)
    give_pj = remote(proj.at[there], proj.at[there], p_s.at[4], p_r.at[4], partner)
    give_pj.start()
    for plane in range(2):
        for j in range(4):
            heads.take(plane, j)
    give_pj.wait_recv()

    def go_body(i):
        four = hq[pl.ds(i * 4, 4), 0:64, :].reshape(256, TOK)
        wo[rows(i, 256), :] = dot_nn(four, cs[...]).astype(BF)
        proj[rows(i, 256), :] = hq[pl.ds(i * 4, 4), 64:128, :].reshape(256, TOK)

    loop(0, 4, go_body)

    def ab_body(i):
        abt[rows(i, 256), :] = dot_nn(wq[rows(i, 256), :], proj[...])
        wq[rows(i, 256), :] = dot_nt(ain_t[rows(i, 256), :], proj[...]).astype(BF)

    loop(0, 2, ab_body)

    nrm[...] = jnp.zeros((8, W), F32)

    def early_body(n):
        here = rows(n, 128)
        a_back = abt[:, here].T
        ga[here, :] = a_back * ag[...]
        nrm[0:1, :] += jnp.sum(a_back * nrmd[here, :], 0, keepdims=True)
        nrm[1:2, :] += jnp.sum(a_back, 0, keepdims=True)

    loop(0, 4, early_body)

    near(use_act)

    gather_act.step_two()
    gather_hid.step_one()

    near(use_hid)
    use_act(0, 2)
    gather_act.step_three()
    gather_act.step_four()

    gather_hid.step_two()

    use_hid(0, 2)
    gather_hid.step_three()
    loop(0, 2, lambda i: back_hid(1, 2 * i + 1))
    gather_hid.step_four()
    back_hid(1, 2)

    def send_ng(k):
        p = (t + k) % NT
        return remote(ngb.at[rows(p, ROWS)], ngr.at[k], ng_s.at[k], ng_r.at[k], (d, p))

    def send_mo(k):
        p = (t + k) % NT
        return remote(mom.at[p // 2], momr.at[k], mo_s.at[k], mo_r.at[k], (d, p))

    def send_nr(k):
        return remote(nrm, nrmr.at[k], nr_s.at[k], nr_r.at[k], (d, (t + k) % NT))

    def tail_body(i):
        n = (t // 2 + 1 + i) % 4
        here = rows(n, 128)
        m_back = mbt[:, here].T
        normed = nrmd[here, :]
        grad = ga[here, :] + m_back * mg[...]
        ngb[here, :] = grad.astype(BF)
        mom[n] = in_rows(jnp.sum(grad, 1, keepdims=True), jnp.sum(grad * normed, 1, keepdims=True))
        nrm[2:3, :] += jnp.sum(m_back * normed, 0, keepdims=True)
        nrm[3:4, :] += jnp.sum(m_back, 0, keepdims=True)

        def send(k):
            @pl.when(k > 0)
            def _():
                send_mo(k).start()
                send_ng(k).start()

        send((2 * n - t + NT) % NT)
        send((2 * n + 1 - t + NT) % NT)

    loop(0, 4, tail_body)

    loop(1, NT, lambda k: send_nr(k).start())
    loop(1, 4, lambda i: grad_hid(1, i))
    loop(1, NT, lambda k: send_mo(k).wait_recv())
    acc = mom[t // 2]
    for k in range(1, NT):
        acc = acc + momr[k]
    m2[0] = acc

    def send_m2(k):
        return remote(m2.at[0], m2.at[k], m2_s.at[k], m2_r.at[k], ((d + k) % ND, t))

    loop(1, ND, lambda k: send_m2(k).start())
    loop(1, 4, lambda i: use_act(1, i))
    loop(1, NT, lambda k: send_ng(k).wait_recv())
    loop(1, NT, lambda k: send_nr(k).wait_recv())
    norm_total = nrm[...]
    for k in range(1, NT):
        norm_total = norm_total + nrmr[k]
    out_n[...] = norm_total[0:4, :]
    grad = ngb[own, :].astype(F32)
    for k in range(1, NT):
        grad = grad + ngr[k].astype(F32)
    loop(1, ND, lambda k: send_m2(k).wait_recv())
    moments = m2[0]
    for k in range(1, ND):
        moments = moments + m2[k]
    turned[...] = jnp.concatenate([moments] * 16, 0).T
    mine = turned[rows(t % 2, ROWS), :]
    first = mine[:, 0:1] * (1.0 / D)
    second = mine[:, 4:5] * (1.0 / D)
    _, inverse = scales(t)
    out_x[...] = (
        c_loc[...].astype(F32) + inverse * (grad - first - nrmd[own, :] * second)
    ).astype(BF)

    def drain_t(k):
        send_tt(k).wait_send()
        send_mo(k).wait_send()
        send_ng(k).wait_send()
        send_nr(k).wait_send()

    def drain_d(k):
        send_st(k).wait_send()
        send_m2(k).wait_send()

    loop(1, NT, drain_t)
    loop(1, ND, drain_d)
    for copy in (give_a, give_kv, give, give_pp, give_pj):
        copy.wait_send()
    pair_drain(d_out, d_in, dp_s, dp_r)
    pair_drain(h_out, h_in, hp_s, hp_r)
    loop(1, NT, lambda k: send_c(k).wait_send())
    for job in (spread_x, down, up, attn, kv_sum, pp_sum, heads, gather_act, gather_hid):
        job.drain()


def write_out(*refs):
    copies = [pltpu.make_async_copy(refs[i], refs[6 + i], refs[12].at[i]) for i in range(6)]
    for copy in copies:
        copy.start()
    for copy in copies:
        copy.wait()


def on_device(
    block_input, cotangent, attn_gain, attn_bias, mlp_gain, mlp_bias, w_qkv, w_out, w_up, w_down
):
    cosine, sine = rope_columns()
    vmem = pl.BlockSpec(memory_space=pltpu.VMEM)
    hbm = pl.BlockSpec(memory_space=pl.ANY)
    dma = pltpu.SemaphoreType.DMA

    def buf(*shape):
        return pltpu.VMEM(shape, BF)

    def wide(*shape):
        return pltpu.VMEM(shape, F32)

    def sums(size, a, width):
        return [
            buf(4, size - a, width), buf(2, size, width),
            buf(2, size, width), buf(2, size, width), buf(a, width),
        ]

    buffers = [
        buf(TOK, W), buf(TOK, W), wide(ND, 8, 128), wide(NT, 8, 128),
        buf(QKV, W),
        buf(TOK, W), buf(TOK, W), buf(W, TOK), buf(W, TOK),
        buf(8, 2, 128, TOK), buf(8, 128, TOK), buf(2, 64, TOK), buf(64, TOK),
        buf(3, 64, TOK), buf(3, 64, TOK), buf(2, 64, TOK),
        *sums(128, 80, TOK),
        buf(8, 2, CH, TOK), buf(8, CH, TOK), *sums(256, 144, TOK),
        buf(8, 2, TOK, CH), buf(8, TOK, CH), *sums(512, 288, CH),
        buf(ND, CH, TOK), buf(ND, CH, TOK), buf(ND, 128, TOK), buf(QKV, TOK),
        buf(2, 64, TOK), buf(64, TOK), buf(3, 64, TOK), buf(3, 64, TOK),
        wide(W, TOK), wide(W, TOK), buf(TOK, W), buf(NT, ROWS, W),
        wide(4, 8, 128), wide(NT, 8, 128), wide(8, W), wide(NT, 8, W), wide(ND, 8, 128),
        wide(TOK, W), wide(TOK, W), wide(128, 128),
    ]
    counts = [4, 9, 9, 9, 9, 16, 16, 8, 8]
    counts += [5, 5, 8, 8, 8, 8] + [17] * 6 + [3] * 4
    counts += [20] * 6 + [8, 8, 8, 8, 8, 8, 16, 16]
    semaphores = [dma((n,)) for n in counts]
    results = pl.pallas_call(
        kernel,
        out_shape=(
            pltpu.VMEM((ROWS, W), BF),
            pltpu.VMEM((4, W), F32),
            pltpu.VMEM((W, QKV), BF),
            pltpu.VMEM((1024, W), BF),
            pltpu.VMEM((W, FF), BF),
            pltpu.VMEM((FF, W), BF),
        ),
        in_specs=[vmem] * 8 + [hbm] * 4,
        out_specs=(vmem,) * 6,
        scratch_shapes=buffers + semaphores,
        compiler_params=pltpu.CompilerParams(
            collective_id=0, has_side_effects=True, vmem_limit_bytes=48 * 2**20
        ),
        cost_estimate=pl.CostEstimate(flops=14 * 10**9, bytes_accessed=21 * 10**6, transcendentals=10**6),
        name="block_backward",
    )(
        block_input, cotangent, attn_gain[None], attn_bias[None], mlp_gain[None], mlp_bias[None],
        cosine, sine, w_qkv, w_out, w_up, w_down,
    )
    return pl.pallas_call(
        write_out,
        out_shape=tuple(jax.ShapeDtypeStruct(r.shape, r.dtype) for r in results),
        in_specs=[vmem] * 6,
        out_specs=(hbm,) * 6,
        scratch_shapes=[dma((6,))],
        compiler_params=pltpu.CompilerParams(vmem_limit_bytes=4 * 2**20),
        name="write_results",
    )(*[pltpu.with_memory_space_constraint(r, pltpu.VMEM) for r in results])


def solution(mesh):
    return jax.shard_map(
        on_device,
        mesh=mesh,
        in_specs=(
            P("tensor", "dp"),
            P("tensor", "dp"),
            P("dp"),
            P("dp"),
            P("dp"),
            P("dp"),
            P("dp", "tensor"),
            P("tensor", "dp"),
            P("dp", "tensor"),
            P("tensor", "dp"),
        ),
        out_specs=(
            P("tensor", "dp"),
            P(None, "dp"),
            P("dp", "tensor"),
            P("tensor", "dp"),
            P("dp", "tensor"),
            P("tensor", "dp"),
        ),
        check_vma=False,
    )
```

```python
import functools
import math

import jax
import jax.numpy as jnp
import numpy as np
from jax import lax
from jax.experimental import pallas as pl
from jax.experimental.pallas import tpu as pltpu
from jax.sharding import PartitionSpec as P

D = 8192
HD = 64
LENGTH = 512
TOK = 512
W = 512
ROWS = 64
NT = 8
ND = 16
FF = 4096
CH = 256
QKV = 1152
MESH = pl.DeviceIdType.MESH
BF = jnp.bfloat16
F32 = jnp.float32


def dot_nn(a, b):
    return jnp.dot(a, b, preferred_element_type=F32)


def dot_nt(a, b):
    return lax.dot_general(a, b, (((1,), (1,)), ((), ())), preferred_element_type=F32)


def gelu_parts(v):
    half = 0.5 * (1.0 + lax.erf(v * 0.7071067811865476))
    return v * half, half + v * jnp.exp(-0.5 * v * v) * 0.3989422804014327


def rope_columns():
    halfway = HD // 2
    position = (np.arange(TOK) % LENGTH).astype(np.float32)
    frequency = (10000.0 ** (-2.0 * np.arange(halfway) / HD)).astype(np.float32)
    angle = frequency[:, None] * position[None, :]
    cosine = np.concatenate([np.cos(angle), np.cos(angle)], 0).astype(np.float32)
    sine = np.concatenate([np.sin(angle), np.sin(angle)], 0).astype(np.float32)
    return jnp.asarray(cosine), jnp.asarray(sine)


def rotate(v, cosine, sine):
    turned = jnp.concatenate([-v[32:], v[:32]], 0)
    return v * cosine + turned * sine


def unrotate(v, cosine, sine):
    scaled = v * sine
    back = jnp.concatenate([scaled[32:], -scaled[:32]], 0)
    return v * cosine + back


class Reduce:
    def __init__(self, place, part, zin, in1, in2m, in2p, zfin, send, recv, split):
        self.place, self.part, self.zin, self.in1 = place, part, zin, in1
        self.in2m, self.in2p, self.zfin, self.send, self.recv = in2m, in2p, zfin, send, recv
        size, a, ma, mb = split
        self.a, self.size = a, size
        self.jobs = ((0, 0, ma, a), (1, 0, ma, a), (0, a, mb, size))

    def copy(self, src, dst, k, device):
        return self.place.remote(src, dst, self.send.at[k], self.recv.at[k], device)

    def block(self, plane, j):
        return self.part.at[self.place.chip(plane, j)]

    def z_first(self, j):
        src = self.block(1, j).at[self.a : self.size]
        return self.copy(src, self.zin.at[j], j, self.place.z_side)

    def one(self, job, way):
        plane, low, mid, high = self.jobs[job]
        here = slice(low, mid) if way == 0 else slice(mid, high)
        device = (self.place.x_up, self.place.x_down)[way]
        return self.copy(self.block(plane, 2).at[here], self.in1.at[plane, here], 4 + 2 * job + way, device)

    def two(self, job, way):
        plane, low, _, high = self.jobs[job]
        here = slice(low, high)
        device = (self.place.x_up, self.place.x_down)[way]
        land = (self.in2m, self.in2p)[way]
        return self.copy(self.block(plane, (1, 3)[way]).at[here], land.at[plane, here], 10 + 2 * job + way, device)

    def z_last(self):
        return self.copy(self.block(1, 0).at[0 : self.a], self.zfin, 16, self.place.z_side)

    def add(self, plane, j, here, more):
        target = self.block(plane, j)
        total = target[here].astype(F32)
        for term in more:
            total = total + term.astype(F32)
        target[here] = total.astype(BF)

    def start(self):
        for job in (1, 0):
            for way in (0, 1):
                self.one(job, way).start()

    def z_merge(self):
        for j in (2, 1, 0, 3):
            self.z_first(j).wait_recv()
            self.add(0, j, slice(self.a, self.size), [self.zin[j]])
            if j == 2:
                self.one(2, 0).start()
                self.one(2, 1).start()

    def step_two(self, job):
        plane, low, mid, high = self.jobs[job]
        for way, here in ((0, slice(low, mid)), (1, slice(mid, high))):
            self.one(job, way).wait_recv()
            self.add(plane, (1, 3)[way], here, [self.in1[plane, here]])
            self.two(job, way).start()

    def step_z(self):
        self.two(1, 0).wait_recv()
        self.two(1, 1).wait_recv()
        here = slice(0, self.a)
        self.add(1, 0, here, [self.in2m[1, here], self.in2p[1, here]])
        self.z_last().start()

    def finish(self):
        for job in (0, 2):
            self.two(job, 0).wait_recv()
            self.two(job, 1).wait_recv()
        self.z_last().wait_recv()

    def total(self, low, high, cols=slice(None)):
        out = self.block(0, 0)[low:high, cols].astype(F32)
        out = out + self.in2m[0, low:high, cols].astype(F32) + self.in2p[0, low:high, cols].astype(F32)
        top = min(high, self.a)
        if top <= low:
            return out
        upper = out[: top - low] + self.zfin[low:top, cols].astype(F32)
        return upper if top == high else jnp.concatenate([upper, out[top - low :]], 0)

    def drain(self):
        for j in range(4):
            self.z_first(j).wait_send()
        for job in range(3):
            for way in range(2):
                self.one(job, way).wait_send()
                self.two(job, way).wait_send()
        self.z_last().wait_send()


class Gather:
    def __init__(self, place, buf, send, recv, split):
        self.place, self.buf, self.send, self.recv = place, buf, send, recv
        size, a, mo, ma = split
        up, down, side = place.x_up, place.x_down, place.z_side
        own, left, right, far = (0, 0), (0, 3), (0, 1), (0, 2)
        z_own, z_left, z_right, z_far = (1, 0), (1, 3), (1, 1), (1, 2)
        self.moves = (
            (own, left, 0, size, up),
            (own, right, 0, size, down),
            (own, z_own, 0, size, side),
            (left, far, 0, mo, up),
            (right, far, mo, size, down),
            (left, z_left, a, size, side),
            (right, z_right, a, size, side),
            (far, z_far, a, size, side),
            (z_own, z_left, 0, a, up),
            (z_own, z_right, 0, a, down),
            (z_left, z_far, 0, ma, up),
            (z_right, z_far, ma, a, down),
        )

    def index(self, where):
        return self.place.chip(*where) * 2 + self.place.c

    def copy(self, index, low, high, k, device):
        at = self.buf.at[index, low:high]
        return self.place.remote(at, at, self.send.at[k], self.recv.at[k], device)

    def go(self, *moves):
        for k in moves:
            src, _, low, high, device = self.moves[k]
            self.copy(self.index(src), low, high, k, device).start()

    def wait(self, *moves):
        for k in moves:
            _, dst, low, high, device = self.moves[k]
            self.copy(self.index(dst), low, high, k, device).wait_recv()

    def hand(self, plane, j, core):
        index = self.place.chip(plane, j) * 2 + core
        k = 12 + j + 4 * plane
        at = self.buf.at[index]
        return self.place.remote(at, at, self.send.at[k], self.recv.at[k], self.place.partner)

    def give(self, *wheres):
        for plane, j in wheres:
            self.hand(plane, j, self.place.c).start()

    def take(self, plane, j):
        self.hand(plane, j, self.place.other).wait_recv()

    def start(self):
        self.go(0, 1, 2)
        self.give((0, 0))

    def step_one(self):
        self.wait(0)
        self.go(3, 5)
        self.wait(1)
        self.go(4, 6)
        self.wait(2)
        self.go(8, 9)
        self.give((0, 3), (0, 1), (1, 0))

    def step_two(self):
        self.wait(3, 4)
        self.go(7)
        self.wait(8)
        self.go(10)
        self.wait(9)
        self.go(11)
        self.give((0, 2))

    def step_three(self):
        self.wait(5, 6)
        self.give((1, 3), (1, 1))

    def step_four(self):
        self.wait(7, 10, 11)
        self.give((1, 2))

    def drain(self):
        for k, (src, _, low, high, device) in enumerate(self.moves):
            self.copy(self.index(src), low, high, k, device).wait_send()
        for plane in range(2):
            for j in range(4):
                self.hand(plane, j, self.place.c).wait_send()


class Spread:
    def __init__(self, place, buf, send, recv):
        self.place, self.buf, self.send, self.recv = place, buf, send, recv
        up, down, side = place.y_up, place.y_down, place.half_side
        own, left, right, far = (0, 0), (0, 3), (0, 1), (0, 2)
        h_own, h_left, h_right, h_far = (1, 0), (1, 3), (1, 1), (1, 2)
        mid = ROWS // 2
        self.moves = (
            (own, left, 0, ROWS, up),
            (own, right, 0, ROWS, down),
            (own, h_own, 0, ROWS, side),
            (left, far, 0, mid, up),
            (right, far, mid, ROWS, down),
            (h_own, h_left, 0, ROWS, up),
            (h_own, h_right, 0, ROWS, down),
            (h_left, h_far, 0, mid, up),
            (h_right, h_far, mid, ROWS, down),
        )

    def copy(self, where, low, high, k, device):
        first = pl.multiple_of(self.place.block(*where) * ROWS + low, 32)
        at = self.buf.at[pl.ds(first, high - low)]
        return self.place.remote(at, at, self.send.at[k], self.recv.at[k], device)

    def go(self, *moves):
        for k in moves:
            src, _, low, high, device = self.moves[k]
            self.copy(src, low, high, k, device).start()

    def wait(self, *moves):
        for k in moves:
            _, dst, low, high, device = self.moves[k]
            self.copy(dst, low, high, k, device).wait_recv()

    def start(self):
        self.go(2, 0, 1)

    def step_one(self):
        self.wait(2)
        self.go(5, 6)
        self.wait(0)
        self.go(3)
        self.wait(1)
        self.go(4)

    def step_two(self):
        self.wait(5)
        self.go(7)
        self.wait(6)
        self.go(8)

    def step_three(self):
        self.wait(3, 4, 7, 8)

    def drain(self):
        for k, (src, _, low, high, device) in enumerate(self.moves):
            self.copy(src, low, high, k, device).wait_send()


class Place:
    def __init__(self):
        self.d = d = lax.axis_index("dp")
        self.t = t = lax.axis_index("tensor")
        self.c = d % 2
        self.other = 1 - self.c
        self.x = x = (d // 2) % 4
        self.z = z = d // 8
        self.partner = (d + 1 - 2 * self.c, t)
        self.x_up = (z * 8 + ((x + 1) % 4) * 2 + self.c, t)
        self.x_down = (z * 8 + ((x + 3) % 4) * 2 + self.c, t)
        self.z_side = ((1 - z) * 8 + x * 2 + self.c, t)
        self.x_even = (z * 8 + (x + 1 - 2 * (x % 2)) * 2 + self.c, t)
        self.x_odd = (z * 8 + ((x + 3 + 2 * (x % 2)) % 4) * 2 + self.c, t)
        self.y = y = t // 2
        self.half = half = t % 2
        self.y_up = (d, ((y + 1) % 4) * 2 + half)
        self.y_down = (d, ((y + 3) % 4) * 2 + half)
        self.half_side = (d, y * 2 + 1 - half)

    def block(self, plane, j):
        return ((self.y + j) % 4) * 2 + (self.half + plane) % 2

    def chip(self, plane, j):
        return ((self.z + plane) % 2) * 4 + (self.x + j) % 4

    def remote(self, src, dst, send, recv, device):
        return pltpu.make_async_remote_copy(
            src_ref=src, dst_ref=dst, send_sem=send, recv_sem=recv, device_id=device, device_id_type=MESH
        )


class Doubling:
    def __init__(self, place, out, into, send, recv):
        self.place, self.out, self.into, self.send, self.recv = place, out, into, send, recv
        self.devices = (place.z_side, place.x_even, place.x_odd)

    def copy(self, k):
        return self.place.remote(
            self.out.at[k], self.into.at[k], self.send.at[k], self.recv.at[k], self.devices[k]
        )

    def start(self, value):
        self.out[0] = value
        self.copy(0).start()

    def step(self, k):
        self.copy(k - 1).wait_recv()
        total = self.out[k - 1].astype(F32) + self.into[k - 1].astype(F32)
        if k == 3:
            return total
        self.out[k] = total.astype(BF)
        self.copy(k).start()
        return total

    def drain(self):
        for k in range(3):
            self.copy(k).wait_send()


def kernel(
    x_loc, c_loc, ag, ab, mg, mb, cosine, sine, wq_hbm, wo_hbm, wu_hbm, wd_hbm,
    out_x, out_n, wq, wo, wu, wd,
    xs, cs, st_in, st, wqt, ain, min_, ain_t, min_t,
    pa, pa_in, pkv, pkv_in, kvo, kvi, kvx,
    t_z, t_1, t_2m, t_2p, t_f,
    d_out, d_in, d_z, d_1, d_2m, d_2p, d_f,
    h_out, h_in, h_z, h_1, h_2m, h_2p, h_f,
    act, hid, hq, proj, pp, pp_in, ppo, ppi,
    abt, mbt, ngb, ngr, mom, momr, nrm, nrmr, m2, nrmd, ga, turned,
    w_sem, x_s, x_r, c_s, c_r, st_s, st_r, tt_s, tt_r,
    p_s, p_r, dp_s, dp_r, hp_s, hp_r, ts, tr, ds, dr, hs, hr, kv_s, kv_r, pp_s, pp_r,
    as_, ar, gs, gr, qs, qr,
    ng_s, ng_r, mo_s, mo_r, nr_s, nr_r, m2_s, m2_r,
):
    place = Place()
    d, t, c, other, partner, remote = place.d, place.t, place.c, place.other, place.partner, place.remote

    def rows(index, size):
        return pl.ds(pl.multiple_of(index * size, size), size)

    def loop(low, high, f):
        def body(k, carry):
            f(k)
            return carry

        lax.fori_loop(low, high, body, 0)

    weights = [
        pltpu.make_async_copy(src, dst, w_sem.at[i])
        for i, (src, dst) in enumerate([(wd_hbm, wd), (wq_hbm, wq), (wo_hbm, wo), (wu_hbm, wu)])
    ]
    for copy in weights:
        copy.start()

    barrier = pltpu.get_barrier_semaphore()
    loop(
        1, NT,
        lambda k: pl.semaphore_signal(barrier, inc=1, device_id=(d, (t + k) % NT), device_id_type=MESH),
    )
    loop(
        1, ND,
        lambda k: pl.semaphore_signal(barrier, inc=1, device_id=((d + k) % ND, t), device_id_type=MESH),
    )

    own = rows(t, ROWS)
    cs[own, :] = c_loc[...]
    xs[own, :] = x_loc[...]
    lane = lax.broadcasted_iota(jnp.int32, (128, 128), 1)

    def in_rows(one, two):
        return jnp.where(lane < 4, one, two).T[0:8]

    xf = x_loc[...].astype(F32)
    pad = jnp.zeros((ROWS, 1), F32)
    st_in[0] = in_rows(
        jnp.concatenate([jnp.sum(xf, 1, keepdims=True), pad], 0),
        jnp.concatenate([jnp.sum(xf * xf, 1, keepdims=True), pad], 0),
    )
    pl.semaphore_wait(barrier, NT - 1 + ND - 1)

    def send_st(k):
        return remote(st_in.at[0], st_in.at[k], st_s.at[k], st_r.at[k], ((d + k) % ND, t))

    def send_tt(k):
        return remote(st.at[t], st.at[t], tt_s.at[k], tt_r.at[k], (d, (t + k) % NT))

    def wait_tt(k):
        p = (t + NT - k) % NT
        remote(st.at[p], st.at[p], tt_s.at[k], tt_r.at[k], (d, (t + k) % NT)).wait_recv()

    def send_c(k):
        return remote(cs.at[own], cs.at[own], c_s.at[k], c_r.at[k], (d, (t + k) % NT))

    def wait_c(k):
        there = rows((t + NT - k) % NT, ROWS)
        remote(cs.at[there], cs.at[there], c_s.at[k], c_r.at[k], (d, (t + k) % NT)).wait_recv()

    spread_x = Spread(place, xs, x_s, x_r)
    loop(1, NT, lambda k: send_c(k).start())
    loop(1, ND, lambda k: send_st(k).start())
    weights[1].wait()
    for i in range(QKV // 128):
        wqt[i * 128 : (i + 1) * 128, :] = wq[:, i * 128 : (i + 1) * 128].T
    loop(1, ND, lambda k: send_st(k).wait_recv())
    total = st_in[0]
    for k in range(1, ND):
        total = total + st_in[k]
    st[t] = total
    loop(1, NT, lambda k: send_tt(k).start())
    loop(1, NT, wait_c)
    spread_x.start()

    def produce(both, job, out, into, send, recv, hook):
        def pair(q, k):
            return remote(out.at[q, other], into.at[q], send.at[k], recv.at[k], partner)

        def body(i):
            @pl.when(i < 4)
            def _():
                j = (2 + 3 * i) % 4
                for plane in (1, 0):
                    q = place.chip(plane, j)
                    out[q, 0], out[q, 1] = both(q)
                    pair(q, 2 * i + plane).start()

            @pl.when(i > 0)
            def _():
                j = (3 * i - 1) % 4
                for plane in (1, 0):
                    q = place.chip(plane, j)
                    pair(q, 2 * (i - 1) + plane).wait_recv()
                    job.part[q] = (out[q, c].astype(F32) + into[q].astype(F32)).astype(BF)
                    if plane == 1:
                        job.z_first(j).start()

            @pl.when(i == 1)
            def _():
                job.start()

            hook(i)

        loop(0, 5, body)

    def pair_drain(out, into, send, recv):
        loop(0, 8, lambda k: remote(out.at[k, other], into.at[k], send.at[k], recv.at[k], partner).wait_send())

    down = Reduce(place, d_in, d_z, d_1, d_2m, d_2p, d_f, ds, dr, (256, 144, 80, 192))
    up = Reduce(place, h_in, h_z, h_1, h_2m, h_2p, h_f, hs, hr, (512, 288, 160, 384))
    attn = Reduce(place, pa_in, t_z, t_1, t_2m, t_2p, t_f, ts, tr, (128, 80, 48, 96))
    weights[0].wait()

    def down_both(q):
        two = dot_nt(wd[rows(q, 2 * CH), :], cs[...]).astype(BF)
        return two[:CH], two[CH:]

    def up_both(q):
        two = dot_nn(min_[...], wu[:, rows(q, 2 * CH)]).astype(BF)
        return two[:, :CH], two[:, CH:]

    def down_hook(i):
        @pl.when(i == 3)
        def _():
            spread_x.step_one()

        @pl.when(i == 4)
        def _():
            down.step_two(1)
            down.step_two(0)
            spread_x.step_two()

    produce(down_both, down, d_out, d_in, dp_s, dp_r, down_hook)

    weights[2].wait()

    def og_body(i):
        og = dot_nt(wo[rows(i, 256), :], cs[...]).astype(BF)
        pa[pl.ds(i * 2, 2), :, 0:64, :] = og.reshape(2, 2, 64, TOK)

    loop(0, 4, og_body)

    spread_x.step_three()
    loop(1, NT, wait_tt)

    def scales(block):
        columns = jnp.concatenate([st[block]] * 16, 0).T
        average = columns[0:ROWS, 0:1] * (1.0 / D)
        spread = columns[0:ROWS, 4:5] * (1.0 / D) - average * average
        return average, lax.rsqrt(spread + 1e-05)

    def norm_body(block):
        here = rows(block, ROWS)
        average, inverse = scales(block)
        normed = (xs[here, :].astype(F32) - average) * inverse
        nrmd[here, :] = normed
        ain[here, :] = (normed * ag[...] + ab[...]).astype(BF)
        min_[here, :] = (normed * mg[...] + mb[...]).astype(BF)

    loop(0, NT, norm_body)

    down.z_merge()

    def part_body(i):
        qq = dot_nt(wqt[rows(i, 256), :], ain[...]).astype(BF)
        pa[pl.ds(i * 2, 2), :, 64:128, :] = qq.reshape(2, 2, 64, TOK)

    pkv[...] = dot_nt(wqt[1024:1152, :], ain[...]).astype(BF).reshape(2, 64, TOK)
    give_kv = remote(pkv.at[other], pkv_in, p_s.at[0], p_r.at[0], partner)
    give_kv.start()
    loop(0, 4, part_body)
    give_a = remote(pa.at[:, other], pa_in, p_s.at[1], p_r.at[1], partner)
    give_a.start()

    kv_sum = Doubling(place, kvo, kvi, kv_s, kv_r)
    give_kv.wait_recv()
    kv_sum.start((pkv[c].astype(F32) + pkv_in[...].astype(F32)).astype(BF))
    give_a.wait_recv()

    def sum_a(q):
        pa_in[q] = (pa[q, c].astype(F32) + pa_in[q].astype(F32)).astype(BF)

    loop(0, 8, sum_a)
    for j in (2, 1, 0, 3):
        attn.z_first(j).start()
    attn.start()

    down.step_two(2)

    weights[3].wait()

    def hook(i):
        @pl.when(i == 2)
        def _():
            down.step_z()

        @pl.when(i == 3)
        def _():
            kv_sum.step(1)

        @pl.when(i == 4)
        def _():
            attn.step_two(1)
            attn.step_two(0)

    produce(up_both, up, h_out, h_in, hp_s, hp_r, hook)

    up.step_two(1)
    up.step_two(0)

    attn.z_merge()
    kv_sum.step(2)
    attn.step_z()
    ain_t[...] = ain[...].T
    min_t[...] = min_[...].T

    up.z_merge()
    up.step_z()

    attn.step_two(2)

    up.step_two(2)

    attn.finish()
    og = attn.total(0, 64).astype(BF)
    q_sum = attn.total(64, 128)
    kv_total = kv_sum.step(3)

    co, si = cosine[...], sine[...]
    queries_f = rotate(q_sum, co, si)
    queries = queries_f.astype(BF)
    kvx[c] = jnp.where(c == 0, rotate(kv_total, co, si), kv_total).astype(BF)
    give = remote(kvx.at[c], kvx.at[c], p_s.at[2], p_r.at[2], partner)
    give.start()
    queries_t = queries_f.T.astype(BF)
    og_tf = og.astype(F32).T
    og_t = og_tf.astype(BF)
    give.wait_recv()
    keys = kvx[0]
    values = kvx[1]
    scaling = 1.0 / math.sqrt(HD)
    key_grad = jnp.zeros((HD, TOK), F32)
    value_grad = jnp.zeros((HD, TOK), F32)
    outs, qgs = [], []
    for n in range(4):
        low, high = n * 128, (n + 1) * 128
        scores = dot_nn(queries_t[low:high], keys) * scaling
        causal = lax.broadcasted_iota(jnp.int32, (128, TOK), 0) + low >= lax.broadcasted_iota(
            jnp.int32, (128, TOK), 1
        )
        raised = jnp.where(causal, jnp.exp(scores), 0.0)
        prob = raised / jnp.sum(raised, -1, keepdims=True)
        prob_low = prob.astype(BF)
        head = dot_nt(prob_low, values).astype(BF).astype(F32)
        dropped = dot_nn(og_t[low:high], values)
        row_dot = jnp.sum(og_tf[low:high] * head, -1, keepdims=True)
        score_grad = (prob * (dropped - row_dot) * scaling).astype(BF)
        qgs.append(dot_nt(keys, score_grad))
        key_grad = key_grad + dot_nn(queries[:, low:high], score_grad)
        value_grad = value_grad + dot_nn(og[:, low:high], prob_low)
        outs.append(head.T)
    hq[d, 0:64, :] = jnp.concatenate(outs, 1).astype(BF)
    hq[d, 64:128, :] = unrotate(jnp.concatenate(qgs, 1), co, si).astype(BF)
    pp[0] = unrotate(key_grad, co, si).astype(BF)
    pp[1] = value_grad.astype(BF)

    heads = Gather(place, hq, qs, qr, (128, 80, 64, 48))
    heads.start()
    give_pp = remote(pp.at[other], pp_in, p_s.at[3], p_r.at[3], partner)
    give_pp.start()

    give_pp.wait_recv()
    pp_sum = Doubling(place, ppo, ppi, pp_s, pp_r)
    pp_sum.start((pp[c].astype(F32) + pp_in[...].astype(F32)).astype(BF))
    down.finish()
    up.finish()

    for h in range(2):
        cols = slice(h * 128, (h + 1) * 128)
        hidden = up.total(0, 512, cols).T
        dact = down.total(h * 128, (h + 1) * 128)
        value, slope = gelu_parts(hidden)
        act[d, cols, :] = value.astype(BF)
        hid[d, cols, :] = (dact * slope).astype(BF)

    gather_act = Gather(place, act, as_, ar, (256, 144, 128, 80))
    gather_hid = Gather(place, hid, gs, gr, (256, 144, 128, 80))
    gather_act.start()
    gather_hid.give((0, 0))
    mbt[...] = jnp.zeros((W, TOK), F32)

    def use_act(plane, j):
        q = place.chip(plane, j)
        gather_act.take(plane, j)
        wd[rows(q, 2 * CH), :] = dot_nn(act[pl.ds(2 * q, 2)].reshape(2 * CH, TOK), cs[...]).astype(BF)

    def back_hid(plane, j):
        q = place.chip(plane, j)
        gather_hid.take(plane, j)
        mbt[...] += dot_nn(wu[:, rows(q, 2 * CH)], hid[pl.ds(2 * q, 2)].reshape(2 * CH, TOK))

    def grad_hid(plane, j):
        q = place.chip(plane, j)
        two = hid[pl.ds(2 * q, 2)].reshape(2 * CH, TOK)
        wu[:, rows(q, 2 * CH)] = dot_nt(min_t[...], two).astype(BF)

    def use_hid(plane, j):
        back_hid(plane, j)
        grad_hid(plane, j)

    def near(f):
        loop(0, 3, lambda i: f((3 - i) // 3, i + i // 2))

    heads.step_one()
    pp_sum.step(1)
    use_act(0, 0)
    use_hid(0, 0)

    gather_hid.go(0, 1, 2)
    heads.step_two()
    pp_sum.step(2)

    gather_act.step_one()
    near(use_act)

    heads.step_three()
    heads.step_four()
    there = rows(16 + c, 64)
    proj[there, :] = pp_sum.step(3).astype(BF)
    give_pj = remote(proj.at[there], proj.at[there], p_s.at[4], p_r.at[4], partner)
    give_pj.start()
    for plane in range(2):
        for j in range(4):
            heads.take(plane, j)
    give_pj.wait_recv()

    def go_body(i):
        four = hq[pl.ds(i * 4, 4), 0:64, :].reshape(256, TOK)
        wo[rows(i, 256), :] = dot_nn(four, cs[...]).astype(BF)
        proj[rows(i, 256), :] = hq[pl.ds(i * 4, 4), 64:128, :].reshape(256, TOK)

    loop(0, 4, go_body)

    def ab_body(i):
        abt[rows(i, 256), :] = dot_nn(wq[rows(i, 256), :], proj[...])
        wq[rows(i, 256), :] = dot_nt(ain_t[rows(i, 256), :], proj[...]).astype(BF)

    loop(0, 2, ab_body)

    nrm[...] = jnp.zeros((8, W), F32)

    def early_body(n):
        here = rows(n, 128)
        a_back = abt[:, here].T
        ga[here, :] = a_back * ag[...]
        nrm[0:1, :] += jnp.sum(a_back * nrmd[here, :], 0, keepdims=True)
        nrm[1:2, :] += jnp.sum(a_back, 0, keepdims=True)

    loop(0, 4, early_body)

    gather_hid.step_one()
    gather_act.step_two()

    near(use_hid)
    use_act(0, 2)
    gather_act.step_three()
    gather_act.step_four()

    gather_hid.step_two()

    use_hid(0, 2)
    gather_hid.step_three()
    loop(0, 2, lambda i: back_hid(1, 2 * i + 1))
    gather_hid.step_four()
    back_hid(1, 2)

    def send_ng(k):
        p = (t + k) % NT
        return remote(ngb.at[rows(p, ROWS)], ngr.at[k], ng_s.at[k], ng_r.at[k], (d, p))

    def send_mo(k):
        p = (t + k) % NT
        return remote(mom.at[p // 2], momr.at[k], mo_s.at[k], mo_r.at[k], (d, p))

    def send_nr(k):
        return remote(nrm, nrmr.at[k], nr_s.at[k], nr_r.at[k], (d, (t + k) % NT))

    def tail_body(i):
        n = (t // 2 + 1 + i) % 4
        here = rows(n, 128)
        m_back = mbt[:, here].T
        normed = nrmd[here, :]
        grad = ga[here, :] + m_back * mg[...]
        ngb[here, :] = grad.astype(BF)
        mom[n] = in_rows(jnp.sum(grad, 1, keepdims=True), jnp.sum(grad * normed, 1, keepdims=True))
        nrm[2:3, :] += jnp.sum(m_back * normed, 0, keepdims=True)
        nrm[3:4, :] += jnp.sum(m_back, 0, keepdims=True)

        def send(k):
            @pl.when(k > 0)
            def _():
                send_mo(k).start()
                send_ng(k).start()

        send((2 * n - t + NT) % NT)
        send((2 * n + 1 - t + NT) % NT)

    loop(0, 4, tail_body)

    loop(1, NT, lambda k: send_nr(k).start())
    loop(1, 4, lambda i: grad_hid(1, i))
    loop(1, NT, lambda k: send_mo(k).wait_recv())
    acc = mom[t // 2]
    for k in range(1, NT):
        acc = acc + momr[k]
    m2[0] = acc

    def send_m2(k):
        return remote(m2.at[0], m2.at[k], m2_s.at[k], m2_r.at[k], ((d + k) % ND, t))

    loop(1, ND, lambda k: send_m2(k).start())
    loop(1, 4, lambda i: use_act(1, i))
    loop(1, NT, lambda k: send_ng(k).wait_recv())
    loop(1, NT, lambda k: send_nr(k).wait_recv())
    norm_total = nrm[...]
    for k in range(1, NT):
        norm_total = norm_total + nrmr[k]
    out_n[...] = norm_total[0:4, :]
    grad = ngb[own, :].astype(F32)
    for k in range(1, NT):
        grad = grad + ngr[k].astype(F32)
    loop(1, ND, lambda k: send_m2(k).wait_recv())
    moments = m2[0]
    for k in range(1, ND):
        moments = moments + m2[k]
    turned[...] = jnp.concatenate([moments] * 16, 0).T
    mine = turned[rows(t % 2, ROWS), :]
    first = mine[:, 0:1] * (1.0 / D)
    second = mine[:, 4:5] * (1.0 / D)
    _, inverse = scales(t)
    out_x[...] = (
        c_loc[...].astype(F32) + inverse * (grad - first - nrmd[own, :] * second)
    ).astype(BF)

    def drain_t(k):
        send_tt(k).wait_send()
        send_mo(k).wait_send()
        send_ng(k).wait_send()
        send_nr(k).wait_send()

    def drain_d(k):
        send_st(k).wait_send()
        send_m2(k).wait_send()

    loop(1, NT, drain_t)
    loop(1, ND, drain_d)
    for copy in (give_a, give_kv, give, give_pp, give_pj):
        copy.wait_send()
    pair_drain(d_out, d_in, dp_s, dp_r)
    pair_drain(h_out, h_in, hp_s, hp_r)
    loop(1, NT, lambda k: send_c(k).wait_send())
    for job in (spread_x, down, up, attn, kv_sum, pp_sum, heads, gather_act, gather_hid):
        job.drain()


def write_out(*refs):
    copies = [pltpu.make_async_copy(refs[i], refs[6 + i], refs[12].at[i]) for i in range(6)]
    for copy in copies:
        copy.start()
    for copy in copies:
        copy.wait()


def on_device(
    block_input, cotangent, attn_gain, attn_bias, mlp_gain, mlp_bias, w_qkv, w_out, w_up, w_down
):
    cosine, sine = rope_columns()
    vmem = pl.BlockSpec(memory_space=pltpu.VMEM)
    hbm = pl.BlockSpec(memory_space=pl.ANY)
    dma = pltpu.SemaphoreType.DMA

    def buf(*shape):
        return pltpu.VMEM(shape, BF)

    def wide(*shape):
        return pltpu.VMEM(shape, F32)

    def sums(size, a, width):
        return [
            buf(4, size - a, width), buf(2, size, width),
            buf(2, size, width), buf(2, size, width), buf(a, width),
        ]

    buffers = [
        buf(TOK, W), buf(TOK, W), wide(ND, 8, 128), wide(NT, 8, 128),
        buf(QKV, W),
        buf(TOK, W), buf(TOK, W), buf(W, TOK), buf(W, TOK),
        buf(8, 2, 128, TOK), buf(8, 128, TOK), buf(2, 64, TOK), buf(64, TOK),
        buf(3, 64, TOK), buf(3, 64, TOK), buf(2, 64, TOK),
        *sums(128, 80, TOK),
        buf(8, 2, CH, TOK), buf(8, CH, TOK), *sums(256, 144, TOK),
        buf(8, 2, TOK, CH), buf(8, TOK, CH), *sums(512, 288, CH),
        buf(ND, CH, TOK), buf(ND, CH, TOK), buf(ND, 128, TOK), buf(QKV, TOK),
        buf(2, 64, TOK), buf(64, TOK), buf(3, 64, TOK), buf(3, 64, TOK),
        wide(W, TOK), wide(W, TOK), buf(TOK, W), buf(NT, ROWS, W),
        wide(4, 8, 128), wide(NT, 8, 128), wide(8, W), wide(NT, 8, W), wide(ND, 8, 128),
        wide(TOK, W), wide(TOK, W), wide(128, 128),
    ]
    counts = [4, 9, 9, 9, 9, 16, 16, 8, 8]
    counts += [5, 5, 8, 8, 8, 8] + [17] * 6 + [3] * 4
    counts += [20] * 6 + [8, 8, 8, 8, 8, 8, 16, 16]
    semaphores = [dma((n,)) for n in counts]
    results = pl.pallas_call(
        kernel,
        out_shape=(
            pltpu.VMEM((ROWS, W), BF),
            pltpu.VMEM((4, W), F32),
            pltpu.VMEM((W, QKV), BF),
            pltpu.VMEM((1024, W), BF),
            pltpu.VMEM((W, FF), BF),
            pltpu.VMEM((FF, W), BF),
        ),
        in_specs=[vmem] * 8 + [hbm] * 4,
        out_specs=(vmem,) * 6,
        scratch_shapes=buffers + semaphores,
        compiler_params=pltpu.CompilerParams(
            collective_id=0, has_side_effects=True, vmem_limit_bytes=48 * 2**20
        ),
        cost_estimate=pl.CostEstimate(flops=14 * 10**9, bytes_accessed=21 * 10**6, transcendentals=10**6),
        name="block_backward",
    )(
        block_input, cotangent, attn_gain[None], attn_bias[None], mlp_gain[None], mlp_bias[None],
        cosine, sine, w_qkv, w_out, w_up, w_down,
    )
    return pl.pallas_call(
        write_out,
        out_shape=tuple(jax.ShapeDtypeStruct(r.shape, r.dtype) for r in results),
        in_specs=[vmem] * 6,
        out_specs=(hbm,) * 6,
        scratch_shapes=[dma((6,))],
        compiler_params=pltpu.CompilerParams(vmem_limit_bytes=4 * 2**20),
        name="write_results",
    )(*[pltpu.with_memory_space_constraint(r, pltpu.VMEM) for r in results])


def solution(mesh):
    return jax.shard_map(
        on_device,
        mesh=mesh,
        in_specs=(
            P("tensor", "dp"),
            P("tensor", "dp"),
            P("dp"),
            P("dp"),
            P("dp"),
            P("dp"),
            P("dp", "tensor"),
            P("tensor", "dp"),
            P("dp", "tensor"),
            P("tensor", "dp"),
        ),
        out_specs=(
            P("tensor", "dp"),
            P(None, "dp"),
            P("dp", "tensor"),
            P("tensor", "dp"),
            P("dp", "tensor"),
            P("tensor", "dp"),
        ),
        check_vma=False,
    )
```
